32 devices in a mesh: seq: 4 (over y, core), head: 2 (over x), dp: 4 (over z).
Axes of the slice: x: 2, y: 2, z: 4, core: 2. Of those that a mesh axis runs over, the one named last changes fastest.
Arguments:
- queries: bfloat16 [4, 2048, 1024], P('dp', 'seq', 'head'), may hold values from -2 to 2
- keys: bfloat16 [4, 2048, 1024], P('dp', 'seq', 'head'), may hold values from -2 to 2
- values: bfloat16 [4, 2048, 1024], P('dp', 'seq', 'head'), may hold values from -6 to 6
- out_proj: bfloat16 [1024, 1024], P('head', 'dp'), may hold values from -0.1875 to 0.1875
- depth_proj: bfloat16 [1024, 1024], P(None, ('head', 'dp')), may hold values from -0.1875 to 0.1875
- code_table: bfloat16 [2, 1024, 1024], P(None, ('head', 'dp')), may hold values from -6 to 6
- code_ids: int32 [4, 2048, 2], P('dp', ('seq', 'head')), may hold values from 0 to 1023
- depth_cotangent: bfloat16 [4, 2048, 2, 1024], P('dp', ('seq', 'head')), may hold values from -6 to 6
Outputs:
- grad_queries: bfloat16 [4, 2048, 1024], P('dp', 'seq', 'head')
- grad_keys: bfloat16 [4, 2048, 1024], P('dp', 'seq', 'head')
- grad_values: bfloat16 [4, 2048, 1024], P('dp', 'seq', 'head')
- grad_out_proj: float32 [1024, 1024], P('head', 'dp')
The draws below stay inside these ranges and needn't reach their ends.
All inputs are finite; a program needn't handle non-finite values.
Results may differ from the reference program's by a relative error of at most 0.024.
Values may be sent and summed in bfloat16 or wider, within the bound.
No kernel may reach another device: no remote copies, remote signals or barrier semaphores. Data moves between devices by JAX's collectives and lax.ppermute only.
A program may use at most 64 MiB of HBM per device.

```python
import jax
import jax.numpy as jnp
from jax import lax

DH = 128
DW = 1024
VOCAB = 1024
LEVELS = 2
GROUP = 512
HEADS = 8
LENGTH = 2048
BATCH = 4
N_SEQ = 4


def place_ends(drawn, stream_key, low, largest):
    longest = drawn.shape.index(max(drawn.shape))
    spots = []
    for shift in (0, 1):
        where = [jax.random.randint(jax.random.fold_in(stream_key, axis), (), 0, length) for axis, length in enumerate(drawn.shape)]
        where[longest] = (where[longest] + shift) % drawn.shape[longest]
        spots.append(tuple(where))
    return drawn.at[spots[0]].set(low).at[spots[1]].set(largest)


def levels(own_key, shape, split, smallest, top_value):
    loudness = 1.0
    for dim, shards_of in split:
        draws = jax.random.uniform(jax.random.fold_in(jax.random.fold_in(own_key, 6), dim), (shards_of,), jnp.float32, smallest / len(split), top_value / len(split))
        loudness = loudness * jnp.repeat(jnp.exp(draws), shape[dim] // shards_of).reshape((-1,) + (1,) * (len(shape) - 1 - dim))
    return loudness


def scatter_about(stream_key, shape, deviation, most, cuts=(), kind=jnp.bfloat16):
    factor_of = levels(stream_key, shape, cuts, -0.22, 0.18) if cuts else 1.0
    array = jax.random.normal(stream_key, shape, jnp.float32) * deviation * factor_of
    return jnp.minimum(jnp.maximum(array, -most), most).astype(kind)


def setup_inputs(seed: int = 0) -> dict:
    seeds = jax.random.split(jax.random.key(seed), 9)
    return {
        "queries": scatter_about(seeds[0], (BATCH, LENGTH, HEADS * DH), 0.3, 2.0, ((0, 4), (1, 4), (2, 2))),
        "keys": scatter_about(seeds[1], (BATCH, LENGTH, HEADS * DH), 0.3, 2.0, ((0, 4), (1, 4), (2, 2))),
        "values": scatter_about(seeds[2], (BATCH, LENGTH, HEADS * DH), 1.0, 6.0, ((0, 4), (1, 4), (2, 2))),
        "out_proj": scatter_about(seeds[3], (HEADS * DH, DW), (HEADS * DH) ** -0.5, 0.1875, ((0, 2), (1, 4))),
        "depth_proj": scatter_about(seeds[4], (DW, DW), DW ** -0.5, 0.1875, ((1, 8),)),
        "code_table": scatter_about(seeds[5], (LEVELS, VOCAB, DW), 1.0, 6.0, ((1, 8),)),
        "code_ids": place_ends(jax.random.randint(seeds[6], (BATCH, LENGTH, LEVELS), 0, VOCAB), jax.random.fold_in(seeds[6], 1), 0, VOCAB - 1).astype(jnp.int32),
        "depth_cotangent": scatter_about(seeds[7], (BATCH, LENGTH, LEVELS, DW), 1.0, 6.0, ((0, 4), (1, 8))),
    }


def causal_mask(size):
    places = jnp.arange(size, dtype=jnp.int32)
    return (places[:, None] >= places[None, :]).astype(jnp.float32)

def depth_forward(carried, code_tab, proj_mat, code_rows):
    vocab_idx = jnp.arange(code_tab.shape[1], dtype=jnp.int32)
    level_outs = []
    for level_idx in range(code_tab.shape[0]):
        onehot = (code_rows[:, level_idx][:, None] == vocab_idx[None, :]).astype(jnp.bfloat16)
        embedded = jnp.dot(onehot, code_tab[level_idx], preferred_element_type=jnp.float32)
        summed = carried + embedded
        normed = (summed * lax.rsqrt(lax.optimization_barrier(jnp.mean(summed * summed, axis=-1, keepdims=True)) + 1e-05)).astype(jnp.bfloat16)
        projected = jnp.dot(normed, proj_mat, preferred_element_type=jnp.float32)
        level_outs.append(projected)
        carried = summed + jax.nn.silu(projected)
    return jnp.stack(level_outs, axis=1)

def depth_grad(rows_in, code_tab, proj_mat, code_rows, cotangent):
    _, pullback = jax.vjp(lambda inputs: depth_forward(inputs, code_tab, proj_mat, code_rows), rows_in)
    return pullback(cotangent.astype(jnp.float32))[0]

def exclusive(stack, backward):
    if backward:
        running = jnp.cumsum(stack[::-1], axis=0)[::-1]
        return jnp.concatenate([running[1:], jnp.zeros_like(stack[:1])], axis=0)
    running = jnp.cumsum(stack, axis=0)
    return jnp.concatenate([jnp.zeros_like(stack[:1]), running[:-1]], axis=0)

def bf_round(value):
    return lax.optimization_barrier(value.astype(jnp.bfloat16)).astype(jnp.float32)

def reference(queries, keys, values, out_proj, depth_proj, code_table, code_ids, depth_cotangent):
    att_scale = float(LENGTH) ** (-0.5)
    head_count = queries.shape[2] // DH
    causal = causal_mask(GROUP)
    shape_four = (N_SEQ, GROUP, head_count, DH)

    def per_sequence(packed):
        query_seq, key_seq, value_seq, code_rows, cotangent = packed
        query_f = query_seq.reshape(shape_four).astype(jnp.float32)
        key_f = key_seq.reshape(shape_four).astype(jnp.float32)
        value_f = value_seq.reshape(shape_four).astype(jnp.float32)
        state_local = jnp.einsum('nchd,nche->nhde', key_f, value_f)
        state_in = bf_round(exclusive(state_local, False))
        scores = bf_round(jnp.einsum('nthd,nshd->nhts', query_f, key_f) * causal)
        attended = (att_scale * (jnp.einsum('nhts,nshe->nthe', scores, value_f) + jnp.einsum('nthd,nhde->nthe', query_f, state_in))).astype(jnp.bfloat16)
        attended_flat = attended.reshape(LENGTH, head_count * DH)
        mixed = jnp.dot(attended_flat, out_proj, preferred_element_type=jnp.float32)
        grad_mixed = depth_grad(mixed, code_table, depth_proj, code_rows, cotangent).astype(jnp.bfloat16)
        grad_att = jnp.dot(grad_mixed, out_proj.T, preferred_element_type=jnp.float32).astype(jnp.bfloat16)
        weight_term = jnp.dot(attended_flat.T, grad_mixed, preferred_element_type=jnp.float32)
        grad_f = grad_att.reshape(shape_four).astype(jnp.float32)
        back_state = bf_round(exclusive(jnp.einsum('nthd,nthe->nhde', query_f, grad_f), True))
        grad_scores = bf_round(jnp.einsum('nthe,nshe->nhts', grad_f, value_f) * causal)
        grad_query = att_scale * (jnp.einsum('nhts,nshd->nthd', grad_scores, key_f) + jnp.einsum('nthe,nhde->nthd', grad_f, state_in))
        grad_key = att_scale * (jnp.einsum('nhts,nthd->nshd', grad_scores, query_f) + jnp.einsum('nshe,nhde->nshd', value_f, back_state))
        grad_value = att_scale * (jnp.einsum('nhts,nthe->nshe', scores, grad_f) + jnp.einsum('nshd,nhde->nshe', key_f, back_state))
        return (grad_query.reshape(LENGTH, head_count * DH).astype(jnp.bfloat16), grad_key.reshape(LENGTH, head_count * DH).astype(jnp.bfloat16), grad_value.reshape(LENGTH, head_count * DH).astype(jnp.bfloat16), weight_term)
    results = lax.map(per_sequence, (queries, keys, values, code_ids, depth_cotangent))
    return (results[0], results[1], results[2], lax.optimization_barrier(jnp.sum(results[3], axis=0)))
```

```python
import jax
import jax.numpy as jnp
from jax import lax
from jax.sharding import PartitionSpec as P

DH = 128
F32 = jnp.float32
BF16 = jnp.bfloat16


def swap(block, axis, mask):
    return lax.ppermute(block, axis, [(i, i ^ mask) for i in range(lax.axis_size(axis))])


def has_bit(index, bit):
    return lax.bitwise_and(index, jnp.int32(bit)) != 0


def in_order(pieces, index):
    pieces = list(pieces)
    bit = 1
    while bit < len(pieces):
        odd = has_bit(index, bit)
        pieces = [jnp.where(odd, pieces[j ^ bit], pieces[j]) for j in range(len(pieces))]
        bit *= 2
    return pieces


def pick(array, index, dim):
    return lax.dynamic_index_in_dim(array, index, dim, keepdims=False)


def exchange(block, axis):
    return [block] + [swap(block, axis, k) for k in range(1, lax.axis_size(axis))]


def dot(a, b, dims):
    return lax.dot_general(a, b, ((dims[0], dims[1]), ((), ())), preferred_element_type=F32)


def earlier_sum(state, backward):
    n_seq = lax.axis_size("seq")
    me = lax.axis_index("seq")
    before = jnp.zeros_like(state)
    total = state
    bit = 1
    while bit < n_seq:
        got = swap(total.astype(BF16), "seq", bit).astype(F32)
        mine = has_bit(me, bit)
        takes = jnp.logical_not(mine) if backward else mine
        before = before + jnp.where(takes, got, 0.0)
        total = total + got
        bit *= 2
    return before.astype(BF16)


def on_device(queries, keys, values, out_proj, depth_proj, code_table, code_ids, depth_cotangent):
    n_seq, n_head, n_dp = (lax.axis_size(a) for a in ("seq", "head", "dp"))
    me_seq, me_head, me_dp = (lax.axis_index(a) for a in ("seq", "head", "dp"))
    group_len, width_dev = queries.shape[1:]
    heads_here = width_dev // DH
    tokens = group_len // n_head
    n_far = n_seq // 2
    me_core = lax.bitwise_and(me_seq, jnp.int32(1))
    me_far = lax.shift_right_logical(me_seq, jnp.int32(1))
    lane = me_core * n_far + me_far
    att_scale = float(group_len * n_seq) ** (-0.5)
    width = code_table.shape[2]
    wide = width // n_seq
    far = [2 * m for m in range(n_far)]

    def far_exchange(block):
        return [block] + [swap(block, "seq", m) for m in far[1:]]

    def seq_lanes(block):
        near = jnp.stack(in_order(far_exchange(block), me_far))
        both = in_order([near, swap(near, "seq", 1)], me_core)
        return jnp.concatenate(both, axis=0)

    ids = code_ids[0].T
    ids_far = jnp.stack(far_exchange(ids))
    ids_rel = jnp.stack([ids_far, swap(ids_far, "seq", 1)])

    table = lax.dynamic_slice_in_dim(code_table, lane * wide, wide, axis=2)
    rows_dev = table.shape[1]
    embedded = []
    row_no = []
    for k_head in range(n_head):
        for k_dp in range(n_dp):
            owner = (me_head ^ k_head) * n_dp + (me_dp ^ k_dp)
            row_no.append(owner * rows_dev + jnp.arange(rows_dev, dtype=jnp.int32))
    row_no = jnp.concatenate(row_no)
    for level in range(table.shape[0]):
        part = jnp.concatenate(exchange(table[level], "dp"), axis=0)
        part = jnp.concatenate(exchange(part, "head"), axis=0)
        level_ids = ids_rel[:, :, level].reshape(-1)
        onehot = (level_ids[:, None] == row_no[None, :]).astype(BF16)
        rel = dot(onehot, part, ((1,), (0,))).astype(BF16).reshape(2, n_far, tokens, wide)
        mine = [rel[:, 0]] + [swap(rel[:, m // 2], "seq", m) for m in far[1:]]
        near = jnp.stack([block[0] for block in mine])
        other = swap(jnp.stack([block[1] for block in mine]), "seq", 1)
        near = jnp.stack(in_order(list(near), me_far))
        other = jnp.stack(in_order(list(other), me_far))
        lanes = jnp.concatenate(in_order([near, other], me_core), axis=0)
        embedded.append(lanes.transpose(1, 0, 2).reshape(tokens, width))

    out_rows = out_proj.shape[0] // n_seq
    out_lane = lax.dynamic_slice_in_dim(out_proj, lane * out_rows, out_rows, axis=0)
    out_part = jnp.concatenate(in_order(exchange(out_lane, "dp"), me_dp), axis=1)
    out_part = jnp.stack(in_order(exchange(out_part, "head"), me_head))
    out_full = seq_lanes(out_part).transpose(1, 0, 2, 3).reshape(n_head * width_dev, width)

    depth_rows = depth_proj.shape[0] // n_seq
    depth_lane = lax.dynamic_slice_in_dim(depth_proj, lane * depth_rows, depth_rows, axis=0)
    depth_part = jnp.concatenate(in_order(exchange(depth_lane, "dp"), me_dp), axis=1)
    depth_part = jnp.concatenate(in_order(exchange(depth_part, "head"), me_head), axis=1)
    proj_mat = seq_lanes(depth_part).reshape(width, width)

    query_rows = queries[0].reshape(group_len, heads_here, DH)
    key_rows = keys[0].reshape(group_len, heads_here, DH)
    value_rows = values[0].reshape(group_len, heads_here, DH)
    places = jnp.arange(group_len, dtype=jnp.int32)
    causal = (places[:, None] >= places[None, :]).astype(F32)
    state_local = jnp.einsum("thd,the->hde", key_rows, value_rows, preferred_element_type=F32)
    state_in = earlier_sum(state_local, False)
    scores = (
        jnp.einsum("thd,shd->hts", query_rows, key_rows, preferred_element_type=F32) * causal
    ).astype(BF16)
    attended = (
        att_scale
        * (
            jnp.einsum("hts,she->the", scores, value_rows, preferred_element_type=F32)
            + jnp.einsum("thd,hde->the", query_rows, state_in, preferred_element_type=F32)
        )
    ).astype(BF16)
    attended = attended.reshape(n_head, tokens, width_dev)
    att_all = [pick(attended, me_head, 0)]
    att_all += [swap(pick(attended, me_head ^ k, 0), "head", k) for k in range(1, n_head)]
    att_all = jnp.concatenate(in_order(att_all, me_head), axis=1)
    mixed = dot(att_all, out_full, ((1,), (0,)))

    cot = depth_cotangent[0]
    n_level = cot.shape[1]
    carried = mixed
    kept = []
    for level in range(n_level):
        summed = carried + embedded[level].astype(F32)
        inv = lax.rsqrt(jnp.mean(summed * summed, axis=-1, keepdims=True) + 1e-05)
        if level < n_level - 1:
            projected = dot((summed * inv).astype(BF16), proj_mat, ((1,), (0,)))
            carried = summed + projected * jax.nn.sigmoid(projected)
        else:
            projected = None
        kept.append((summed, inv, projected))
    grad = None
    for level in reversed(range(n_level)):
        summed, inv, projected = kept[level]
        grad_proj = cot[:, level, :]
        if grad is not None:
            gate = jax.nn.sigmoid(projected)
            slope = gate * (1.0 + projected * (1.0 - gate))
            grad_proj = (grad_proj.astype(F32) + grad * slope).astype(BF16)
        grad_normed = dot(grad_proj, proj_mat, ((1,), (1,)))
        along = jnp.mean(grad_normed * summed, axis=-1, keepdims=True)
        grad_sum = grad_normed * inv - summed * (along * inv * inv * inv)
        grad = grad_sum if grad is None else grad + grad_sum
    grad_mixed = grad.astype(BF16)

    out_heads = out_full.reshape(n_head, width_dev, width)
    grad_rows = []
    for k in range(1, n_head):
        part = dot(grad_mixed, pick(out_heads, me_head ^ k, 0), ((1,), (1,))).astype(BF16)
        grad_rows.append(swap(part, "head", k))
    own_part = dot(grad_mixed, pick(out_heads, me_head, 0), ((1,), (1,))).astype(BF16)
    grad_rows = jnp.concatenate(in_order([own_part] + grad_rows, me_head), axis=0)
    grad_rows = grad_rows.reshape(group_len, heads_here, DH)

    rows = width_dev // n_seq
    att_lanes = att_all.reshape(tokens, n_head, 2, n_far, rows)

    def term(core):
        part = pick(att_lanes, core, 2).reshape(tokens, n_head * n_far * rows)
        return dot(part, grad_mixed, ((0,), (0,)))

    got = swap(term(1 - me_core).astype(BF16), "seq", 1)
    chip = term(me_core) + got.astype(F32)
    chip = chip.reshape(n_head, n_far, rows, width)
    total = pick(pick(chip, me_head, 0), me_far, 0)
    for m in far:
        for k in range(n_head):
            if m or k:
                piece = pick(pick(chip, me_head ^ k, 0), me_far ^ (m // 2), 0).astype(BF16)
                mask = m * n_head + k
                total = total + swap(piece, ("seq", "head"), mask).astype(F32)
    columns = total.reshape(rows, n_dp, width // n_dp)
    block = pick(columns, me_dp, 1)
    for k in range(1, n_dp):
        block = block + swap(pick(columns, me_dp ^ k, 1).astype(BF16), "dp", k).astype(F32)
    grad_out_proj = seq_lanes(block.astype(BF16)).reshape(width_dev, width // n_dp).astype(F32)

    back_local = jnp.einsum("thd,the->hde", query_rows, grad_rows, preferred_element_type=F32)
    back_state = earlier_sum(back_local, True)
    grad_scores = (
        jnp.einsum("the,she->hts", grad_rows, value_rows, preferred_element_type=F32) * causal
    ).astype(BF16)
    grad_query = att_scale * (
        jnp.einsum("hts,shd->thd", grad_scores, key_rows, preferred_element_type=F32)
        + jnp.einsum("the,hde->thd", grad_rows, state_in, preferred_element_type=F32)
    )
    grad_key = att_scale * (
        jnp.einsum("hts,thd->shd", grad_scores, query_rows, preferred_element_type=F32)
        + jnp.einsum("she,hde->shd", value_rows, back_state, preferred_element_type=F32)
    )
    grad_value = att_scale * (
        jnp.einsum("hts,the->she", scores, grad_rows, preferred_element_type=F32)
        + jnp.einsum("shd,hde->she", key_rows, back_state, preferred_element_type=F32)
    )
    out_shape = (1, group_len, width_dev)
    return (
        grad_query.reshape(out_shape).astype(BF16),
        grad_key.reshape(out_shape).astype(BF16),
        grad_value.reshape(out_shape).astype(BF16),
        grad_out_proj,
    )


def solution(mesh):
    in_specs = (
        P("dp", "seq", "head"),
        P("dp", "seq", "head"),
        P("dp", "seq", "head"),
        P("head", "dp"),
        P(None, ("head", "dp")),
        P(None, ("head", "dp"), None),
        P("dp", ("seq", "head"), None),
        P("dp", ("seq", "head"), None, None),
    )
    out_specs = (
        P("dp", "seq", "head"),
        P("dp", "seq", "head"),
        P("dp", "seq", "head"),
        P("head", "dp"),
    )
    return jax.shard_map(
        on_device, mesh=mesh, in_specs=in_specs, out_specs=out_specs, check_vma=False
    )
```

```python
import jax
import jax.numpy as jnp
from jax import lax
from jax.experimental import pallas as pl
from jax.experimental.pallas import tpu as pltpu
from jax.sharding import PartitionSpec as P

DH = 128
F32 = jnp.float32
BF16 = jnp.bfloat16


def swap(block, axis, mask):
    return lax.ppermute(block, axis, [(i, i ^ mask) for i in range(lax.axis_size(axis))])


def has_bit(index, bit):
    return lax.bitwise_and(index, jnp.int32(bit)) != 0


def in_order(pieces, index):
    pieces = list(pieces)
    bit = 1
    while bit < len(pieces):
        odd = has_bit(index, bit)
        pieces = [jnp.where(odd, pieces[j ^ bit], pieces[j]) for j in range(len(pieces))]
        bit *= 2
    return pieces


def pick(array, index, dim):
    return lax.dynamic_index_in_dim(array, index, dim, keepdims=False)


def exchange(block, axis):
    return [block] + [swap(block, axis, k) for k in range(1, lax.axis_size(axis))]


def dot(a, b, dims):
    return lax.dot_general(a, b, ((dims[0], dims[1]), ((), ())), preferred_element_type=F32)


def earlier_sum(state, backward):
    n_seq = lax.axis_size("seq")
    me = lax.axis_index("seq")
    before = jnp.zeros_like(state)
    total = state
    bit = 1
    while bit < n_seq:
        got = swap(total.astype(BF16), "seq", bit).astype(F32)
        mine = has_bit(me, bit)
        takes = jnp.logical_not(mine) if backward else mine
        before = before + jnp.where(takes, got, 0.0)
        total = total + got
        bit *= 2
    return before.astype(BF16)


def on_device_any(queries, keys, values, out_proj, depth_proj, code_table, code_ids, depth_cotangent):
    n_seq, n_head, n_dp = (lax.axis_size(a) for a in ("seq", "head", "dp"))
    me_seq, me_head, me_dp = (lax.axis_index(a) for a in ("seq", "head", "dp"))
    group_len, width_dev = queries.shape[1:]
    heads_here = width_dev // DH
    tokens = group_len // n_head
    n_far = n_seq // 2
    me_core = lax.bitwise_and(me_seq, jnp.int32(1))
    me_far = lax.shift_right_logical(me_seq, jnp.int32(1))
    lane = me_core * n_far + me_far
    att_scale = float(group_len * n_seq) ** (-0.5)
    width = code_table.shape[2]
    wide = width // n_seq
    far = [2 * m for m in range(n_far)]

    def far_exchange(block):
        return [block] + [swap(block, "seq", m) for m in far[1:]]

    def seq_lanes(block):
        near = jnp.stack(in_order(far_exchange(block), me_far))
        both = in_order([near, swap(near, "seq", 1)], me_core)
        return jnp.concatenate(both, axis=0)

    ids = code_ids[0].T
    ids_far = jnp.stack(far_exchange(ids))
    ids_rel = jnp.stack([ids_far, swap(ids_far, "seq", 1)])

    table = lax.dynamic_slice_in_dim(code_table, lane * wide, wide, axis=2)
    rows_dev = table.shape[1]
    embedded = []
    row_no = []
    for k_head in range(n_head):
        for k_dp in range(n_dp):
            owner = (me_head ^ k_head) * n_dp + (me_dp ^ k_dp)
            row_no.append(owner * rows_dev + jnp.arange(rows_dev, dtype=jnp.int32))
    row_no = jnp.concatenate(row_no)
    for level in range(table.shape[0]):
        part = jnp.concatenate(exchange(table[level], "dp"), axis=0)
        part = jnp.concatenate(exchange(part, "head"), axis=0)
        level_ids = ids_rel[:, :, level].reshape(-1)
        onehot = (level_ids[:, None] == row_no[None, :]).astype(BF16)
        rel = dot(onehot, part, ((1,), (0,))).astype(BF16).reshape(2, n_far, tokens, wide)
        mine = [rel[:, 0]] + [swap(rel[:, m // 2], "seq", m) for m in far[1:]]
        near = jnp.stack([block[0] for block in mine])
        other = swap(jnp.stack([block[1] for block in mine]), "seq", 1)
        near = jnp.stack(in_order(list(near), me_far))
        other = jnp.stack(in_order(list(other), me_far))
        lanes = jnp.concatenate(in_order([near, other], me_core), axis=0)
        embedded.append(lanes.transpose(1, 0, 2).reshape(tokens, width))

    out_rows = out_proj.shape[0] // n_seq
    out_lane = lax.dynamic_slice_in_dim(out_proj, lane * out_rows, out_rows, axis=0)
    out_part = jnp.concatenate(in_order(exchange(out_lane, "dp"), me_dp), axis=1)
    out_part = jnp.stack(in_order(exchange(out_part, "head"), me_head))
    out_full = seq_lanes(out_part).transpose(1, 0, 2, 3).reshape(n_head * width_dev, width)

    depth_rows = depth_proj.shape[0] // n_seq
    depth_lane = lax.dynamic_slice_in_dim(depth_proj, lane * depth_rows, depth_rows, axis=0)
    depth_part = jnp.concatenate(in_order(exchange(depth_lane, "dp"), me_dp), axis=1)
    depth_part = jnp.concatenate(in_order(exchange(depth_part, "head"), me_head), axis=1)
    proj_mat = seq_lanes(depth_part).reshape(width, width)

    query_rows = queries[0].reshape(group_len, heads_here, DH)
    key_rows = keys[0].reshape(group_len, heads_here, DH)
    value_rows = values[0].reshape(group_len, heads_here, DH)
    places = jnp.arange(group_len, dtype=jnp.int32)
    causal = (places[:, None] >= places[None, :]).astype(F32)
    state_local = jnp.einsum("thd,the->hde", key_rows, value_rows, preferred_element_type=F32)
    state_in = earlier_sum(state_local, False)
    scores = (
        jnp.einsum("thd,shd->hts", query_rows, key_rows, preferred_element_type=F32) * causal
    ).astype(BF16)
    attended = (
        att_scale
        * (
            jnp.einsum("hts,she->the", scores, value_rows, preferred_element_type=F32)
            + jnp.einsum("thd,hde->the", query_rows, state_in, preferred_element_type=F32)
        )
    ).astype(BF16)
    attended = attended.reshape(n_head, tokens, width_dev)
    att_all = [pick(attended, me_head, 0)]
    att_all += [swap(pick(attended, me_head ^ k, 0), "head", k) for k in range(1, n_head)]
    att_all = jnp.concatenate(in_order(att_all, me_head), axis=1)
    mixed = dot(att_all, out_full, ((1,), (0,)))

    cot = depth_cotangent[0]
    n_level = cot.shape[1]
    carried = mixed
    kept = []
    for level in range(n_level):
        summed = carried + embedded[level].astype(F32)
        inv = lax.rsqrt(jnp.mean(summed * summed, axis=-1, keepdims=True) + 1e-05)
        if level < n_level - 1:
            projected = dot((summed * inv).astype(BF16), proj_mat, ((1,), (0,)))
            carried = summed + projected * jax.nn.sigmoid(projected)
        else:
            projected = None
        kept.append((summed, inv, projected))
    grad = None
    for level in reversed(range(n_level)):
        summed, inv, projected = kept[level]
        grad_proj = cot[:, level, :]
        if grad is not None:
            gate = jax.nn.sigmoid(projected)
            slope = gate * (1.0 + projected * (1.0 - gate))
            grad_proj = (grad_proj.astype(F32) + grad * slope).astype(BF16)
        grad_normed = dot(grad_proj, proj_mat, ((1,), (1,)))
        along = jnp.mean(grad_normed * summed, axis=-1, keepdims=True)
        grad_sum = grad_normed * inv - summed * (along * inv * inv * inv)
        grad = grad_sum if grad is None else grad + grad_sum
    grad_mixed = grad.astype(BF16)

    out_heads = out_full.reshape(n_head, width_dev, width)
    grad_rows = []
    for k in range(1, n_head):
        part = dot(grad_mixed, pick(out_heads, me_head ^ k, 0), ((1,), (1,))).astype(BF16)
        grad_rows.append(swap(part, "head", k))
    own_part = dot(grad_mixed, pick(out_heads, me_head, 0), ((1,), (1,))).astype(BF16)
    grad_rows = jnp.concatenate(in_order([own_part] + grad_rows, me_head), axis=0)
    grad_rows = grad_rows.reshape(group_len, heads_here, DH)

    rows = width_dev // n_seq
    att_lanes = att_all.reshape(tokens, n_head, 2, n_far, rows)

    def term(core):
        part = pick(att_lanes, core, 2).reshape(tokens, n_head * n_far * rows)
        return dot(part, grad_mixed, ((0,), (0,)))

    got = swap(term(1 - me_core).astype(BF16), "seq", 1)
    chip = term(me_core) + got.astype(F32)
    chip = chip.reshape(n_head, n_far, rows, width)
    total = pick(pick(chip, me_head, 0), me_far, 0)
    for m in far:
        for k in range(n_head):
            if m or k:
                piece = pick(pick(chip, me_head ^ k, 0), me_far ^ (m // 2), 0).astype(BF16)
                mask = m * n_head + k
                total = total + swap(piece, ("seq", "head"), mask).astype(F32)
    columns = total.reshape(rows, n_dp, width // n_dp)
    block = pick(columns, me_dp, 1)
    for k in range(1, n_dp):
        block = block + swap(pick(columns, me_dp ^ k, 1).astype(BF16), "dp", k).astype(F32)
    grad_out_proj = seq_lanes(block.astype(BF16)).reshape(width_dev, width // n_dp).astype(F32)

    back_local = jnp.einsum("thd,the->hde", query_rows, grad_rows, preferred_element_type=F32)
    back_state = earlier_sum(back_local, True)
    grad_scores = (
        jnp.einsum("the,she->hts", grad_rows, value_rows, preferred_element_type=F32) * causal
    ).astype(BF16)
    grad_query = att_scale * (
        jnp.einsum("hts,shd->thd", grad_scores, key_rows, preferred_element_type=F32)
        + jnp.einsum("the,hde->thd", grad_rows, state_in, preferred_element_type=F32)
    )
    grad_key = att_scale * (
        jnp.einsum("hts,thd->shd", grad_scores, query_rows, preferred_element_type=F32)
        + jnp.einsum("she,hde->shd", value_rows, back_state, preferred_element_type=F32)
    )
    grad_value = att_scale * (
        jnp.einsum("hts,the->she", scores, grad_rows, preferred_element_type=F32)
        + jnp.einsum("shd,hde->she", key_rows, back_state, preferred_element_type=F32)
    )
    out_shape = (1, group_len, width_dev)
    return (
        grad_query.reshape(out_shape).astype(BF16),
        grad_key.reshape(out_shape).astype(BF16),
        grad_value.reshape(out_shape).astype(BF16),
        grad_out_proj,
    )


VMEM_BYTES = 48 * 1024 * 1024


def run(body, outs, where, *args):
    vmem = pl.BlockSpec(memory_space=pltpu.VMEM)
    return pl.pallas_call(
        body,
        out_shape=outs,
        in_specs=[pl.BlockSpec(memory_space=pltpu.SMEM)] + [vmem] * len(args),
        out_specs=[vmem] * len(outs),
        compiler_params=pltpu.CompilerParams(vmem_limit_bytes=VMEM_BYTES),
    )(where, *args)


def shaped(shape, dtype=BF16):
    return jax.ShapeDtypeStruct(shape, dtype)


def at(index, size):
    return pl.ds(pl.multiple_of(index * size, size), size)


HEAD, DP = 4, 5


def prepare(where, out_proj, depth_proj, code_table):
    rows, cols = out_proj.shape
    d_rows, d_cols = depth_proj.shape
    n_level, t_rows, t_cols = code_table.shape
    rows, d_rows, t_cols = rows // 4, d_rows // 4, t_cols // 4

    def body(where_ref, o_ref, d_ref, t_ref, o_out, d_out, *t_out):
        o_out[...] = o_ref[...]
        d_out[...] = d_ref[...]
        for level, out in enumerate(t_out):
            out[...] = t_ref[level]

    def whole(shape):
        return pl.BlockSpec(shape, lambda i, w: (0,) * len(shape))

    return pl.pallas_call(
        body,
        out_shape=[shaped((rows, cols)), shaped((d_rows, d_cols))] + [shaped((t_rows, t_cols))] * n_level,
        grid_spec=pltpu.PrefetchScalarGridSpec(
            num_scalar_prefetch=1,
            grid=(1,),
            in_specs=[
                pl.BlockSpec((rows, cols), lambda i, w: (w[0], 0)),
                pl.BlockSpec((d_rows, d_cols), lambda i, w: (w[0], 0)),
                pl.BlockSpec((n_level, t_rows, t_cols), lambda i, w: (0, 0, w[0])),
            ],
            out_specs=[whole((rows, cols)), whole((d_rows, d_cols))] + [whole((t_rows, t_cols))] * n_level,
        ),
    )(where, out_proj, depth_proj, code_table)


def side_by_side(where, pieces):
    rows, cols = pieces[0].shape

    def body(where_ref, *refs):
        out = refs[-1]
        for k, ref in enumerate(refs[:-1]):
            out[:, at(where_ref[DP] ^ k, cols)] = ref[...]

    return run(body, [shaped((rows, cols * len(pieces)))], where, *pieces)[0]


def stacked(where, pieces):
    rows, cols = pieces[0].shape

    def body(where_ref, *refs):
        for k, ref in enumerate(refs[:-1]):
            refs[-1][k * rows:(k + 1) * rows, :] = ref[...]

    return run(body, [shaped((rows * len(pieces), cols))], where, *pieces)[0]


def embed(where, ids, own, got, n_dp):
    tokens = ids.shape[1]
    half, cols = own.shape
    rows_dev = half // n_dp

    def body(where_ref, ids_ref, own_ref, got_ref, *outs):
        place = lax.broadcasted_iota(jnp.int32, (tokens, half), 1)
        piece = place // rows_dev
        within = place % rows_dev
        owner = jnp.bitwise_xor(piece, where_ref[DP])
        base = owner * rows_dev + within
        columns = ids_ref[...].T
        for m, out in enumerate(outs):
            col = columns[:, m:m + 1]
            total = None
            for k, ref in enumerate((own_ref, got_ref)):
                start = (where_ref[HEAD] ^ k) * half
                hot = (base == col - start).astype(F32).astype(BF16)
                part = jnp.dot(hot, ref[...], preferred_element_type=F32)
                total = part if total is None else total + part
            out[...] = total.astype(BF16)

    return run(body, [shaped((tokens, cols))] * 4, where, ids, own, got)


def lanes_together(where, pieces):
    rows, cols = pieces[0].shape

    def body(where_ref, *refs):
        for m, ref in enumerate(refs[:-1]):
            refs[-1][:, at(where_ref[m], cols)] = ref[...]

    return run(body, [shaped((rows, cols * 4))], where, *pieces)[0]


def depth_together(where, blocks, cot):
    rows, cols = blocks[0].shape
    width = rows * 4
    last = cot.shape[1] // width - 1

    def body(where_ref, *refs):
        cot_ref, full, grad = refs[8:]
        for m in range(4):
            for x in range(2):
                full[at(where_ref[m], rows), at(where_ref[HEAD] ^ x, cols)] = refs[2 * m + x][...]
        cot_last = cot_ref[:, last * width:(last + 1) * width]
        grad[...] = dot(cot_last, full[...], ((1,), (1,)))

    return run(body, [shaped((width, width)), shaped((cot.shape[0], width), F32)], where, *blocks, cot)


def local_states(where, keys, values, dtype=BF16):
    heads = keys.shape[1] // DH

    def body(where_ref, k_ref, v_ref, out):
        for i in range(heads):
            cut = slice(i * DH, (i + 1) * DH)
            out[i] = dot(k_ref[:, cut], v_ref[:, cut], ((0,), (0,))).astype(dtype)

    return run(body, [shaped((heads, DH, DH), dtype)], where, keys, values)[0]


def lower(size):
    rows = lax.broadcasted_iota(jnp.int32, (size, size), 0)
    cols = lax.broadcasted_iota(jnp.int32, (size, size), 1)
    return rows >= cols


def upper(size):
    rows = lax.broadcasted_iota(jnp.int32, (size, size), 0)
    cols = lax.broadcasted_iota(jnp.int32, (size, size), 1)
    return rows <= cols


def attend(where, queries, keys, values, from_core, from_far, att_scale):
    length, width_dev = queries.shape
    heads = width_dev // DH

    def body(where_ref, q_ref, k_ref, v_ref, core_ref, far_ref, att, state):
        near = (where_ref[0] // 2).astype(F32)
        far = (where_ref[0] % 2).astype(F32)
        keep = lower(length)
        for i in range(heads):
            cut = slice(i * DH, (i + 1) * DH)
            state[i] = (core_ref[i].astype(F32) * near + far_ref[i].astype(F32) * far).astype(BF16)
            q = q_ref[:, cut]
            scores = jnp.where(keep, dot(q, k_ref[:, cut], ((1,), (1,))), 0.0).astype(BF16)
            both = jnp.dot(scores, v_ref[:, cut], preferred_element_type=F32)
            both += jnp.dot(q, state[i], preferred_element_type=F32)
            att[:, cut] = (att_scale * both).astype(BF16)

    return run(
        body, [shaped((length, width_dev)), shaped((heads, DH, DH))], where, queries, keys, values, from_core, from_far
    )


def mix(where, attended, blocks, other):
    length = attended.shape[0] // 2
    width = blocks[0].shape[1]
    dtype = BF16 if other else F32

    def body(where_ref, att, *refs):
        rows = at(where_ref[HEAD] ^ (1 if other else 0), length)
        total = None
        for m in range(4):
            part = jnp.dot(att[rows, at(where_ref[m], DH)], refs[m][...], preferred_element_type=F32)
            total = part if total is None else total + part
        refs[-1][...] = total.astype(dtype)

    return run(body, [shaped((length, width), dtype)], where, attended, *blocks)[0]


def weight_terms(where, attended, grad_own, grad_got):
    tokens, width = grad_own.shape

    def body(where_ref, att, own, got, send, keep):
        def term(m):
            total = None
            for k, ref in enumerate((own, got)):
                a = att[at(where_ref[HEAD] ^ k, tokens), at(where_ref[m], DH)]
                part = dot(a, ref[...], ((0,), (0,)))
                total = part if total is None else total + part
            return total

        send[0] = term(2).astype(BF16)
        send[1] = term(3).astype(BF16)
        keep[0] = term(0)
        keep[1] = term(1)

    return run(
        body, [shaped((2, DH, width)), shaped((2, DH, width), F32)], where, attended, grad_own, grad_got
    )


def add_core(where, keep, got):
    shape = keep.shape[1:]

    def body(where_ref, keep_ref, got_ref, send, rest):
        rest[...] = keep_ref[0] + got_ref[0].astype(F32)
        send[...] = (keep_ref[1] + got_ref[1].astype(F32)).astype(BF16)

    return run(body, [shaped(shape), shaped(shape, F32)], where, keep, got)


def add_far(where, keep, got, n_dp):
    rows, width = keep.shape
    cols = width // n_dp

    def body(where_ref, keep_ref, got_ref, rest, *send):
        for k in range(n_dp):
            cut = at(where_ref[DP] ^ k, cols)
            total = keep_ref[:, cut] + got_ref[:, cut].astype(F32)
            if k:
                send[k - 1][...] = total.astype(BF16)
            else:
                rest[...] = total

    return run(body, [shaped((rows, cols), F32)] + [shaped((rows, cols))] * (n_dp - 1), where, keep, got)


def add_all(where, keep, got):
    def body(where_ref, keep_ref, *refs):
        total = keep_ref[...]
        for ref in refs[:-1]:
            total = total + ref[...].astype(F32)
        refs[-1][...] = total.astype(BF16)

    return run(body, [shaped(keep.shape)], where, keep, *got)[0]


def rows_together(where, pieces):
    rows, cols = pieces[0].shape

    def body(where_ref, *refs):
        for m, ref in enumerate(refs[:-1]):
            refs[-1][at(where_ref[m], rows), :] = ref[...].astype(F32)

    return run(body, [shaped((rows * 4, cols), F32)], where, *pieces)[0]


def grad_attend(where, grad_own, grad_got, blocks, queries):
    tokens, width = grad_own.shape
    length, width_dev = queries.shape

    def body(where_ref, own, got, o0, o1, o2, o3, q_ref, rows, back):
        for m, block in enumerate((o0, o1, o2, o3)):
            for k, ref in enumerate((own, got)):
                part = dot(ref[...], block[...], ((1,), (1,))).astype(BF16)
                rows[at(where_ref[HEAD] ^ k, tokens), at(where_ref[m], DH)] = part
        for i in range(width_dev // DH):
            cut = slice(i * DH, (i + 1) * DH)
            back[i] = dot(q_ref[:, cut], rows[:, cut], ((0,), (0,))).astype(BF16)

    outs = [shaped((length, width_dev)), shaped((width_dev // DH, DH, DH))]
    return run(body, outs, where, grad_own, grad_got, *blocks, queries)


def query_grads(where, grad_rows, keys, values, state, att_scale):
    length, width_dev = keys.shape

    def body(where_ref, g_ref, k_ref, v_ref, s_ref, out):
        keep = lower(length)
        for i in range(width_dev // DH):
            cut = slice(i * DH, (i + 1) * DH)
            g = g_ref[:, cut]
            scores = jnp.where(keep, dot(g, v_ref[:, cut], ((1,), (1,))), 0.0).astype(BF16)
            both = jnp.dot(scores, k_ref[:, cut], preferred_element_type=F32)
            both += dot(g, s_ref[i], ((1,), (1,)))
            out[:, cut] = (att_scale * both).astype(BF16)

    return run(body, [shaped((length, width_dev))], where, grad_rows, keys, values, state)[0]


def key_value_grads(where, grad_rows, queries, keys, values, from_core, from_far, att_scale):
    length, width_dev = keys.shape

    def body(where_ref, g_ref, q_ref, k_ref, v_ref, core_ref, far_ref, dk, dv):
        near = 1.0 - (where_ref[0] // 2).astype(F32)
        far = 1.0 - (where_ref[0] % 2).astype(F32)
        keep = upper(length)
        for i in range(width_dev // DH):
            cut = slice(i * DH, (i + 1) * DH)
            g, q, k, v = g_ref[:, cut], q_ref[:, cut], k_ref[:, cut], v_ref[:, cut]
            back = (core_ref[i].astype(F32) * near + far_ref[i].astype(F32) * far).astype(BF16)
            grad_scores = jnp.where(keep, dot(v, g, ((1,), (1,))), 0.0).astype(BF16)
            both = jnp.dot(grad_scores, q, preferred_element_type=F32)
            both += dot(v, back, ((1,), (1,)))
            dk[:, cut] = (att_scale * both).astype(BF16)
            scores = jnp.where(keep, dot(k, q, ((1,), (1,))), 0.0).astype(BF16)
            both = jnp.dot(scores, g, preferred_element_type=F32)
            both += jnp.dot(k, back, preferred_element_type=F32)
            dv[:, cut] = (att_scale * both).astype(BF16)

    outs = [shaped((length, width_dev))] * 2
    return run(body, outs, where, grad_rows, queries, keys, values, from_core, from_far)


def fits(queries, out_proj, depth_proj, code_table):
    n_seq, n_head = lax.axis_size("seq"), lax.axis_size("head")
    return (
        n_seq == 4
        and n_head == 2
        and queries.shape[2] == 4 * DH
        and code_table.shape[0] == 2
        and out_proj.shape[1] % 128 == 0
        and depth_proj.shape[1] % 128 == 0
        and code_table.shape[1] % 128 == 0
    )


def on_device(queries, keys, values, out_proj, depth_proj, code_table, code_ids, depth_cotangent):
    if not fits(queries, out_proj, depth_proj, code_table):
        return on_device_any(
            queries, keys, values, out_proj, depth_proj, code_table, code_ids, depth_cotangent
        )
    n_dp = lax.axis_size("dp")
    me_seq, me_head, me_dp = (lax.axis_index(a) for a in ("seq", "head", "dp"))
    group_len = queries.shape[1]
    width = code_table.shape[2]
    att_scale = float(group_len * lax.axis_size("seq")) ** (-0.5)
    core, far = me_seq % 2, me_seq // 2
    lane = 2 * core + far
    where = jnp.stack([lane, lane ^ 1, lane ^ 2, lane ^ 3, me_head, me_dp]).astype(jnp.int32)
    queries, keys, values = queries[0], keys[0], values[0]

    def far_swap(block):
        return swap(block, "seq", 2)

    def core_swap(block):
        return swap(block, "seq", 1)

    def all_lanes(block):
        got = far_swap(block)
        return [block, got, core_swap(block), core_swap(got)]

    out_lane, depth_lane, *table_lanes = prepare(where, out_proj, depth_proj, code_table)
    ids = code_ids[0].T
    ids_rel = all_lanes(ids)

    out_part = side_by_side(where, exchange(out_lane, "dp"))
    out_blocks = all_lanes(out_part)

    depth_part = side_by_side(where, exchange(depth_lane, "dp"))
    depth_got = swap(depth_part, "head", 1)
    own_lanes, got_lanes = all_lanes(depth_part), all_lanes(depth_got)
    depth_blocks = [block for pair in zip(own_lanes, got_lanes) for block in pair]

    embedded = []
    for level, table in enumerate(table_lanes):
        part = stacked(where, exchange(table, "dp"))
        got = swap(part, "head", 1)
        level_ids = jnp.stack([i[level] for i in ids_rel])
        for_own, for_far, for_core, for_core_far = embed(where, level_ids, part, got, n_dp)
        from_far, pass_on = far_swap(for_far), far_swap(for_core_far)
        pieces = [for_own, from_far, core_swap(for_core), core_swap(pass_on)]
        embedded.append(lanes_together(where, pieces))

    state = local_states(where, keys, values)
    state_core = core_swap(state)
    chip = (state.astype(F32) + state_core.astype(F32)).astype(BF16)
    state_far = far_swap(chip)
    attended, state_in = attend(where, queries, keys, values, state_core, state_far, att_scale)

    mixed_got = swap(mix(where, attended, out_blocks, True), "head", 1)
    mixed = mix(where, attended, out_blocks, False) + mixed_got.astype(F32)

    cot = depth_cotangent[0].reshape(depth_cotangent.shape[1], -1)
    proj_mat, grad_last = depth_together(where, depth_blocks, cot)
    sum_0 = mixed + embedded[0].astype(F32)
    inv_0 = lax.rsqrt(jnp.mean(sum_0 * sum_0, axis=-1, keepdims=True) + 1e-05)
    projected = dot((sum_0 * inv_0).astype(BF16), proj_mat, ((1,), (0,)))
    gate = jax.nn.sigmoid(projected)
    sum_1 = sum_0 + projected * gate + embedded[1].astype(F32)
    inv_1 = lax.rsqrt(jnp.mean(sum_1 * sum_1, axis=-1, keepdims=True) + 1e-05)
    along = jnp.mean(grad_last * sum_1, axis=-1, keepdims=True)
    grad = grad_last * inv_1 - sum_1 * (along * inv_1 * inv_1 * inv_1)
    slope = gate * (1.0 + projected * (1.0 - gate))
    grad_proj = (cot[:, :width].astype(F32) + grad * slope).astype(BF16)
    grad_normed = dot(grad_proj, proj_mat, ((1,), (1,)))
    along = jnp.mean(grad_normed * sum_0, axis=-1, keepdims=True)
    grad = grad + grad_normed * inv_0 - sum_0 * (along * inv_0 * inv_0 * inv_0)
    grad_mixed = grad.astype(BF16)

    grad_got = swap(grad_mixed, "head", 1)
    send, keep = weight_terms(where, attended, grad_mixed, grad_got)
    send, keep = add_core(where, keep, core_swap(send))
    keep, *send = add_far(where, keep, far_swap(send), n_dp)
    block = add_all(where, keep, [swap(s, "dp", k + 1) for k, s in enumerate(send)])
    grad_out_proj = rows_together(where, all_lanes(block))

    grad_rows, back = grad_attend(where, grad_mixed, grad_got, out_blocks, queries)
    back_core = core_swap(back)
    back_far = far_swap((back.astype(F32) + back_core.astype(F32)).astype(BF16))
    grad_query = query_grads(where, grad_rows, keys, values, state_in, att_scale)
    grad_key, grad_value = key_value_grads(
        where, grad_rows, queries, keys, values, back_core, back_far, att_scale
    )
    return grad_query[None], grad_key[None], grad_value[None], grad_out_proj


def solution(mesh):
    in_specs = (
        P("dp", "seq", "head"),
        P("dp", "seq", "head"),
        P("dp", "seq", "head"),
        P("head", "dp"),
        P(None, ("head", "dp")),
        P(None, ("head", "dp"), None),
        P("dp", ("seq", "head"), None),
        P("dp", ("seq", "head"), None, None),
    )
    out_specs = (
        P("dp", "seq", "head"),
        P("dp", "seq", "head"),
        P("dp", "seq", "head"),
        P("head", "dp"),
    )
    return jax.shard_map(
        on_device, mesh=mesh, in_specs=in_specs, out_specs=out_specs, check_vma=False
    )
```

```python
import jax
import jax.numpy as jnp
from jax import lax
from jax.experimental import pallas as pl
from jax.experimental.pallas import tpu as pltpu
from jax.sharding import PartitionSpec as P

DH = 128
F32 = jnp.float32
BF16 = jnp.bfloat16


def swap(block, axis, mask):
    return lax.ppermute(block, axis, [(i, i ^ mask) for i in range(lax.axis_size(axis))])


def has_bit(index, bit):
    return lax.bitwise_and(index, jnp.int32(bit)) != 0


def in_order(pieces, index):
    pieces = list(pieces)
    bit = 1
    while bit < len(pieces):
        odd = has_bit(index, bit)
        pieces = [jnp.where(odd, pieces[j ^ bit], pieces[j]) for j in range(len(pieces))]
        bit *= 2
    return pieces


def pick(array, index, dim):
    return lax.dynamic_index_in_dim(array, index, dim, keepdims=False)


def exchange(block, axis):
    return [block] + [swap(block, axis, k) for k in range(1, lax.axis_size(axis))]


def dot(a, b, dims):
    return lax.dot_general(a, b, ((dims[0], dims[1]), ((), ())), preferred_element_type=F32)


def earlier_sum(state, backward):
    n_seq = lax.axis_size("seq")
    me = lax.axis_index("seq")
    before = jnp.zeros_like(state)
    total = state
    bit = 1
    while bit < n_seq:
        got = swap(total.astype(BF16), "seq", bit).astype(F32)
        mine = has_bit(me, bit)
        takes = jnp.logical_not(mine) if backward else mine
        before = before + jnp.where(takes, got, 0.0)
        total = total + got
        bit *= 2
    return before.astype(BF16)


def on_device_any(queries, keys, values, out_proj, depth_proj, code_table, code_ids, depth_cotangent):
    n_seq, n_head, n_dp = (lax.axis_size(a) for a in ("seq", "head", "dp"))
    me_seq, me_head, me_dp = (lax.axis_index(a) for a in ("seq", "head", "dp"))
    group_len, width_dev = queries.shape[1:]
    heads_here = width_dev // DH
    tokens = group_len // n_head
    n_far = n_seq // 2
    me_core = lax.bitwise_and(me_seq, jnp.int32(1))
    me_far = lax.shift_right_logical(me_seq, jnp.int32(1))
    lane = me_core * n_far + me_far
    att_scale = float(group_len * n_seq) ** (-0.5)
    width = code_table.shape[2]
    wide = width // n_seq
    far = [2 * m for m in range(n_far)]

    def far_exchange(block):
        return [block] + [swap(block, "seq", m) for m in far[1:]]

    def seq_lanes(block):
        near = jnp.stack(in_order(far_exchange(block), me_far))
        both = in_order([near, swap(near, "seq", 1)], me_core)
        return jnp.concatenate(both, axis=0)

    ids = code_ids[0].T
    ids_far = jnp.stack(far_exchange(ids))
    ids_rel = jnp.stack([ids_far, swap(ids_far, "seq", 1)])

    table = lax.dynamic_slice_in_dim(code_table, lane * wide, wide, axis=2)
    rows_dev = table.shape[1]
    embedded = []
    row_no = []
    for k_head in range(n_head):
        for k_dp in range(n_dp):
            owner = (me_head ^ k_head) * n_dp + (me_dp ^ k_dp)
            row_no.append(owner * rows_dev + jnp.arange(rows_dev, dtype=jnp.int32))
    row_no = jnp.concatenate(row_no)
    for level in range(table.shape[0]):
        part = jnp.concatenate(exchange(table[level], "dp"), axis=0)
        part = jnp.concatenate(exchange(part, "head"), axis=0)
        level_ids = ids_rel[:, :, level].reshape(-1)
        onehot = (level_ids[:, None] == row_no[None, :]).astype(BF16)
        rel = dot(onehot, part, ((1,), (0,))).astype(BF16).reshape(2, n_far, tokens, wide)
        mine = [rel[:, 0]] + [swap(rel[:, m // 2], "seq", m) for m in far[1:]]
        near = jnp.stack([block[0] for block in mine])
        other = swap(jnp.stack([block[1] for block in mine]), "seq", 1)
        near = jnp.stack(in_order(list(near), me_far))
        other = jnp.stack(in_order(list(other), me_far))
        lanes = jnp.concatenate(in_order([near, other], me_core), axis=0)
        embedded.append(lanes.transpose(1, 0, 2).reshape(tokens, width))

    out_rows = out_proj.shape[0] // n_seq
    out_lane = lax.dynamic_slice_in_dim(out_proj, lane * out_rows, out_rows, axis=0)
    out_part = jnp.concatenate(in_order(exchange(out_lane, "dp"), me_dp), axis=1)
    out_part = jnp.stack(in_order(exchange(out_part, "head"), me_head))
    out_full = seq_lanes(out_part).transpose(1, 0, 2, 3).reshape(n_head * width_dev, width)

    depth_rows = depth_proj.shape[0] // n_seq
    depth_lane = lax.dynamic_slice_in_dim(depth_proj, lane * depth_rows, depth_rows, axis=0)
    depth_part = jnp.concatenate(in_order(exchange(depth_lane, "dp"), me_dp), axis=1)
    depth_part = jnp.concatenate(in_order(exchange(depth_part, "head"), me_head), axis=1)
    proj_mat = seq_lanes(depth_part).reshape(width, width)

    query_rows = queries[0].reshape(group_len, heads_here, DH)
    key_rows = keys[0].reshape(group_len, heads_here, DH)
    value_rows = values[0].reshape(group_len, heads_here, DH)
    places = jnp.arange(group_len, dtype=jnp.int32)
    causal = (places[:, None] >= places[None, :]).astype(F32)
    state_local = jnp.einsum("thd,the->hde", key_rows, value_rows, preferred_element_type=F32)
    state_in = earlier_sum(state_local, False)
    scores = (
        jnp.einsum("thd,shd->hts", query_rows, key_rows, preferred_element_type=F32) * causal
    ).astype(BF16)
    attended = (
        att_scale
        * (
            jnp.einsum("hts,she->the", scores, value_rows, preferred_element_type=F32)
            + jnp.einsum("thd,hde->the", query_rows, state_in, preferred_element_type=F32)
        )
    ).astype(BF16)
    attended = attended.reshape(n_head, tokens, width_dev)
    att_all = [pick(attended, me_head, 0)]
    att_all += [swap(pick(attended, me_head ^ k, 0), "head", k) for k in range(1, n_head)]
    att_all = jnp.concatenate(in_order(att_all, me_head), axis=1)
    mixed = dot(att_all, out_full, ((1,), (0,)))

    cot = depth_cotangent[0]
    n_level = cot.shape[1]
    carried = mixed
    kept = []
    for level in range(n_level):
        summed = carried + embedded[level].astype(F32)
        inv = lax.rsqrt(jnp.mean(summed * summed, axis=-1, keepdims=True) + 1e-05)
        if level < n_level - 1:
            projected = dot((summed * inv).astype(BF16), proj_mat, ((1,), (0,)))
            carried = summed + projected * jax.nn.sigmoid(projected)
        else:
            projected = None
        kept.append((summed, inv, projected))
    grad = None
    for level in reversed(range(n_level)):
        summed, inv, projected = kept[level]
        grad_proj = cot[:, level, :]
        if grad is not None:
            gate = jax.nn.sigmoid(projected)
            slope = gate * (1.0 + projected * (1.0 - gate))
            grad_proj = (grad_proj.astype(F32) + grad * slope).astype(BF16)
        grad_normed = dot(grad_proj, proj_mat, ((1,), (1,)))
        along = jnp.mean(grad_normed * summed, axis=-1, keepdims=True)
        grad_sum = grad_normed * inv - summed * (along * inv * inv * inv)
        grad = grad_sum if grad is None else grad + grad_sum
    grad_mixed = grad.astype(BF16)

    out_heads = out_full.reshape(n_head, width_dev, width)
    grad_rows = []
    for k in range(1, n_head):
        part = dot(grad_mixed, pick(out_heads, me_head ^ k, 0), ((1,), (1,))).astype(BF16)
        grad_rows.append(swap(part, "head", k))
    own_part = dot(grad_mixed, pick(out_heads, me_head, 0), ((1,), (1,))).astype(BF16)
    grad_rows = jnp.concatenate(in_order([own_part] + grad_rows, me_head), axis=0)
    grad_rows = grad_rows.reshape(group_len, heads_here, DH)

    rows = width_dev // n_seq
    att_lanes = att_all.reshape(tokens, n_head, 2, n_far, rows)

    def term(core):
        part = pick(att_lanes, core, 2).reshape(tokens, n_head * n_far * rows)
        return dot(part, grad_mixed, ((0,), (0,)))

    got = swap(term(1 - me_core).astype(BF16), "seq", 1)
    chip = term(me_core) + got.astype(F32)
    chip = chip.reshape(n_head, n_far, rows, width)
    total = pick(pick(chip, me_head, 0), me_far, 0)
    for m in far:
        for k in range(n_head):
            if m or k:
                piece = pick(pick(chip, me_head ^ k, 0), me_far ^ (m // 2), 0).astype(BF16)
                mask = m * n_head + k
                total = total + swap(piece, ("seq", "head"), mask).astype(F32)
    columns = total.reshape(rows, n_dp, width // n_dp)
    block = pick(columns, me_dp, 1)
    for k in range(1, n_dp):
        block = block + swap(pick(columns, me_dp ^ k, 1).astype(BF16), "dp", k).astype(F32)
    grad_out_proj = seq_lanes(block.astype(BF16)).reshape(width_dev, width // n_dp).astype(F32)

    back_local = jnp.einsum("thd,the->hde", query_rows, grad_rows, preferred_element_type=F32)
    back_state = earlier_sum(back_local, True)
    grad_scores = (
        jnp.einsum("the,she->hts", grad_rows, value_rows, preferred_element_type=F32) * causal
    ).astype(BF16)
    grad_query = att_scale * (
        jnp.einsum("hts,shd->thd", grad_scores, key_rows, preferred_element_type=F32)
        + jnp.einsum("the,hde->thd", grad_rows, state_in, preferred_element_type=F32)
    )
    grad_key = att_scale * (
        jnp.einsum("hts,thd->shd", grad_scores, query_rows, preferred_element_type=F32)
        + jnp.einsum("she,hde->shd", value_rows, back_state, preferred_element_type=F32)
    )
    grad_value = att_scale * (
        jnp.einsum("hts,the->she", scores, grad_rows, preferred_element_type=F32)
        + jnp.einsum("shd,hde->she", key_rows, back_state, preferred_element_type=F32)
    )
    out_shape = (1, group_len, width_dev)
    return (
        grad_query.reshape(out_shape).astype(BF16),
        grad_key.reshape(out_shape).astype(BF16),
        grad_value.reshape(out_shape).astype(BF16),
        grad_out_proj,
    )


VMEM_BYTES = 48 * 1024 * 1024


def run(body, outs, where, *args):
    vmem = pl.BlockSpec(memory_space=pltpu.VMEM)
    return pl.pallas_call(
        body,
        out_shape=outs,
        in_specs=[pl.BlockSpec(memory_space=pltpu.SMEM)] + [vmem] * len(args),
        out_specs=[vmem] * len(outs),
        compiler_params=pltpu.CompilerParams(vmem_limit_bytes=VMEM_BYTES),
    )(where, *args)


def shaped(shape, dtype=BF16):
    return jax.ShapeDtypeStruct(shape, dtype)


def at(index, size):
    return pl.ds(pl.multiple_of(index * size, size), size)


HEAD, DP, SEQ = 4, 5, 6


def own_lane():
    me = lax.axis_index("seq")
    return 2 * (me % 2) + me // 2


def copies(body_of, outs, args):
    n_copies = len(body_of(None))

    def body(*refs):
        sems = refs[-1]
        going = [pltpu.make_async_copy(src, dst, sems.at[i]) for i, (src, dst) in enumerate(body_of(refs[:-1]))]
        for copy in going:
            copy.start()
        for copy in going:
            copy.wait()

    anywhere = pl.BlockSpec(memory_space=pl.ANY)
    return pl.pallas_call(
        body,
        out_shape=outs,
        in_specs=[anywhere] * len(args),
        out_specs=pl.BlockSpec(memory_space=pltpu.VMEM),
        scratch_shapes=[pltpu.SemaphoreType.DMA((n_copies,))],
    )(*args)


def first_lanes(code_table, depth_proj, n_dp):
    t_rows, t_cols = code_table.shape[1], code_table.shape[2] // 4
    d_half, d_cols = depth_proj.shape[0] // 8, depth_proj.shape[1]

    def views(refs):
        if refs is None:
            return [0] * (3 * n_dp)
        table, depth, lanes = refs
        found = []
        for k in range(n_dp):
            found.append((table.at[0, :, at(own_lane(), t_cols)], lanes.at[k, 0:t_rows]))
            for half in range(2):
                found.append(
                    (
                        depth.at[at(2 * own_lane() + half, d_half)],
                        lanes.at[k, t_rows:t_rows + d_half, half * d_cols:(half + 1) * d_cols],
                    )
                )
        return found

    return copies(views, shaped((n_dp, t_rows + d_half, t_cols)), [code_table, depth_proj])


def second_lanes(code_table, out_proj, after):
    t_rows, t_cols = code_table.shape[1], code_table.shape[2] // 4
    rows, cols = out_proj.shape[0] // 2, out_proj.shape[1]

    def views(refs):
        if refs is None:
            return [0, 1]
        table, out, _, lanes = refs
        return [
            (table.at[1, :, at(own_lane(), t_cols)], lanes.at[0:t_rows]),
            (out.at[at(own_lane() // 2, rows)], lanes.at[t_rows:t_rows + rows]),
        ]

    return copies(views, shaped((t_rows + rows, cols)), [code_table, out_proj, after])


def first_parts(where, pieces, t_rows):
    n, d_half, t_cols = pieces.shape
    d_half, d_cols = d_half - t_rows, t_cols // 2
    top, fold = n * t_rows, 2 * d_half

    def body(where_ref, ref, both, depth, top_fold):
        for k in range(n):
            both[k * t_rows:(k + 1) * t_rows, :] = ref[where_ref[DP] ^ k, :t_rows]
            place = where_ref[DP] ^ k
            cols = at(place % 2, d_cols)
            for half in range(2):
                part = ref[place, t_rows:, half * d_cols:(half + 1) * d_cols]
                row = pl.multiple_of((place // 2) * fold + half * d_half, d_half)
                both[pl.ds(pl.multiple_of(top + row, d_half), d_half), cols] = part
                depth[pl.ds(row, d_half), cols] = part
        top_fold[...] = depth[:fold]

    rows = fold * n // 2
    return run(body, [shaped((top + rows, t_cols)), shaped((rows, t_cols)), shaped((fold, t_cols))], where, pieces)


def table_part(where, pieces, t_rows):
    n, cols = len(pieces), pieces[0].shape[1]

    def body(where_ref, *refs):
        for k in range(n):
            refs[n][k * t_rows:(k + 1) * t_rows, :] = refs[k][:t_rows]

    return run(body, [shaped((n * t_rows, cols))], where, *pieces)[0]


def out_part(where, pieces, t_rows):
    rows, cols = pieces[0].shape[0] - t_rows, pieces[0].shape[1]
    n = len(pieces)
    first = 160

    def body(where_ref, *refs):
        out, head, tail = refs[n:]
        for k in range(n):
            cut = at(where_ref[DP] ^ k, cols)
            out[:, cut] = refs[k][t_rows:]
            head[:, cut] = refs[k][t_rows:t_rows + first]
            tail[:, cut] = refs[k][t_rows + first:]

    outs = [shaped((rows, n * cols)), shaped((first, n * cols)), shaped((rows - first, n * cols))]
    return run(body, outs, where, *pieces)


def embed(where, packed, top, level, n_level, tokens, own, got, half, n_dp):
    folds = tokens // DH
    n_rows = id_rows(n_level, tokens)
    rows, cols = own.shape
    rows_dev, extra = half // n_dp, rows - half
    late = extra // 2

    def body(where_ref, mine_ref, core_ref, far_ref, own_ref, got_ref, *outs):
        def ids_of(ref, start):
            all_ids = ref[start:start + 2 * n_level * folds].astype(F32)
            mine = level * folds
            high = all_ids[mine:mine + folds]
            low = all_ids[(n_level * folds) + mine:(n_level * folds) + mine + folds]
            ids = high * 32.0 + low
            return jnp.concatenate([ids[f:f + 1] for f in range(folds)], axis=1)

        place = lax.broadcasted_iota(jnp.int32, (tokens, half), 1)
        owner = jnp.bitwise_xor(place // rows_dev, where_ref[DP])
        base = owner * rows_dev + place % rows_dev
        rows_of = [(mine_ref, top), (core_ref, top), (far_ref, top), (far_ref, top + n_rows)]
        columns = jnp.concatenate([ids_of(*r) for r in rows_of], axis=0).T.astype(jnp.int32)
        for m in (2, 3, 1, 0):
            col = columns[:, m:m + 1]
            total = None
            for k, ref in enumerate((own_ref, got_ref)):
                start = (where_ref[HEAD] ^ k) * half
                hot = (base == col - start).astype(F32).astype(BF16)
                part = jnp.dot(hot, ref[:half], preferred_element_type=F32)
                total = part if total is None else total + part
            total = total.astype(BF16)
            if m < 2:
                outs[m][:tokens] = total
            else:
                outs[2][(m - 2) * tokens:(m - 1) * tokens, :] = total
        if extra:
            outs[1][tokens:] = got_ref[half:]
            outs[2][2 * tokens:2 * tokens + extra] = got_ref[half:]
            outs[2][2 * tokens + extra:] = own_ref[rows - late:]

    outs = [shaped((tokens, cols)), shaped((tokens + extra, cols)), shaped((2 * tokens + extra + late, cols))]
    return run(body, outs, where, *packed, own, got)


def depth_grad(where, folds, first, second, mixed, mixed_got, cot):
    arrays, which = [], []
    for array, _ in folds + first + second:
        found = [i for i, other in enumerate(arrays) if other is array]
        if not found:
            arrays.append(array)
        which.append(found[0] if found else len(arrays) - 1)
    starts = [start for _, start in folds + first + second]
    tokens, width = mixed.shape
    cols = width // 4
    chunk = 32

    def body(where_ref, *refs):
        parts = refs[:len(arrays)]
        mixed_ref, got_ref, cot_ref, out, full, sum_ref, mid_ref, last_ref, row_ref = refs[len(arrays):]
        for n in range(16):
            m, x, j = n // 4, n // 2 % 2, n % 2
            place = (where_ref[HEAD] ^ x) * 2 + j
            full[at(where_ref[m], cols), at(place, cols)] = parts[which[n]][starts[n]:starts[n] + cols]

        def rows_of(i):
            return pl.ds(pl.multiple_of(i * chunk, chunk), chunk)

        def lane_rows(i, n):
            return parts[which[n]][pl.ds(pl.multiple_of(starts[n] + i * chunk, chunk), chunk), :].astype(F32)

        def inverse(total):
            return lax.rsqrt(jnp.mean(total * total, axis=-1, keepdims=True) + 1e-05)

        def enter(i, carry):
            rows = rows_of(i)
            for m in range(4):
                cut = at(where_ref[m], cols)
                sum_ref[rows, cut] = mixed_ref[rows, cut] + got_ref[rows, cut].astype(F32) + lane_rows(i, 16 + m)
            total = sum_ref[rows, :]
            row_ref[rows, :] = (total * inverse(total)).astype(BF16)
            return carry

        lax.fori_loop(0, tokens // chunk, enter, 0, unroll=True)
        mid_ref[...] = jnp.dot(row_ref[...], full[...], preferred_element_type=F32)
        last_ref[...] = dot(cot_ref[:, width:], full[...], ((1,), (1,)))

        def middle(i, carry):
            rows = rows_of(i)
            projected = mid_ref[rows, :]
            gate = jax.nn.sigmoid(projected)
            mid_ref[rows, :] = sum_ref[rows, :] + projected * gate
            for m in range(4):
                cut = at(where_ref[m], cols)
                mid_ref[rows, cut] += lane_rows(i, 20 + m)
            total = mid_ref[rows, :]
            inv = inverse(total)
            grad = last_ref[rows, :]
            along = jnp.mean(grad * total, axis=-1, keepdims=True)
            grad = grad * inv - total * (along * inv * inv * inv)
            last_ref[rows, :] = grad
            slope = gate * (1.0 + projected * (1.0 - gate))
            row_ref[rows, :] = (cot_ref[rows, :width].astype(F32) + grad * slope).astype(BF16)
            return carry

        lax.fori_loop(0, tokens // chunk, middle, 0, unroll=True)
        mid_ref[...] = dot(row_ref[...], full[...], ((1,), (1,)))

        def leave(i, carry):
            rows = rows_of(i)
            total = sum_ref[rows, :]
            inv = inverse(total)
            grad = mid_ref[rows, :]
            along = jnp.mean(grad * total, axis=-1, keepdims=True)
            grad = last_ref[rows, :] + grad * inv - total * (along * inv * inv * inv)
            out[rows, :] = grad.astype(BF16)
            return carry

        lax.fori_loop(0, tokens // chunk, leave, 0, unroll=True)

    vmem = pl.BlockSpec(memory_space=pltpu.VMEM)
    return pl.pallas_call(
        body,
        out_shape=shaped((tokens, width)),
        in_specs=[pl.BlockSpec(memory_space=pltpu.SMEM)] + [vmem] * (len(arrays) + 3),
        out_specs=vmem,
        scratch_shapes=[
            pltpu.VMEM((width, width), BF16),
            pltpu.VMEM((tokens, width), F32),
            pltpu.VMEM((tokens, width), F32),
            pltpu.VMEM((tokens, width), F32),
            pltpu.VMEM((tokens, width), BF16),
        ],
        compiler_params=pltpu.CompilerParams(vmem_limit_bytes=VMEM_BYTES),
    )(where, *arrays, mixed, mixed_got, cot)


def id_rows(n_level, tokens):
    return -(-2 * n_level * (tokens // DH) // 16) * 16


def pack(where, keys, values, ids):
    heads = keys.shape[1] // DH
    n_level, tokens = ids.shape
    folds = tokens // DH
    top = heads * DH

    def body(where_ref, k_ref, v_ref, ids_ref, out):
        parts = []
        for level in range(n_level):
            for fold in range(folds):
                parts.append(ids_ref[level:level + 1, fold * DH:(fold + 1) * DH])
        whole = jnp.concatenate(parts, axis=0)
        both = jnp.concatenate([whole // 32, whole % 32], axis=0).astype(F32).astype(BF16)
        out[top:top + 2 * n_level * folds] = both
        for i in range(heads):
            cut = slice(i * DH, (i + 1) * DH)
            out[cut] = dot(k_ref[:, cut], v_ref[:, cut], ((0,), (0,))).astype(BF16)

    return run(body, [shaped((top + id_rows(n_level, tokens), DH))], where, keys, values, ids)[0]


def pack_chip(where, own, core, top):
    rows = own.shape[0] - top

    def body(where_ref, own_ref, core_ref, out):
        out[:top] = (own_ref[:top].astype(F32) + core_ref[:top].astype(F32)).astype(BF16)
        out[top:top + rows] = own_ref[top:]
        out[top + rows:] = core_ref[top:]

    return run(body, [shaped((top + 2 * rows, DH))], where, own, core)[0]


def lower(size):
    rows = lax.broadcasted_iota(jnp.int32, (size, size), 0)
    cols = lax.broadcasted_iota(jnp.int32, (size, size), 1)
    return rows >= cols


def upper(size):
    rows = lax.broadcasted_iota(jnp.int32, (size, size), 0)
    cols = lax.broadcasted_iota(jnp.int32, (size, size), 1)
    return rows <= cols


def attend(where, queries, keys, values, from_core, from_far, att_scale):
    length, width_dev = queries.shape
    heads = width_dev // DH

    def body(where_ref, q_ref, k_ref, v_ref, core_ref, far_ref, att, state):
        near = (where_ref[0] // 2).astype(F32)
        far = (where_ref[0] % 2).astype(F32)
        keep = lower(length)
        for i in range(heads):
            cut = slice(i * DH, (i + 1) * DH)
            state[i] = (core_ref[cut].astype(F32) * near + far_ref[cut].astype(F32) * far).astype(BF16)
            q = q_ref[:, cut]
            scores = jnp.where(keep, dot(q, k_ref[:, cut], ((1,), (1,))), 0.0).astype(BF16)
            both = jnp.dot(scores, v_ref[:, cut], preferred_element_type=F32)
            both += jnp.dot(q, state[i], preferred_element_type=F32)
            att[:, cut] = (att_scale * both).astype(BF16)

    return run(
        body, [shaped((length, width_dev)), shaped((heads, DH, DH))], where, queries, keys, values, from_core, from_far
    )


def mix_own(where, attended, own_rows):
    length = attended.shape[0] // 2
    half, width = own_rows.shape

    def body(where_ref, att, own, out):
        core = where_ref[0] // 2
        for k in range(2):
            rows = at(where_ref[HEAD] ^ (1 - k), length)
            out[k] = jnp.dot(att[rows, at(core, half)], own[...], preferred_element_type=F32)

    return run(body, [shaped((2, length, width), F32)], where, attended, own_rows)[0]


def mix(where, attended, part, got_head, got_tail, other):
    length = attended.shape[0] // 2
    width = part.shape[2]
    half = got_head.shape[0] + got_tail.shape[0]
    dtype = BF16 if other else F32

    def body(where_ref, att, part_ref, head, tail, out):
        rows = at(where_ref[HEAD] ^ (1 if other else 0), length)
        core = where_ref[0] // 2
        got = jnp.concatenate([head[...], tail[...]], axis=0)
        total = part_ref[0 if other else 1]
        total += jnp.dot(att[rows, at(1 - core, half)], got, preferred_element_type=F32)
        out[...] = total.astype(dtype)

    return run(body, [shaped((length, width), dtype)], where, attended, part, got_head, got_tail)[0]


def weight_terms(where, attended, grad_own, grad_got):
    tokens, width = grad_own.shape

    def body(where_ref, att, own, got, send, keep):
        def term(m):
            total = None
            for k, ref in enumerate((own, got)):
                a = att[at(where_ref[HEAD] ^ k, tokens), at(where_ref[m], DH)]
                part = dot(a, ref[...], ((0,), (0,)))
                total = part if total is None else total + part
            return total

        send[0] = term(2).astype(BF16)
        send[1] = term(3).astype(BF16)
        keep[0] = term(0)
        keep[1] = term(1)

    return run(
        body, [shaped((2, DH, width)), shaped((2, DH, width), F32)], where, attended, grad_own, grad_got
    )


def add_core(where, keep, got):
    shape = keep.shape[1:]

    def body(where_ref, keep_ref, got_ref, send, rest):
        rest[...] = keep_ref[0] + got_ref[0].astype(F32)
        send[...] = (keep_ref[1] + got_ref[1].astype(F32)).astype(BF16)

    return run(body, [shaped(shape), shaped(shape, F32)], where, keep, got)


def add_far(where, keep, got, n_dp):
    rows, width = keep.shape
    cols = width // n_dp

    def body(where_ref, keep_ref, got_ref, rest, *send):
        for k in range(n_dp):
            cut = at(where_ref[DP] ^ k, cols)
            total = keep_ref[:, cut] + got_ref[:, cut].astype(F32)
            if k:
                send[k - 1][...] = total.astype(BF16)
            else:
                rest[...] = total

    return run(body, [shaped((rows, cols), F32)] + [shaped((rows, cols))] * (n_dp - 1), where, keep, got)


def add_all(where, keep, got):
    def body(where_ref, keep_ref, *refs):
        total = keep_ref[...]
        for ref in refs[:-1]:
            total = total + ref[...].astype(F32)
        refs[-1][...] = total.astype(BF16)

    return run(body, [shaped(keep.shape)], where, keep, *got)[0]


def rows_together(where, pieces):
    rows, cols = pieces[0].shape

    def body(where_ref, *refs):
        for m, ref in enumerate(refs[:-1]):
            refs[-1][at(where_ref[m], rows), :] = ref[...].astype(F32)

    return run(body, [shaped((rows * 4, cols), F32)], where, *pieces)[0]


def grad_attend(where, grad_own, grad_got, own_rows, got_head, got_tail, queries):
    tokens, width = grad_own.shape
    length, width_dev = queries.shape
    half = width_dev // 2

    def body(where_ref, own, got, o_own, head, tail, q_ref, rows, back):
        for c in range(2):
            block = o_own[...] if c == 0 else jnp.concatenate([head[...], tail[...]], axis=0)
            for k, ref in enumerate((own, got)):
                part = dot(ref[...], block, ((1,), (1,))).astype(BF16)
                rows[at(where_ref[HEAD] ^ k, tokens), at((where_ref[0] // 2) ^ c, half)] = part
        for i in range(width_dev // DH):
            cut = slice(i * DH, (i + 1) * DH)
            back[i] = dot(q_ref[:, cut], rows[:, cut], ((0,), (0,))).astype(BF16)

    outs = [shaped((length, width_dev)), shaped((width_dev // DH, DH, DH))]
    return run(body, outs, where, grad_own, grad_got, own_rows, got_head, got_tail, queries)


def query_grads(where, grad_rows, keys, values, state, att_scale):
    length, width_dev = keys.shape

    def body(where_ref, g_ref, k_ref, v_ref, s_ref, out):
        keep = lower(length)
        for i in range(width_dev // DH):
            cut = slice(i * DH, (i + 1) * DH)
            g = g_ref[:, cut]
            scores = jnp.where(keep, dot(g, v_ref[:, cut], ((1,), (1,))), 0.0).astype(BF16)
            both = jnp.dot(scores, k_ref[:, cut], preferred_element_type=F32)
            both += dot(g, s_ref[i], ((1,), (1,)))
            out[:, cut] = (att_scale * both).astype(BF16)

    return run(body, [shaped((length, width_dev))], where, grad_rows, keys, values, state)[0]


def key_value_grads(where, grad_rows, queries, keys, values, from_core, from_far, att_scale):
    length, width_dev = keys.shape

    def body(where_ref, g_ref, q_ref, k_ref, v_ref, core_ref, far_ref, dk, dv):
        near = 1.0 - (where_ref[0] // 2).astype(F32)
        far = 1.0 - (where_ref[0] % 2).astype(F32)
        keep = upper(length)
        for i in range(width_dev // DH):
            cut = slice(i * DH, (i + 1) * DH)
            g, q, k, v = g_ref[:, cut], q_ref[:, cut], k_ref[:, cut], v_ref[:, cut]
            back = (core_ref[i].astype(F32) * near + far_ref[i].astype(F32) * far).astype(BF16)
            grad_scores = jnp.where(keep, dot(v, g, ((1,), (1,))), 0.0).astype(BF16)
            both = jnp.dot(grad_scores, q, preferred_element_type=F32)
            both += dot(v, back, ((1,), (1,)))
            dk[:, cut] = (att_scale * both).astype(BF16)
            scores = jnp.where(keep, dot(k, q, ((1,), (1,))), 0.0).astype(BF16)
            both = jnp.dot(scores, g, preferred_element_type=F32)
            both += jnp.dot(k, back, preferred_element_type=F32)
            dv[:, cut] = (att_scale * both).astype(BF16)

    outs = [shaped((length, width_dev))] * 2
    return run(body, outs, where, grad_rows, queries, keys, values, from_core, from_far)


def fits(queries, out_proj, depth_proj, code_table, code_ids):
    n_seq, n_head = lax.axis_size("seq"), lax.axis_size("head")
    return (
        n_seq == 4
        and n_head == 2
        and queries.shape[2] == 4 * DH
        and code_table.shape[0] == 2
        and out_proj.shape[1] % 128 == 0
        and depth_proj.shape[1] % 128 == 0
        and code_table.shape[1] % 128 == 0
        and code_ids.shape[1] % DH == 0
        and code_table.shape[1] * n_head * lax.axis_size("dp") <= 32 * 256
    )


def on_device(queries, keys, values, out_proj, depth_proj, code_table, code_ids, depth_cotangent):
    if not fits(queries, out_proj, depth_proj, code_table, code_ids):
        return on_device_any(
            queries, keys, values, out_proj, depth_proj, code_table, code_ids, depth_cotangent
        )
    n_dp = lax.axis_size("dp")
    me_seq, me_head, me_dp = (lax.axis_index(a) for a in ("seq", "head", "dp"))
    group_len = queries.shape[1]
    width = code_table.shape[2]
    att_scale = float(group_len * lax.axis_size("seq")) ** (-0.5)
    core, far = me_seq % 2, me_seq // 2
    lane = 2 * core + far
    where = jnp.stack([lane, lane ^ 1, lane ^ 2, lane ^ 3, me_head, me_dp, me_seq]).astype(jnp.int32)
    queries, keys, values = queries[0], keys[0], values[0]

    def far_swap(block):
        return swap(block, "seq", 2)

    def core_swap(block):
        return swap(block, "seq", 1)

    def all_lanes(block):
        got = far_swap(block)
        return [block, got, core_swap(block), core_swap(got)]

    t_rows, tokens = code_table.shape[1], code_ids.shape[1]
    half = t_rows * n_dp
    lanes_0 = first_lanes(code_table, depth_proj, n_dp)
    pieces_0 = lax.all_to_all(lanes_0, "dp", 0, 0)
    lanes_1 = second_lanes(code_table, out_proj, lanes_0)
    pieces_1 = exchange(lanes_1, "dp")

    top = keys.shape[1]
    keys, values, _ = lax.optimization_barrier((keys, values, lanes_1))
    mine = pack(where, keys, values, code_ids[0].T)
    from_core = core_swap(mine)
    chip = pack_chip(where, mine, from_core, top)
    from_far = far_swap(chip)
    packed = (mine, from_core, from_far)

    attended, state_in = attend(where, queries, keys, values, from_core, from_far, att_scale)

    pieces_0, _ = lax.optimization_barrier((pieces_0, attended))
    part_0, depth_part, depth_top = first_parts(where, pieces_0, t_rows)
    got_0 = swap(part_0, "head", 1)
    depth_far = far_swap(depth_top)

    pieces_1, depth_far = lax.optimization_barrier((pieces_1, depth_far))
    out_rows, out_head, out_tail = out_part(where, pieces_1, t_rows)
    got_head, got_tail = core_swap(out_head), core_swap(out_tail)
    part_1 = table_part(where, pieces_1, t_rows)
    got_1 = swap(part_1, "head", 1)

    mixed_part = mix_own(where, attended, out_rows)
    got_0, got_head, _, _ = lax.optimization_barrier((got_0, got_head, part_1, mixed_part))
    own_0, to_core, to_far = embed(where, packed, top, 0, 2, tokens, part_0, got_0, half, n_dp)
    far_0 = far_swap(to_far)

    got_tail, _ = lax.optimization_barrier((got_tail, to_far))
    mixed_send = mix(where, attended, mixed_part, got_head, got_tail, True)
    mixed_got = swap(mixed_send, "head", 1)
    mixed = mix(where, attended, mixed_part, got_head, got_tail, False)
    core_0 = core_swap(to_core)

    got_1, _, _ = lax.optimization_barrier((got_1, mixed, mixed_send))
    own_1, to_core, to_far = embed(where, packed, top, 1, 2, tokens, part_1, got_1, half, n_dp)
    far_1 = far_swap(to_far)
    depth_core, depth_core_far = core_swap(depth_part), core_swap(depth_far)
    far_0, far_1, mixed_got, depth_core, depth_core_far, core_0 = lax.optimization_barrier(
        (far_0, far_1, mixed_got, depth_core, depth_core_far, core_0)
    )
    core_far_0, core_1, core_far_1 = core_swap(far_0), core_swap(to_core), core_swap(far_1)

    fold, end = depth_top.shape[0], 2 * tokens
    folds = [(depth_part, 0), (depth_part, fold), (got_0, half), (got_0, half + fold)]
    folds += [(depth_far, 0), (far_0, end + 2 * fold), (far_0, end), (far_0, end + fold)]
    folds += [(depth_core, 0), (depth_core, fold), (core_0, tokens), (core_0, tokens + fold)]
    folds += [(depth_core_far, 0), (core_far_0, end + 2 * fold), (core_far_0, end), (core_far_0, end + fold)]
    first = [(own_0, 0), (far_0, 0), (core_0, 0), (core_far_0, tokens)]
    second = [(own_1, 0), (far_1, 0), (core_1, 0), (core_far_1, tokens)]
    cot = depth_cotangent[0].reshape(tokens, -1)
    grad_mixed = depth_grad(where, folds, first, second, mixed, mixed_got, cot)

    grad_got = swap(grad_mixed, "head", 1)
    send, keep = weight_terms(where, attended, grad_mixed, grad_got)
    send, keep = add_core(where, keep, core_swap(send))
    from_far = far_swap(send)
    grad_rows, back = grad_attend(where, grad_mixed, grad_got, out_rows, got_head, got_tail, queries)
    back_core = core_swap(back)
    grad_query = query_grads(where, grad_rows, keys, values, state_in, att_scale)
    back_chip = (back.astype(F32) + back_core.astype(F32)).astype(BF16)
    back_far = far_swap(back_chip)
    from_far, grad_query, _ = lax.optimization_barrier((from_far, grad_query, back_chip))
    keep, *send = add_far(where, keep, from_far, n_dp)
    got = [swap(s, "dp", k + 1) for k, s in enumerate(send)]
    grad_key, grad_value = key_value_grads(
        where, grad_rows, queries, keys, values, back_core, back_far, att_scale
    )
    got, grad_key, grad_value = lax.optimization_barrier((got, grad_key, grad_value))
    block = add_all(where, keep, got)
    grad_out_proj = rows_together(where, all_lanes(block))
    return grad_query[None], grad_key[None], grad_value[None], grad_out_proj


def solution(mesh):
    in_specs = (
        P("dp", "seq", "head"),
        P("dp", "seq", "head"),
        P("dp", "seq", "head"),
        P("head", "dp"),
        P(None, ("head", "dp")),
        P(None, ("head", "dp"), None),
        P("dp", ("seq", "head"), None),
        P("dp", ("seq", "head"), None, None),
    )
    out_specs = (
        P("dp", "seq", "head"),
        P("dp", "seq", "head"),
        P("dp", "seq", "head"),
        P("head", "dp"),
    )
    return jax.shard_map(
        on_device, mesh=mesh, in_specs=in_specs, out_specs=out_specs, check_vma=False
    )
```

```python
import jax
import jax.numpy as jnp
from jax import lax
from jax.experimental import pallas as pl
from jax.experimental.pallas import tpu as pltpu
from jax.sharding import PartitionSpec as P

DH = 128
F32 = jnp.float32
BF16 = jnp.bfloat16


def swap(block, axis, mask):
    return lax.ppermute(block, axis, [(i, i ^ mask) for i in range(lax.axis_size(axis))])


def has_bit(index, bit):
    return lax.bitwise_and(index, jnp.int32(bit)) != 0


def in_order(pieces, index):
    pieces = list(pieces)
    bit = 1
    while bit < len(pieces):
        odd = has_bit(index, bit)
        pieces = [jnp.where(odd, pieces[j ^ bit], pieces[j]) for j in range(len(pieces))]
        bit *= 2
    return pieces


def pick(array, index, dim):
    return lax.dynamic_index_in_dim(array, index, dim, keepdims=False)


def exchange(block, axis):
    return [block] + [swap(block, axis, k) for k in range(1, lax.axis_size(axis))]


def dot(a, b, dims):
    return lax.dot_general(a, b, ((dims[0], dims[1]), ((), ())), preferred_element_type=F32)


def earlier_sum(state, backward):
    n_seq = lax.axis_size("seq")
    me = lax.axis_index("seq")
    before = jnp.zeros_like(state)
    total = state
    bit = 1
    while bit < n_seq:
        got = swap(total.astype(BF16), "seq", bit).astype(F32)
        mine = has_bit(me, bit)
        takes = jnp.logical_not(mine) if backward else mine
        before = before + jnp.where(takes, got, 0.0)
        total = total + got
        bit *= 2
    return before.astype(BF16)


def on_device_any(queries, keys, values, out_proj, depth_proj, code_table, code_ids, depth_cotangent):
    n_seq, n_head, n_dp = (lax.axis_size(a) for a in ("seq", "head", "dp"))
    me_seq, me_head, me_dp = (lax.axis_index(a) for a in ("seq", "head", "dp"))
    group_len, width_dev = queries.shape[1:]
    heads_here = width_dev // DH
    tokens = group_len // n_head
    n_far = n_seq // 2
    me_core = lax.bitwise_and(me_seq, jnp.int32(1))
    me_far = lax.shift_right_logical(me_seq, jnp.int32(1))
    lane = me_core * n_far + me_far
    att_scale = float(group_len * n_seq) ** (-0.5)
    width = code_table.shape[2]
    wide = width // n_seq
    far = [2 * m for m in range(n_far)]

    def far_exchange(block):
        return [block] + [swap(block, "seq", m) for m in far[1:]]

    def seq_lanes(block):
        near = jnp.stack(in_order(far_exchange(block), me_far))
        both = in_order([near, swap(near, "seq", 1)], me_core)
        return jnp.concatenate(both, axis=0)

    ids = code_ids[0].T
    ids_far = jnp.stack(far_exchange(ids))
    ids_rel = jnp.stack([ids_far, swap(ids_far, "seq", 1)])

    table = lax.dynamic_slice_in_dim(code_table, lane * wide, wide, axis=2)
    rows_dev = table.shape[1]
    embedded = []
    row_no = []
    for k_head in range(n_head):
        for k_dp in range(n_dp):
            owner = (me_head ^ k_head) * n_dp + (me_dp ^ k_dp)
            row_no.append(owner * rows_dev + jnp.arange(rows_dev, dtype=jnp.int32))
    row_no = jnp.concatenate(row_no)
    for level in range(table.shape[0]):
        part = jnp.concatenate(exchange(table[level], "dp"), axis=0)
        part = jnp.concatenate(exchange(part, "head"), axis=0)
        level_ids = ids_rel[:, :, level].reshape(-1)
        onehot = (level_ids[:, None] == row_no[None, :]).astype(BF16)
        rel = dot(onehot, part, ((1,), (0,))).astype(BF16).reshape(2, n_far, tokens, wide)
        mine = [rel[:, 0]] + [swap(rel[:, m // 2], "seq", m) for m in far[1:]]
        near = jnp.stack([block[0] for block in mine])
        other = swap(jnp.stack([block[1] for block in mine]), "seq", 1)
        near = jnp.stack(in_order(list(near), me_far))
        other = jnp.stack(in_order(list(other), me_far))
        lanes = jnp.concatenate(in_order([near, other], me_core), axis=0)
        embedded.append(lanes.transpose(1, 0, 2).reshape(tokens, width))

    out_rows = out_proj.shape[0] // n_seq
    out_lane = lax.dynamic_slice_in_dim(out_proj, lane * out_rows, out_rows, axis=0)
    out_part = jnp.concatenate(in_order(exchange(out_lane, "dp"), me_dp), axis=1)
    out_part = jnp.stack(in_order(exchange(out_part, "head"), me_head))
    out_full = seq_lanes(out_part).transpose(1, 0, 2, 3).reshape(n_head * width_dev, width)

    depth_rows = depth_proj.shape[0] // n_seq
    depth_lane = lax.dynamic_slice_in_dim(depth_proj, lane * depth_rows, depth_rows, axis=0)
    depth_part = jnp.concatenate(in_order(exchange(depth_lane, "dp"), me_dp), axis=1)
    depth_part = jnp.concatenate(in_order(exchange(depth_part, "head"), me_head), axis=1)
    proj_mat = seq_lanes(depth_part).reshape(width, width)

    query_rows = queries[0].reshape(group_len, heads_here, DH)
    key_rows = keys[0].reshape(group_len, heads_here, DH)
    value_rows = values[0].reshape(group_len, heads_here, DH)
    places = jnp.arange(group_len, dtype=jnp.int32)
    causal = (places[:, None] >= places[None, :]).astype(F32)
    state_local = jnp.einsum("thd,the->hde", key_rows, value_rows, preferred_element_type=F32)
    state_in = earlier_sum(state_local, False)
    scores = (
        jnp.einsum("thd,shd->hts", query_rows, key_rows, preferred_element_type=F32) * causal
    ).astype(BF16)
    attended = (
        att_scale
        * (
            jnp.einsum("hts,she->the", scores, value_rows, preferred_element_type=F32)
            + jnp.einsum("thd,hde->the", query_rows, state_in, preferred_element_type=F32)
        )
    ).astype(BF16)
    attended = attended.reshape(n_head, tokens, width_dev)
    att_all = [pick(attended, me_head, 0)]
    att_all += [swap(pick(attended, me_head ^ k, 0), "head", k) for k in range(1, n_head)]
    att_all = jnp.concatenate(in_order(att_all, me_head), axis=1)
    mixed = dot(att_all, out_full, ((1,), (0,)))

    cot = depth_cotangent[0]
    n_level = cot.shape[1]
    carried = mixed
    kept = []
    for level in range(n_level):
        summed = carried + embedded[level].astype(F32)
        inv = lax.rsqrt(jnp.mean(summed * summed, axis=-1, keepdims=True) + 1e-05)
        if level < n_level - 1:
            projected = dot((summed * inv).astype(BF16), proj_mat, ((1,), (0,)))
            carried = summed + projected * jax.nn.sigmoid(projected)
        else:
            projected = None
        kept.append((summed, inv, projected))
    grad = None
    for level in reversed(range(n_level)):
        summed, inv, projected = kept[level]
        grad_proj = cot[:, level, :]
        if grad is not None:
            gate = jax.nn.sigmoid(projected)
            slope = gate * (1.0 + projected * (1.0 - gate))
            grad_proj = (grad_proj.astype(F32) + grad * slope).astype(BF16)
        grad_normed = dot(grad_proj, proj_mat, ((1,), (1,)))
        along = jnp.mean(grad_normed * summed, axis=-1, keepdims=True)
        grad_sum = grad_normed * inv - summed * (along * inv * inv * inv)
        grad = grad_sum if grad is None else grad + grad_sum
    grad_mixed = grad.astype(BF16)

    out_heads = out_full.reshape(n_head, width_dev, width)
    grad_rows = []
    for k in range(1, n_head):
        part = dot(grad_mixed, pick(out_heads, me_head ^ k, 0), ((1,), (1,))).astype(BF16)
        grad_rows.append(swap(part, "head", k))
    own_part = dot(grad_mixed, pick(out_heads, me_head, 0), ((1,), (1,))).astype(BF16)
    grad_rows = jnp.concatenate(in_order([own_part] + grad_rows, me_head), axis=0)
    grad_rows = grad_rows.reshape(group_len, heads_here, DH)

    rows = width_dev // n_seq
    att_lanes = att_all.reshape(tokens, n_head, 2, n_far, rows)

    def term(core):
        part = pick(att_lanes, core, 2).reshape(tokens, n_head * n_far * rows)
        return dot(part, grad_mixed, ((0,), (0,)))

    got = swap(term(1 - me_core).astype(BF16), "seq", 1)
    chip = term(me_core) + got.astype(F32)
    chip = chip.reshape(n_head, n_far, rows, width)
    total = pick(pick(chip, me_head, 0), me_far, 0)
    for m in far:
        for k in range(n_head):
            if m or k:
                piece = pick(pick(chip, me_head ^ k, 0), me_far ^ (m // 2), 0).astype(BF16)
                mask = m * n_head + k
                total = total + swap(piece, ("seq", "head"), mask).astype(F32)
    columns = total.reshape(rows, n_dp, width // n_dp)
    block = pick(columns, me_dp, 1)
    for k in range(1, n_dp):
        block = block + swap(pick(columns, me_dp ^ k, 1).astype(BF16), "dp", k).astype(F32)
    grad_out_proj = seq_lanes(block.astype(BF16)).reshape(width_dev, width // n_dp).astype(F32)

    back_local = jnp.einsum("thd,the->hde", query_rows, grad_rows, preferred_element_type=F32)
    back_state = earlier_sum(back_local, True)
    grad_scores = (
        jnp.einsum("the,she->hts", grad_rows, value_rows, preferred_element_type=F32) * causal
    ).astype(BF16)
    grad_query = att_scale * (
        jnp.einsum("hts,shd->thd", grad_scores, key_rows, preferred_element_type=F32)
        + jnp.einsum("the,hde->thd", grad_rows, state_in, preferred_element_type=F32)
    )
    grad_key = att_scale * (
        jnp.einsum("hts,thd->shd", grad_scores, query_rows, preferred_element_type=F32)
        + jnp.einsum("she,hde->shd", value_rows, back_state, preferred_element_type=F32)
    )
    grad_value = att_scale * (
        jnp.einsum("hts,the->she", scores, grad_rows, preferred_element_type=F32)
        + jnp.einsum("shd,hde->she", key_rows, back_state, preferred_element_type=F32)
    )
    out_shape = (1, group_len, width_dev)
    return (
        grad_query.reshape(out_shape).astype(BF16),
        grad_key.reshape(out_shape).astype(BF16),
        grad_value.reshape(out_shape).astype(BF16),
        grad_out_proj,
    )


VMEM_BYTES = 48 * 1024 * 1024


def run(body, outs, where, *args):
    vmem = pl.BlockSpec(memory_space=pltpu.VMEM)
    return pl.pallas_call(
        body,
        out_shape=outs,
        in_specs=[pl.BlockSpec(memory_space=pltpu.SMEM)] + [vmem] * len(args),
        out_specs=[vmem] * len(outs),
        compiler_params=pltpu.CompilerParams(vmem_limit_bytes=VMEM_BYTES),
    )(where, *args)


def shaped(shape, dtype=BF16):
    return jax.ShapeDtypeStruct(shape, dtype)


def at(index, size):
    return pl.ds(pl.multiple_of(index * size, size), size)


HEAD, DP, SEQ = 4, 5, 6


def own_lane():
    me = lax.axis_index("seq")
    return 2 * (me % 2) + me // 2


def copies(body_of, outs, args):
    n_copies = len(body_of(None))

    def body(*refs):
        sems = refs[-1]
        going = [pltpu.make_async_copy(src, dst, sems.at[i]) for i, (src, dst) in enumerate(body_of(refs[:-1]))]
        for copy in going:
            copy.start()
        for copy in going:
            copy.wait()

    anywhere = pl.BlockSpec(memory_space=pl.ANY)
    return pl.pallas_call(
        body,
        out_shape=outs,
        in_specs=[anywhere] * len(args),
        out_specs=pl.BlockSpec(memory_space=pltpu.VMEM),
        scratch_shapes=[pltpu.SemaphoreType.DMA((n_copies,))],
    )(*args)


def first_lanes(code_table, depth_proj, n_dp):
    t_rows, t_cols = code_table.shape[1], code_table.shape[2] // 4
    d_half, d_cols = depth_proj.shape[0] // 8, depth_proj.shape[1]

    def views(refs):
        if refs is None:
            return [0] * (3 * n_dp)
        table, depth, lanes = refs
        found = []
        for k in range(n_dp):
            found.append((table.at[0, :, at(own_lane(), t_cols)], lanes.at[k, 0:t_rows]))
            for half in range(2):
                found.append(
                    (
                        depth.at[at(2 * own_lane() + half, d_half)],
                        lanes.at[k, t_rows:t_rows + d_half, half * d_cols:(half + 1) * d_cols],
                    )
                )
        return found

    return copies(views, shaped((n_dp, t_rows + d_half, t_cols)), [code_table, depth_proj])


def second_lanes(code_table, out_proj, after):
    t_rows, t_cols = code_table.shape[1], code_table.shape[2] // 4
    rows, cols = out_proj.shape[0] // 2, out_proj.shape[1]

    def views(refs):
        if refs is None:
            return [0, 1]
        table, out, _, lanes = refs
        return [
            (table.at[1, :, at(own_lane(), t_cols)], lanes.at[0:t_rows]),
            (out.at[at(own_lane() // 2, rows)], lanes.at[t_rows:t_rows + rows]),
        ]

    return copies(views, shaped((t_rows + rows, cols)), [code_table, out_proj, after])


def first_parts(where, pieces, t_rows, early):
    n, d_half, t_cols = pieces.shape
    d_half, d_cols = d_half - t_rows, t_cols // 2
    top, fold = n * t_rows, 2 * d_half

    def body(where_ref, ref, both, depth, top_fold):
        for k in range(n):
            both[k * t_rows:(k + 1) * t_rows, :] = ref[where_ref[DP] ^ k, :t_rows]
            place = where_ref[DP] ^ k
            cols = at(place % 2, d_cols)
            for half in range(2):
                part = ref[place, t_rows:, half * d_cols:(half + 1) * d_cols]
                row = pl.multiple_of((place // 2) * fold + half * d_half, d_half)
                both[pl.ds(pl.multiple_of(top + row, d_half), d_half), cols] = part
                depth[pl.ds(row, d_half), cols] = part
        top_fold[...] = depth[:early]

    rows = fold * n // 2
    return run(body, [shaped((top + rows, t_cols)), shaped((rows, t_cols)), shaped((early, t_cols))], where, pieces)


def second_parts(where, pieces, distances, t_rows):
    rows, cols = pieces[0].shape[0] - t_rows, pieces[0].shape[1]
    n = len(pieces)
    first = rows * 5 // 8

    def body(where_ref, *refs):
        table, head, tail = refs[n:]
        for k, ref in zip(distances, refs):
            cut = at(where_ref[DP] ^ k, cols)
            table[k * t_rows:(k + 1) * t_rows, :] = ref[:t_rows]
            head[:, cut] = ref[t_rows:t_rows + first]
            tail[:, cut] = ref[t_rows + first:]

    outs = [shaped((n * t_rows, cols)), shaped((first, n * cols)), shaped((rows - first, n * cols))]
    return run(body, outs, where, *pieces)


def embed(where, packed, top, level, n_level, tokens, own, got, half, n_dp, late):
    folds = tokens // DH
    n_rows = id_rows(n_level, tokens)
    rows, cols = own.shape
    rows_dev, extra = half // n_dp, rows - half

    def body(where_ref, mine_ref, core_ref, far_ref, own_ref, got_ref, *outs):
        def ids_of(ref, start):
            all_ids = ref[start:start + 2 * n_level * folds].astype(F32)
            mine = level * folds
            high = all_ids[mine:mine + folds]
            low = all_ids[(n_level * folds) + mine:(n_level * folds) + mine + folds]
            ids = high * 32.0 + low
            return jnp.concatenate([ids[f:f + 1] for f in range(folds)], axis=1)

        place = lax.broadcasted_iota(jnp.int32, (tokens, half), 1)
        owner = jnp.bitwise_xor(place // rows_dev, where_ref[DP])
        base = owner * rows_dev + place % rows_dev
        rows_of = [(mine_ref, top), (core_ref, top), (far_ref, top), (far_ref, top + n_rows)]
        columns = jnp.concatenate([ids_of(*r) for r in rows_of], axis=0).T.astype(jnp.int32)
        for m in (2, 3, 1, 0):
            col = columns[:, m:m + 1]
            total = None
            for k, ref in enumerate((own_ref, got_ref)):
                start = (where_ref[HEAD] ^ k) * half
                hot = (base == col - start).astype(F32).astype(BF16)
                part = jnp.dot(hot, ref[:half], preferred_element_type=F32)
                total = part if total is None else total + part
            total = total.astype(BF16)
            if m < 2:
                outs[m][:tokens] = total
            else:
                outs[2][(m - 2) * tokens:(m - 1) * tokens, :] = total
        if extra:
            outs[1][tokens:] = got_ref[half:]
            outs[2][2 * tokens:2 * tokens + extra] = got_ref[half:]
            outs[2][2 * tokens + extra:] = own_ref[rows - late:]

    outs = [shaped((tokens, cols)), shaped((tokens + extra, cols)), shaped((2 * tokens + extra + late, cols))]
    return run(body, outs, where, *packed, own, got)


def depth_grad(where, folds, rest, late, first, second, mixed, mixed_got, cot):
    arrays, which = [], []
    for array, _ in folds + first + second:
        found = [i for i, other in enumerate(arrays) if other is array]
        if not found:
            arrays.append(array)
        which.append(found[0] if found else len(arrays) - 1)
    starts = [start for _, start in folds + first + second]
    tokens, width = mixed.shape
    cols = width // 4
    chunk = 32

    def body(where_ref, *refs):
        parts = refs[:len(arrays)]
        mixed_ref, got_ref, cot_ref, out, full, sum_ref, mid_ref, last_ref, row_ref = refs[len(arrays):]
        for n in range(16):
            m, x, j = n // 4, n // 2 % 2, n % 2
            place = (where_ref[HEAD] ^ x) * 2 + j
            if rest[n] is None:
                full[at(where_ref[m], cols), at(place, cols)] = parts[which[n]][starts[n]:starts[n] + cols]
            else:
                main = pl.ds(pl.multiple_of(where_ref[m] * cols, cols), cols - late)
                tail = pl.ds(pl.multiple_of(where_ref[m] * cols + cols - late, 16), late)
                array = next(i for i, other in enumerate(arrays) if other is rest[n][0])
                full[main, at(place, cols)] = parts[which[n]][starts[n]:starts[n] + cols - late]
                full[tail, at(place, cols)] = parts[array][rest[n][1]:rest[n][1] + late]

        def rows_of(i):
            return pl.ds(pl.multiple_of(i * chunk, chunk), chunk)

        def lane_rows(i, n):
            return parts[which[n]][pl.ds(pl.multiple_of(starts[n] + i * chunk, chunk), chunk), :].astype(F32)

        def inverse(total):
            return lax.rsqrt(jnp.mean(total * total, axis=-1, keepdims=True) + 1e-05)

        def enter(i, carry):
            rows = rows_of(i)
            for m in range(4):
                cut = at(where_ref[m], cols)
                sum_ref[rows, cut] = mixed_ref[rows, cut] + got_ref[rows, cut].astype(F32) + lane_rows(i, 16 + m)
            total = sum_ref[rows, :]
            row_ref[rows, :] = (total * inverse(total)).astype(BF16)
            return carry

        lax.fori_loop(0, tokens // chunk, enter, 0, unroll=True)
        mid_ref[...] = jnp.dot(row_ref[...], full[...], preferred_element_type=F32)
        last_ref[...] = dot(cot_ref[:, width:], full[...], ((1,), (1,)))

        def middle(i, carry):
            rows = rows_of(i)
            projected = mid_ref[rows, :]
            gate = jax.nn.sigmoid(projected)
            mid_ref[rows, :] = sum_ref[rows, :] + projected * gate
            for m in range(4):
                cut = at(where_ref[m], cols)
                mid_ref[rows, cut] += lane_rows(i, 20 + m)
            total = mid_ref[rows, :]
            inv = inverse(total)
            grad = last_ref[rows, :]
            along = jnp.mean(grad * total, axis=-1, keepdims=True)
            grad = grad * inv - total * (along * inv * inv * inv)
            last_ref[rows, :] = grad
            slope = gate * (1.0 + projected * (1.0 - gate))
            row_ref[rows, :] = (cot_ref[rows, :width].astype(F32) + grad * slope).astype(BF16)
            return carry

        lax.fori_loop(0, tokens // chunk, middle, 0, unroll=True)
        mid_ref[...] = dot(row_ref[...], full[...], ((1,), (1,)))

        def leave(i, carry):
            rows = rows_of(i)
            total = sum_ref[rows, :]
            inv = inverse(total)
            grad = mid_ref[rows, :]
            along = jnp.mean(grad * total, axis=-1, keepdims=True)
            grad = last_ref[rows, :] + grad * inv - total * (along * inv * inv * inv)
            out[rows, :] = grad.astype(BF16)
            return carry

        lax.fori_loop(0, tokens // chunk, leave, 0, unroll=True)

    vmem = pl.BlockSpec(memory_space=pltpu.VMEM)
    return pl.pallas_call(
        body,
        out_shape=shaped((tokens, width)),
        in_specs=[pl.BlockSpec(memory_space=pltpu.SMEM)] + [vmem] * (len(arrays) + 3),
        out_specs=vmem,
        scratch_shapes=[
            pltpu.VMEM((width, width), BF16),
            pltpu.VMEM((tokens, width), F32),
            pltpu.VMEM((tokens, width), F32),
            pltpu.VMEM((tokens, width), F32),
            pltpu.VMEM((tokens, width), BF16),
        ],
        compiler_params=pltpu.CompilerParams(vmem_limit_bytes=VMEM_BYTES),
    )(where, *arrays, mixed, mixed_got, cot)


def id_rows(n_level, tokens):
    return -(-2 * n_level * (tokens // DH) // 16) * 16


def pack(where, keys, values, ids):
    heads = keys.shape[1] // DH
    n_level, tokens = ids.shape
    folds = tokens // DH
    top = heads * DH

    def body(where_ref, k_ref, v_ref, ids_ref, out):
        parts = []
        for level in range(n_level):
            for fold in range(folds):
                parts.append(ids_ref[level:level + 1, fold * DH:(fold + 1) * DH])
        whole = jnp.concatenate(parts, axis=0)
        both = jnp.concatenate([whole // 32, whole % 32], axis=0).astype(F32).astype(BF16)
        out[top:top + 2 * n_level * folds] = both
        for i in range(heads):
            cut = slice(i * DH, (i + 1) * DH)
            out[cut] = dot(k_ref[:, cut], v_ref[:, cut], ((0,), (0,))).astype(BF16)

    return run(body, [shaped((top + id_rows(n_level, tokens), DH))], where, keys, values, ids)[0]


def pack_chip(where, own, core, top):
    rows = own.shape[0] - top

    def body(where_ref, own_ref, core_ref, out):
        out[:top] = (own_ref[:top].astype(F32) + core_ref[:top].astype(F32)).astype(BF16)
        out[top:top + rows] = own_ref[top:]
        out[top + rows:] = core_ref[top:]

    return run(body, [shaped((top + 2 * rows, DH))], where, own, core)[0]


def lower(size):
    rows = lax.broadcasted_iota(jnp.int32, (size, size), 0)
    cols = lax.broadcasted_iota(jnp.int32, (size, size), 1)
    return rows >= cols


def upper(size):
    rows = lax.broadcasted_iota(jnp.int32, (size, size), 0)
    cols = lax.broadcasted_iota(jnp.int32, (size, size), 1)
    return rows <= cols


def attend(where, queries, keys, values, from_core, from_far, att_scale):
    length, width_dev = queries.shape
    heads = width_dev // DH

    def body(where_ref, q_ref, k_ref, v_ref, core_ref, far_ref, att, state):
        near = (where_ref[0] // 2).astype(F32)
        far = (where_ref[0] % 2).astype(F32)
        keep = lower(length)
        for i in range(heads):
            cut = slice(i * DH, (i + 1) * DH)
            state[i] = (core_ref[cut].astype(F32) * near + far_ref[cut].astype(F32) * far).astype(BF16)
            q = q_ref[:, cut]
            scores = jnp.where(keep, dot(q, k_ref[:, cut], ((1,), (1,))), 0.0).astype(BF16)
            both = jnp.dot(scores, v_ref[:, cut], preferred_element_type=F32)
            both += jnp.dot(q, state[i], preferred_element_type=F32)
            att[:, cut] = (att_scale * both).astype(BF16)

    return run(
        body, [shaped((length, width_dev)), shaped((heads, DH, DH))], where, queries, keys, values, from_core, from_far
    )


def mix_own(where, attended, head, tail):
    length = attended.shape[0] // 2
    half, width = head.shape[0] + tail.shape[0], head.shape[1]

    def body(where_ref, att, head_ref, tail_ref, out):
        core = where_ref[0] // 2
        own = jnp.concatenate([head_ref[...], tail_ref[...]], axis=0)
        for k in range(2):
            rows = at(where_ref[HEAD] ^ (1 - k), length)
            out[k] = jnp.dot(att[rows, at(core, half)], own, preferred_element_type=F32)

    return run(body, [shaped((2, length, width), F32)], where, attended, head, tail)[0]


def mix(where, attended, part, got_head, got_tail, other):
    length = attended.shape[0] // 2
    width = part.shape[2]
    half = got_head.shape[0] + got_tail.shape[0]
    dtype = BF16 if other else F32

    def body(where_ref, att, part_ref, head, tail, out):
        rows = at(where_ref[HEAD] ^ (1 if other else 0), length)
        core = where_ref[0] // 2
        got = jnp.concatenate([head[...], tail[...]], axis=0)
        total = part_ref[0 if other else 1]
        total += jnp.dot(att[rows, at(1 - core, half)], got, preferred_element_type=F32)
        out[...] = total.astype(dtype)

    return run(body, [shaped((length, width), dtype)], where, attended, part, got_head, got_tail)[0]


def weight_terms(where, attended, grad_own, grad_got):
    tokens, width = grad_own.shape

    def body(where_ref, att, own, got, send, keep):
        def term(m):
            total = None
            for k, ref in enumerate((own, got)):
                a = att[at(where_ref[HEAD] ^ k, tokens), at(where_ref[m], DH)]
                part = dot(a, ref[...], ((0,), (0,)))
                total = part if total is None else total + part
            return total

        send[0] = term(2).astype(BF16)
        send[1] = term(3).astype(BF16)
        keep[0] = term(0)
        keep[1] = term(1)

    return run(
        body, [shaped((2, DH, width)), shaped((2, DH, width), F32)], where, attended, grad_own, grad_got
    )


def add_core(where, keep, got):
    shape = keep.shape[1:]

    def body(where_ref, keep_ref, got_ref, send, rest):
        rest[...] = keep_ref[0] + got_ref[0].astype(F32)
        send[...] = (keep_ref[1] + got_ref[1].astype(F32)).astype(BF16)

    return run(body, [shaped(shape), shaped(shape, F32)], where, keep, got)


def add_far(where, keep, got, n_dp):
    rows, width = keep.shape
    cols = width // n_dp

    def body(where_ref, keep_ref, got_ref, rest, *send):
        for k in range(n_dp):
            cut = at(where_ref[DP] ^ k, cols)
            total = keep_ref[:, cut] + got_ref[:, cut].astype(F32)
            if k:
                send[k - 1][...] = total.astype(BF16)
            else:
                rest[...] = total

    return run(body, [shaped((rows, cols), F32)] + [shaped((rows, cols))] * (n_dp - 1), where, keep, got)


def add_all(where, keep, got):
    def body(where_ref, keep_ref, *refs):
        total = keep_ref[...]
        for ref in refs[:-1]:
            total = total + ref[...].astype(F32)
        refs[-1][...] = total.astype(BF16)

    return run(body, [shaped(keep.shape)], where, keep, *got)[0]


def rows_together(where, pieces):
    rows, cols = pieces[0].shape

    def body(where_ref, *refs):
        for m, ref in enumerate(refs[:-1]):
            refs[-1][at(where_ref[m], rows), :] = ref[...].astype(F32)

    return run(body, [shaped((rows * 4, cols), F32)], where, *pieces)[0]


def grad_attend(where, grad_own, grad_got, own_head, own_tail, got_head, got_tail, queries):
    tokens, width = grad_own.shape
    length, width_dev = queries.shape
    half = width_dev // 2

    def body(where_ref, own, got, head, tail, got_head, got_tail, q_ref, rows, back):
        for c, ends in enumerate(((head, tail), (got_head, got_tail))):
            block = jnp.concatenate([ends[0][...], ends[1][...]], axis=0)
            for k, ref in enumerate((own, got)):
                part = dot(ref[...], block, ((1,), (1,))).astype(BF16)
                rows[at(where_ref[HEAD] ^ k, tokens), at((where_ref[0] // 2) ^ c, half)] = part
        for i in range(width_dev // DH):
            cut = slice(i * DH, (i + 1) * DH)
            back[i] = dot(q_ref[:, cut], rows[:, cut], ((0,), (0,))).astype(BF16)

    outs = [shaped((length, width_dev)), shaped((width_dev // DH, DH, DH))]
    return run(body, outs, where, grad_own, grad_got, own_head, own_tail, got_head, got_tail, queries)


def query_grads(where, grad_rows, keys, values, state, att_scale):
    length, width_dev = keys.shape

    def body(where_ref, g_ref, k_ref, v_ref, s_ref, out):
        keep = lower(length)
        for i in range(width_dev // DH):
            cut = slice(i * DH, (i + 1) * DH)
            g = g_ref[:, cut]
            scores = jnp.where(keep, dot(g, v_ref[:, cut], ((1,), (1,))), 0.0).astype(BF16)
            both = jnp.dot(scores, k_ref[:, cut], preferred_element_type=F32)
            both += dot(g, s_ref[i], ((1,), (1,)))
            out[:, cut] = (att_scale * both).astype(BF16)

    return run(body, [shaped((length, width_dev))], where, grad_rows, keys, values, state)[0]


def key_value_parts(where, grad_rows, queries, keys, values):
    length, width_dev = keys.shape

    def body(where_ref, g_ref, q_ref, k_ref, v_ref, dk, dv):
        keep = upper(length)
        for i in range(width_dev // DH):
            cut = slice(i * DH, (i + 1) * DH)
            g, q, k, v = g_ref[:, cut], q_ref[:, cut], k_ref[:, cut], v_ref[:, cut]
            grad_scores = jnp.where(keep, dot(v, g, ((1,), (1,))), 0.0).astype(BF16)
            dk[:, cut] = jnp.dot(grad_scores, q, preferred_element_type=F32)
            scores = jnp.where(keep, dot(k, q, ((1,), (1,))), 0.0).astype(BF16)
            dv[:, cut] = jnp.dot(scores, g, preferred_element_type=F32)

    outs = [shaped((length, width_dev), F32)] * 2
    return run(body, outs, where, grad_rows, queries, keys, values)


def key_value_grads(where, key_part, value_part, keys, values, from_core, from_far, att_scale):
    length, width_dev = keys.shape

    def body(where_ref, kp_ref, vp_ref, k_ref, v_ref, core_ref, far_ref, dk, dv):
        near = 1.0 - (where_ref[0] // 2).astype(F32)
        far = 1.0 - (where_ref[0] % 2).astype(F32)
        for i in range(width_dev // DH):
            cut = slice(i * DH, (i + 1) * DH)
            back = (core_ref[i].astype(F32) * near + far_ref[i].astype(F32) * far).astype(BF16)
            both = kp_ref[:, cut] + dot(v_ref[:, cut], back, ((1,), (1,)))
            dk[:, cut] = (att_scale * both).astype(BF16)
            both = vp_ref[:, cut] + jnp.dot(k_ref[:, cut], back, preferred_element_type=F32)
            dv[:, cut] = (att_scale * both).astype(BF16)

    outs = [shaped((length, width_dev))] * 2
    return run(body, outs, where, key_part, value_part, keys, values, from_core, from_far)


def fits(queries, out_proj, depth_proj, code_table, code_ids):
    n_seq, n_head = lax.axis_size("seq"), lax.axis_size("head")
    return (
        n_seq == 4
        and n_head == 2
        and queries.shape[2] == 4 * DH
        and code_table.shape[0] == 2
        and out_proj.shape[1] % 128 == 0
        and depth_proj.shape[1] % 128 == 0
        and code_table.shape[1] % 128 == 0
        and code_ids.shape[1] % DH == 0
        and code_table.shape[1] * n_head * lax.axis_size("dp") <= 32 * 256
    )


def on_device(queries, keys, values, out_proj, depth_proj, code_table, code_ids, depth_cotangent):
    if not fits(queries, out_proj, depth_proj, code_table, code_ids):
        return on_device_any(
            queries, keys, values, out_proj, depth_proj, code_table, code_ids, depth_cotangent
        )
    n_dp = lax.axis_size("dp")
    me_seq, me_head, me_dp = (lax.axis_index(a) for a in ("seq", "head", "dp"))
    group_len = queries.shape[1]
    width = code_table.shape[2]
    att_scale = float(group_len * lax.axis_size("seq")) ** (-0.5)
    core, far = me_seq % 2, me_seq // 2
    lane = 2 * core + far
    where = jnp.stack([lane, lane ^ 1, lane ^ 2, lane ^ 3, me_head, me_dp, me_seq]).astype(jnp.int32)
    queries, keys, values = queries[0], keys[0], values[0]

    def far_swap(block):
        return swap(block, "seq", 2)

    def core_swap(block):
        return swap(block, "seq", 1)

    def all_lanes(block):
        got = far_swap(block)
        return [block, got, core_swap(block), core_swap(got)]

    t_rows, tokens = code_table.shape[1], code_ids.shape[1]
    half = t_rows * n_dp
    lanes_0 = first_lanes(code_table, depth_proj, n_dp)
    pieces_0 = lax.all_to_all(lanes_0, "dp", 0, 0)
    lanes_1 = second_lanes(code_table, out_proj, lanes_0)
    distances = [n_dp // 2] + [k for k in range(1, n_dp) if k != n_dp // 2]
    pieces_1 = [lanes_1] + [swap(lanes_1, "dp", k) for k in distances]

    top = keys.shape[1]
    keys, values, _ = lax.optimization_barrier((keys, values, lanes_1))
    mine = pack(where, keys, values, code_ids[0].T)
    from_core = core_swap(mine)
    chip = pack_chip(where, mine, from_core, top)
    from_far = far_swap(chip)
    packed = (mine, from_core, from_far)

    attended, state_in = attend(where, queries, keys, values, from_core, from_far, att_scale)

    pieces_0, _ = lax.optimization_barrier((pieces_0, attended))
    fold = depth_proj.shape[0] // 4
    early = fold + fold * 7 // 16
    late = 2 * fold - early
    part_0, depth_part, depth_top = first_parts(where, pieces_0, t_rows, early)
    got_0 = swap(part_0, "head", 1)
    depth_far = far_swap(depth_top)

    pieces_1, depth_far = lax.optimization_barrier((pieces_1, depth_far))
    part_1, out_head, out_tail = second_parts(where, pieces_1, [0, *distances], t_rows)
    got_head, got_tail = core_swap(out_head), core_swap(out_tail)
    got_1 = swap(part_1, "head", 1)

    mixed_part = mix_own(where, attended, out_head, out_tail)
    got_0, got_head, _ = lax.optimization_barrier((got_0, got_head, part_1))
    own_0, to_core, to_far = embed(where, packed, top, 0, 2, tokens, part_0, got_0, half, n_dp, late)
    far_0 = far_swap(to_far)

    got_tail, _ = lax.optimization_barrier((got_tail, to_far))
    mixed_send = mix(where, attended, mixed_part, got_head, got_tail, True)
    mixed_got = swap(mixed_send, "head", 1)
    mixed = mix(where, attended, mixed_part, got_head, got_tail, False)
    core_0 = core_swap(to_core)

    got_1, _, _ = lax.optimization_barrier((got_1, mixed, mixed_send))
    own_1, to_core, to_far = embed(where, packed, top, 1, 2, tokens, part_1, got_1, half, n_dp, 0)
    far_1 = far_swap(to_far)
    depth_core, depth_core_far = core_swap(depth_part), core_swap(depth_far)
    far_0, far_1, mixed_got, depth_core, depth_core_far, core_0 = lax.optimization_barrier(
        (far_0, far_1, mixed_got, depth_core, depth_core_far, core_0)
    )
    core_far_0, core_1, core_far_1 = core_swap(far_0), core_swap(to_core), core_swap(far_1)

    end = 2 * tokens
    folds = [(depth_part, 0), (depth_part, fold), (got_0, half), (got_0, half + fold)]
    folds += [(depth_far, 0), (depth_far, fold), (far_0, end), (far_0, end + fold)]
    folds += [(depth_core, 0), (depth_core, fold), (core_0, tokens), (core_0, tokens + fold)]
    folds += [(depth_core_far, 0), (depth_core_far, fold), (core_far_0, end), (core_far_0, end + fold)]
    rest = [None] * 16
    rest[5], rest[13] = (far_0, end + 2 * fold), (core_far_0, end + 2 * fold)
    first = [(own_0, 0), (far_0, 0), (core_0, 0), (core_far_0, tokens)]
    second = [(own_1, 0), (far_1, 0), (core_1, 0), (core_far_1, tokens)]
    cot = depth_cotangent[0].reshape(tokens, -1)
    grad_mixed = depth_grad(where, folds, rest, late, first, second, mixed, mixed_got, cot)

    grad_got = swap(grad_mixed, "head", 1)
    send, keep = weight_terms(where, attended, grad_mixed, grad_got)
    send, keep = add_core(where, keep, core_swap(send))
    from_far = far_swap(send)
    grad_rows, back = grad_attend(where, grad_mixed, grad_got, out_head, out_tail, got_head, got_tail, queries)
    back_core = core_swap(back)
    back_chip = (back.astype(F32) + back_core.astype(F32)).astype(BF16)
    key_part, value_part = key_value_parts(where, grad_rows, queries, keys, values)
    grad_query = query_grads(where, grad_rows, keys, values, state_in, att_scale)
    from_far, key_part, value_part, grad_query, back_chip = lax.optimization_barrier(
        (from_far, key_part, value_part, grad_query, back_chip)
    )
    keep, *send = add_far(where, keep, from_far, n_dp)
    got = [swap(send[k - 1], "dp", k) for k in reversed(range(1, n_dp))]
    back_chip, keep = lax.optimization_barrier((back_chip, keep))
    back_far = far_swap(back_chip)
    block = add_all(where, keep, got)
    blocks = [block, far_swap(block), core_swap(block), swap(block, "seq", 3)]
    key_part, block = lax.optimization_barrier((key_part, block))
    grad_key, grad_value = key_value_grads(
        where, key_part, value_part, keys, values, back_core, back_far, att_scale
    )
    blocks, grad_key, grad_value = lax.optimization_barrier((blocks, grad_key, grad_value))
    grad_out_proj = rows_together(where, blocks)
    return grad_query[None], grad_key[None], grad_value[None], grad_out_proj


def solution(mesh):
    in_specs = (
        P("dp", "seq", "head"),
        P("dp", "seq", "head"),
        P("dp", "seq", "head"),
        P("head", "dp"),
        P(None, ("head", "dp")),
        P(None, ("head", "dp"), None),
        P("dp", ("seq", "head"), None),
        P("dp", ("seq", "head"), None, None),
    )
    out_specs = (
        P("dp", "seq", "head"),
        P("dp", "seq", "head"),
        P("dp", "seq", "head"),
        P("head", "dp"),
    )
    return jax.shard_map(
        on_device, mesh=mesh, in_specs=in_specs, out_specs=out_specs, check_vma=False
    )
```

```python
import jax
import jax.numpy as jnp
from jax import lax
from jax.experimental import pallas as pl
from jax.experimental.pallas import tpu as pltpu
from jax.sharding import PartitionSpec as P

DH = 128
F32 = jnp.float32
BF16 = jnp.bfloat16


def swap(block, axis, mask):
    return lax.ppermute(block, axis, [(i, i ^ mask) for i in range(lax.axis_size(axis))])


def has_bit(index, bit):
    return lax.bitwise_and(index, jnp.int32(bit)) != 0


def in_order(pieces, index):
    pieces = list(pieces)
    bit = 1
    while bit < len(pieces):
        odd = has_bit(index, bit)
        pieces = [jnp.where(odd, pieces[j ^ bit], pieces[j]) for j in range(len(pieces))]
        bit *= 2
    return pieces


def pick(array, index, dim):
    return lax.dynamic_index_in_dim(array, index, dim, keepdims=False)


def exchange(block, axis):
    return [block] + [swap(block, axis, k) for k in range(1, lax.axis_size(axis))]


def dot(a, b, dims):
    return lax.dot_general(a, b, ((dims[0], dims[1]), ((), ())), preferred_element_type=F32)


def earlier_sum(state, backward):
    n_seq = lax.axis_size("seq")
    me = lax.axis_index("seq")
    before = jnp.zeros_like(state)
    total = state
    bit = 1
    while bit < n_seq:
        got = swap(total.astype(BF16), "seq", bit).astype(F32)
        mine = has_bit(me, bit)
        takes = jnp.logical_not(mine) if backward else mine
        before = before + jnp.where(takes, got, 0.0)
        total = total + got
        bit *= 2
    return before.astype(BF16)


def on_device_any(queries, keys, values, out_proj, depth_proj, code_table, code_ids, depth_cotangent):
    n_seq, n_head, n_dp = (lax.axis_size(a) for a in ("seq", "head", "dp"))
    me_seq, me_head, me_dp = (lax.axis_index(a) for a in ("seq", "head", "dp"))
    group_len, width_dev = queries.shape[1:]
    heads_here = width_dev // DH
    tokens = group_len // n_head
    n_far = n_seq // 2
    me_core = lax.bitwise_and(me_seq, jnp.int32(1))
    me_far = lax.shift_right_logical(me_seq, jnp.int32(1))
    lane = me_core * n_far + me_far
    att_scale = float(group_len * n_seq) ** (-0.5)
    width = code_table.shape[2]
    wide = width // n_seq
    far = [2 * m for m in range(n_far)]

    def far_exchange(block):
        return [block] + [swap(block, "seq", m) for m in far[1:]]

    def seq_lanes(block):
        near = jnp.stack(in_order(far_exchange(block), me_far))
        both = in_order([near, swap(near, "seq", 1)], me_core)
        return jnp.concatenate(both, axis=0)

    ids = code_ids[0].T
    ids_far = jnp.stack(far_exchange(ids))
    ids_rel = jnp.stack([ids_far, swap(ids_far, "seq", 1)])

    table = lax.dynamic_slice_in_dim(code_table, lane * wide, wide, axis=2)
    rows_dev = table.shape[1]
    embedded = []
    row_no = []
    for k_head in range(n_head):
        for k_dp in range(n_dp):
            owner = (me_head ^ k_head) * n_dp + (me_dp ^ k_dp)
            row_no.append(owner * rows_dev + jnp.arange(rows_dev, dtype=jnp.int32))
    row_no = jnp.concatenate(row_no)
    for level in range(table.shape[0]):
        part = jnp.concatenate(exchange(table[level], "dp"), axis=0)
        part = jnp.concatenate(exchange(part, "head"), axis=0)
        level_ids = ids_rel[:, :, level].reshape(-1)
        onehot = (level_ids[:, None] == row_no[None, :]).astype(BF16)
        rel = dot(onehot, part, ((1,), (0,))).astype(BF16).reshape(2, n_far, tokens, wide)
        mine = [rel[:, 0]] + [swap(rel[:, m // 2], "seq", m) for m in far[1:]]
        near = jnp.stack([block[0] for block in mine])
        other = swap(jnp.stack([block[1] for block in mine]), "seq", 1)
        near = jnp.stack(in_order(list(near), me_far))
        other = jnp.stack(in_order(list(other), me_far))
        lanes = jnp.concatenate(in_order([near, other], me_core), axis=0)
        embedded.append(lanes.transpose(1, 0, 2).reshape(tokens, width))

    out_rows = out_proj.shape[0] // n_seq
    out_lane = lax.dynamic_slice_in_dim(out_proj, lane * out_rows, out_rows, axis=0)
    out_part = jnp.concatenate(in_order(exchange(out_lane, "dp"), me_dp), axis=1)
    out_part = jnp.stack(in_order(exchange(out_part, "head"), me_head))
    out_full = seq_lanes(out_part).transpose(1, 0, 2, 3).reshape(n_head * width_dev, width)

    depth_rows = depth_proj.shape[0] // n_seq
    depth_lane = lax.dynamic_slice_in_dim(depth_proj, lane * depth_rows, depth_rows, axis=0)
    depth_part = jnp.concatenate(in_order(exchange(depth_lane, "dp"), me_dp), axis=1)
    depth_part = jnp.concatenate(in_order(exchange(depth_part, "head"), me_head), axis=1)
    proj_mat = seq_lanes(depth_part).reshape(width, width)

    query_rows = queries[0].reshape(group_len, heads_here, DH)
    key_rows = keys[0].reshape(group_len, heads_here, DH)
    value_rows = values[0].reshape(group_len, heads_here, DH)
    places = jnp.arange(group_len, dtype=jnp.int32)
    causal = (places[:, None] >= places[None, :]).astype(F32)
    state_local = jnp.einsum("thd,the->hde", key_rows, value_rows, preferred_element_type=F32)
    state_in = earlier_sum(state_local, False)
    scores = (
        jnp.einsum("thd,shd->hts", query_rows, key_rows, preferred_element_type=F32) * causal
    ).astype(BF16)
    attended = (
        att_scale
        * (
            jnp.einsum("hts,she->the", scores, value_rows, preferred_element_type=F32)
            + jnp.einsum("thd,hde->the", query_rows, state_in, preferred_element_type=F32)
        )
    ).astype(BF16)
    attended = attended.reshape(n_head, tokens, width_dev)
    att_all = [pick(attended, me_head, 0)]
    att_all += [swap(pick(attended, me_head ^ k, 0), "head", k) for k in range(1, n_head)]
    att_all = jnp.concatenate(in_order(att_all, me_head), axis=1)
    mixed = dot(att_all, out_full, ((1,), (0,)))

    cot = depth_cotangent[0]
    n_level = cot.shape[1]
    carried = mixed
    kept = []
    for level in range(n_level):
        summed = carried + embedded[level].astype(F32)
        inv = lax.rsqrt(jnp.mean(summed * summed, axis=-1, keepdims=True) + 1e-05)
        if level < n_level - 1:
            projected = dot((summed * inv).astype(BF16), proj_mat, ((1,), (0,)))
            carried = summed + projected * jax.nn.sigmoid(projected)
        else:
            projected = None
        kept.append((summed, inv, projected))
    grad = None
    for level in reversed(range(n_level)):
        summed, inv, projected = kept[level]
        grad_proj = cot[:, level, :]
        if grad is not None:
            gate = jax.nn.sigmoid(projected)
            slope = gate * (1.0 + projected * (1.0 - gate))
            grad_proj = (grad_proj.astype(F32) + grad * slope).astype(BF16)
        grad_normed = dot(grad_proj, proj_mat, ((1,), (1,)))
        along = jnp.mean(grad_normed * summed, axis=-1, keepdims=True)
        grad_sum = grad_normed * inv - summed * (along * inv * inv * inv)
        grad = grad_sum if grad is None else grad + grad_sum
    grad_mixed = grad.astype(BF16)

    out_heads = out_full.reshape(n_head, width_dev, width)
    grad_rows = []
    for k in range(1, n_head):
        part = dot(grad_mixed, pick(out_heads, me_head ^ k, 0), ((1,), (1,))).astype(BF16)
        grad_rows.append(swap(part, "head", k))
    own_part = dot(grad_mixed, pick(out_heads, me_head, 0), ((1,), (1,))).astype(BF16)
    grad_rows = jnp.concatenate(in_order([own_part] + grad_rows, me_head), axis=0)
    grad_rows = grad_rows.reshape(group_len, heads_here, DH)

    rows = width_dev // n_seq
    att_lanes = att_all.reshape(tokens, n_head, 2, n_far, rows)

    def term(core):
        part = pick(att_lanes, core, 2).reshape(tokens, n_head * n_far * rows)
        return dot(part, grad_mixed, ((0,), (0,)))

    got = swap(term(1 - me_core).astype(BF16), "seq", 1)
    chip = term(me_core) + got.astype(F32)
    chip = chip.reshape(n_head, n_far, rows, width)
    total = pick(pick(chip, me_head, 0), me_far, 0)
    for m in far:
        for k in range(n_head):
            if m or k:
                piece = pick(pick(chip, me_head ^ k, 0), me_far ^ (m // 2), 0).astype(BF16)
                mask = m * n_head + k
                total = total + swap(piece, ("seq", "head"), mask).astype(F32)
    columns = total.reshape(rows, n_dp, width // n_dp)
    block = pick(columns, me_dp, 1)
    for k in range(1, n_dp):
        block = block + swap(pick(columns, me_dp ^ k, 1).astype(BF16), "dp", k).astype(F32)
    grad_out_proj = seq_lanes(block.astype(BF16)).reshape(width_dev, width // n_dp).astype(F32)

    back_local = jnp.einsum("thd,the->hde", query_rows, grad_rows, preferred_element_type=F32)
    back_state = earlier_sum(back_local, True)
    grad_scores = (
        jnp.einsum("the,she->hts", grad_rows, value_rows, preferred_element_type=F32) * causal
    ).astype(BF16)
    grad_query = att_scale * (
        jnp.einsum("hts,shd->thd", grad_scores, key_rows, preferred_element_type=F32)
        + jnp.einsum("the,hde->thd", grad_rows, state_in, preferred_element_type=F32)
    )
    grad_key = att_scale * (
        jnp.einsum("hts,thd->shd", grad_scores, query_rows, preferred_element_type=F32)
        + jnp.einsum("she,hde->shd", value_rows, back_state, preferred_element_type=F32)
    )
    grad_value = att_scale * (
        jnp.einsum("hts,the->she", scores, grad_rows, preferred_element_type=F32)
        + jnp.einsum("shd,hde->she", key_rows, back_state, preferred_element_type=F32)
    )
    out_shape = (1, group_len, width_dev)
    return (
        grad_query.reshape(out_shape).astype(BF16),
        grad_key.reshape(out_shape).astype(BF16),
        grad_value.reshape(out_shape).astype(BF16),
        grad_out_proj,
    )


VMEM_BYTES = 48 * 1024 * 1024


def run(body, outs, where, *args):
    vmem = pl.BlockSpec(memory_space=pltpu.VMEM)
    return pl.pallas_call(
        body,
        out_shape=outs,
        in_specs=[pl.BlockSpec(memory_space=pltpu.SMEM)] + [vmem] * len(args),
        out_specs=[vmem] * len(outs),
        compiler_params=pltpu.CompilerParams(vmem_limit_bytes=VMEM_BYTES),
    )(where, *args)


def shaped(shape, dtype=BF16):
    return jax.ShapeDtypeStruct(shape, dtype)


def at(index, size):
    return pl.ds(pl.multiple_of(index * size, size), size)


HEAD, DP, SEQ = 4, 5, 6


def own_lane():
    me = lax.axis_index("seq")
    return 2 * (me % 2) + me // 2


def copies(body_of, outs, args):
    n_copies = len(body_of(None))

    def body(*refs):
        sems = refs[-1]
        going = [pltpu.make_async_copy(src, dst, sems.at[i]) for i, (src, dst) in enumerate(body_of(refs[:-1]))]
        for copy in going:
            copy.start()
        for copy in going:
            copy.wait()

    anywhere = pl.BlockSpec(memory_space=pl.ANY)
    return pl.pallas_call(
        body,
        out_shape=outs,
        in_specs=[anywhere] * len(args),
        out_specs=pl.BlockSpec(memory_space=pltpu.VMEM),
        scratch_shapes=[pltpu.SemaphoreType.DMA((n_copies,))],
    )(*args)


def first_lanes(code_table, depth_proj, n_dp):
    t_rows, t_cols = code_table.shape[1], code_table.shape[2] // 4
    d_half, d_cols = depth_proj.shape[0] // 8, depth_proj.shape[1]

    def body(table, depth, lanes, sems):
        moves = [(table.at[0, :, at(own_lane(), t_cols)], lanes.at[0, 0:t_rows])]
        for half in range(2):
            cols = slice(half * d_cols, (half + 1) * d_cols)
            moves.append((depth.at[at(2 * own_lane() + half, d_half)], lanes.at[0, t_rows:t_rows + d_half, cols]))
        going = [pltpu.make_async_copy(src, dst, sems.at[i]) for i, (src, dst) in enumerate(moves)]
        for copy in going:
            copy.start()
        for copy in going:
            copy.wait()
        for k in range(1, n_dp):
            lanes[k] = lanes[0]

    return pl.pallas_call(
        body,
        out_shape=shaped((n_dp, t_rows + d_half, t_cols)),
        in_specs=[pl.BlockSpec(memory_space=pl.ANY)] * 2,
        out_specs=pl.BlockSpec(memory_space=pltpu.VMEM),
        scratch_shapes=[pltpu.SemaphoreType.DMA((3,))],
    )(code_table, depth_proj)


def second_lanes(code_table, out_proj, after):
    t_rows, t_cols = code_table.shape[1], code_table.shape[2] // 4
    rows, cols = out_proj.shape[0] // 2, out_proj.shape[1]

    def views(refs):
        if refs is None:
            return [0, 1]
        table, out, _, lanes = refs
        return [
            (table.at[1, :, at(own_lane(), t_cols)], lanes.at[0:t_rows]),
            (out.at[at(own_lane() // 2, rows)], lanes.at[t_rows:t_rows + rows]),
        ]

    return copies(views, shaped((t_rows + rows, cols)), [code_table, out_proj, after])


def first_parts(where, pieces, t_rows, early):
    n, d_half, t_cols = pieces.shape
    d_half, d_cols = d_half - t_rows, t_cols // 2
    top, fold = n * t_rows, 2 * d_half

    def body(where_ref, ref, both, depth, top_fold):
        for k in range(n):
            both[k * t_rows:(k + 1) * t_rows, :] = ref[where_ref[DP] ^ k, :t_rows]
            place = where_ref[DP] ^ k
            cols = at(place % 2, d_cols)
            for half in range(2):
                part = ref[place, t_rows:, half * d_cols:(half + 1) * d_cols]
                row = pl.multiple_of((place // 2) * fold + half * d_half, d_half)
                both[pl.ds(pl.multiple_of(top + row, d_half), d_half), cols] = part
                depth[pl.ds(row, d_half), cols] = part
        top_fold[...] = depth[:early]

    rows = fold * n // 2
    return run(body, [shaped((top + rows, t_cols)), shaped((rows, t_cols)), shaped((early, t_cols))], where, pieces)


def second_parts(where, pieces, distances, t_rows):
    rows, cols = pieces[0].shape[0] - t_rows, pieces[0].shape[1]
    n = len(pieces)
    first = rows * 5 // 8

    def body(where_ref, *refs):
        table, head, tail = refs[n:]
        for k, ref in zip(distances, refs):
            cut = at(where_ref[DP] ^ k, cols)
            table[k * t_rows:(k + 1) * t_rows, :] = ref[:t_rows]
            head[:, cut] = ref[t_rows:t_rows + first]
            tail[:, cut] = ref[t_rows + first:]

    outs = [shaped((n * t_rows, cols)), shaped((first, n * cols)), shaped((rows - first, n * cols))]
    return run(body, outs, where, *pieces)


def embed(where, packed, top, level, n_level, tokens, own, got, half, n_dp, late):
    folds = tokens // DH
    n_rows = id_rows(n_level, tokens)
    rows, cols = own.shape
    rows_dev, extra = half // n_dp, rows - half

    def body(where_ref, mine_ref, core_ref, far_ref, own_ref, got_ref, *outs):
        def ids_of(ref, start):
            all_ids = ref[start:start + 2 * n_level * folds].astype(F32)
            mine = level * folds
            high = all_ids[mine:mine + folds]
            low = all_ids[(n_level * folds) + mine:(n_level * folds) + mine + folds]
            ids = high * 32.0 + low
            return jnp.concatenate([ids[f:f + 1] for f in range(folds)], axis=1)

        place = lax.broadcasted_iota(jnp.int32, (tokens, half), 1)
        owner = jnp.bitwise_xor(place // rows_dev, where_ref[DP])
        base = owner * rows_dev + place % rows_dev
        rows_of = [(mine_ref, top), (core_ref, top), (far_ref, top), (far_ref, top + n_rows)]
        columns = jnp.concatenate([ids_of(*r) for r in rows_of], axis=0).T.astype(jnp.int32)
        for m in (2, 3, 1, 0):
            col = columns[:, m:m + 1]
            total = None
            for k, ref in enumerate((own_ref, got_ref)):
                start = (where_ref[HEAD] ^ k) * half
                hot = (base == col - start).astype(F32).astype(BF16)
                part = jnp.dot(hot, ref[:half], preferred_element_type=F32)
                total = part if total is None else total + part
            total = total.astype(BF16)
            if m < 2:
                outs[m][:tokens] = total
            else:
                outs[2][(m - 2) * tokens:(m - 1) * tokens, :] = total
        if extra:
            outs[1][tokens:] = got_ref[half:]
            outs[2][2 * tokens:2 * tokens + extra] = got_ref[half:]
            outs[2][2 * tokens + extra:] = own_ref[rows - late:]

    outs = [shaped((tokens, cols)), shaped((tokens + extra, cols)), shaped((2 * tokens + extra + late, cols))]
    return run(body, outs, where, *packed, own, got)


def depth_grad(where, folds, rest, late, first, second, mixed, mixed_got, cot):
    arrays, which = [], []
    for array, _ in folds + first + second:
        found = [i for i, other in enumerate(arrays) if other is array]
        if not found:
            arrays.append(array)
        which.append(found[0] if found else len(arrays) - 1)
    starts = [start for _, start in folds + first + second]
    tokens, width = mixed.shape
    cols = width // 4
    chunk = 32

    def body(where_ref, *refs):
        parts = refs[:len(arrays)]
        mixed_ref, got_ref, cot_ref, out, full, sum_ref, mid_ref, last_ref, row_ref = refs[len(arrays):]
        for n in range(16):
            m, x, j = n // 4, n // 2 % 2, n % 2
            place = (where_ref[HEAD] ^ x) * 2 + j
            if rest[n] is None:
                full[at(where_ref[m], cols), at(place, cols)] = parts[which[n]][starts[n]:starts[n] + cols]
            else:
                main = pl.ds(pl.multiple_of(where_ref[m] * cols, cols), cols - late)
                tail = pl.ds(pl.multiple_of(where_ref[m] * cols + cols - late, 16), late)
                array = next(i for i, other in enumerate(arrays) if other is rest[n][0])
                full[main, at(place, cols)] = parts[which[n]][starts[n]:starts[n] + cols - late]
                full[tail, at(place, cols)] = parts[array][rest[n][1]:rest[n][1] + late]

        def rows_of(i):
            return pl.ds(pl.multiple_of(i * chunk, chunk), chunk)

        def lane_rows(i, n):
            return parts[which[n]][pl.ds(pl.multiple_of(starts[n] + i * chunk, chunk), chunk), :].astype(F32)

        def inverse(total):
            return lax.rsqrt(jnp.mean(total * total, axis=-1, keepdims=True) + 1e-05)

        def enter(i, carry):
            rows = rows_of(i)
            for m in range(4):
                cut = at(where_ref[m], cols)
                sum_ref[rows, cut] = mixed_ref[rows, cut] + got_ref[rows, cut].astype(F32) + lane_rows(i, 16 + m)
            total = sum_ref[rows, :]
            row_ref[rows, :] = (total * inverse(total)).astype(BF16)
            return carry

        lax.fori_loop(0, tokens // chunk, enter, 0, unroll=True)
        mid_ref[...] = jnp.dot(row_ref[...], full[...], preferred_element_type=F32)
        last_ref[...] = dot(cot_ref[:, width:], full[...], ((1,), (1,)))

        def middle(i, carry):
            rows = rows_of(i)
            projected = mid_ref[rows, :]
            gate = jax.nn.sigmoid(projected)
            mid_ref[rows, :] = sum_ref[rows, :] + projected * gate
            for m in range(4):
                cut = at(where_ref[m], cols)
                mid_ref[rows, cut] += lane_rows(i, 20 + m)
            total = mid_ref[rows, :]
            inv = inverse(total)
            grad = last_ref[rows, :]
            along = jnp.mean(grad * total, axis=-1, keepdims=True)
            grad = grad * inv - total * (along * inv * inv * inv)
            last_ref[rows, :] = grad
            slope = gate * (1.0 + projected * (1.0 - gate))
            row_ref[rows, :] = (cot_ref[rows, :width].astype(F32) + grad * slope).astype(BF16)
            return carry

        lax.fori_loop(0, tokens // chunk, middle, 0, unroll=True)
        mid_ref[...] = dot(row_ref[...], full[...], ((1,), (1,)))

        def leave(i, carry):
            rows = rows_of(i)
            total = sum_ref[rows, :]
            inv = inverse(total)
            grad = mid_ref[rows, :]
            along = jnp.mean(grad * total, axis=-1, keepdims=True)
            grad = last_ref[rows, :] + grad * inv - total * (along * inv * inv * inv)
            out[rows, :] = grad.astype(BF16)
            return carry

        lax.fori_loop(0, tokens // chunk, leave, 0, unroll=True)

    vmem = pl.BlockSpec(memory_space=pltpu.VMEM)
    return pl.pallas_call(
        body,
        out_shape=shaped((tokens, width)),
        in_specs=[pl.BlockSpec(memory_space=pltpu.SMEM)] + [vmem] * (len(arrays) + 3),
        out_specs=vmem,
        scratch_shapes=[
            pltpu.VMEM((width, width), BF16),
            pltpu.VMEM((tokens, width), F32),
            pltpu.VMEM((tokens, width), F32),
            pltpu.VMEM((tokens, width), F32),
            pltpu.VMEM((tokens, width), BF16),
        ],
        compiler_params=pltpu.CompilerParams(vmem_limit_bytes=VMEM_BYTES),
    )(where, *arrays, mixed, mixed_got, cot)


def id_rows(n_level, tokens):
    return -(-2 * n_level * (tokens // DH) // 16) * 16


def pack(where, keys, values, ids):
    heads = keys.shape[1] // DH
    n_level, tokens = ids.shape
    folds = tokens // DH
    top = heads * DH

    def body(where_ref, k_ref, v_ref, ids_ref, out):
        parts = []
        for level in range(n_level):
            for fold in range(folds):
                parts.append(ids_ref[level:level + 1, fold * DH:(fold + 1) * DH])
        whole = jnp.concatenate(parts, axis=0)
        both = jnp.concatenate([whole // 32, whole % 32], axis=0).astype(F32).astype(BF16)
        out[top:top + 2 * n_level * folds] = both
        for i in range(heads):
            cut = slice(i * DH, (i + 1) * DH)
            out[cut] = dot(k_ref[:, cut], v_ref[:, cut], ((0,), (0,))).astype(BF16)

    return run(body, [shaped((top + id_rows(n_level, tokens), DH))], where, keys, values, ids)[0]


def pack_chip(where, own, core, top):
    rows = own.shape[0] - top

    def body(where_ref, own_ref, core_ref, out):
        out[:top] = (own_ref[:top].astype(F32) + core_ref[:top].astype(F32)).astype(BF16)
        out[top:top + rows] = own_ref[top:]
        out[top + rows:] = core_ref[top:]

    return run(body, [shaped((top + 2 * rows, DH))], where, own, core)[0]


def lower(size):
    rows = lax.broadcasted_iota(jnp.int32, (size, size), 0)
    cols = lax.broadcasted_iota(jnp.int32, (size, size), 1)
    return rows >= cols


def upper(size):
    rows = lax.broadcasted_iota(jnp.int32, (size, size), 0)
    cols = lax.broadcasted_iota(jnp.int32, (size, size), 1)
    return rows <= cols


def attend(where, queries, keys, values, from_core, from_far, att_scale):
    length, width_dev = queries.shape
    heads = width_dev // DH

    def body(where_ref, q_ref, k_ref, v_ref, core_ref, far_ref, att, state):
        near = (where_ref[0] // 2).astype(F32)
        far = (where_ref[0] % 2).astype(F32)
        keep = lower(length)
        for i in range(heads):
            cut = slice(i * DH, (i + 1) * DH)
            state[i] = (core_ref[cut].astype(F32) * near + far_ref[cut].astype(F32) * far).astype(BF16)
            q = q_ref[:, cut]
            scores = jnp.where(keep, dot(q, k_ref[:, cut], ((1,), (1,))), 0.0).astype(BF16)
            both = jnp.dot(scores, v_ref[:, cut], preferred_element_type=F32)
            both += jnp.dot(q, state[i], preferred_element_type=F32)
            att[:, cut] = (att_scale * both).astype(BF16)

    return run(
        body, [shaped((length, width_dev)), shaped((heads, DH, DH))], where, queries, keys, values, from_core, from_far
    )


def mix_own(where, attended, head, tail):
    length = attended.shape[0] // 2
    half, width = head.shape[0] + tail.shape[0], head.shape[1]

    def body(where_ref, att, head_ref, tail_ref, out):
        core = where_ref[0] // 2
        own = jnp.concatenate([head_ref[...], tail_ref[...]], axis=0)
        for k in range(2):
            rows = at(where_ref[HEAD] ^ (1 - k), length)
            out[k] = jnp.dot(att[rows, at(core, half)], own, preferred_element_type=F32)

    return run(body, [shaped((2, length, width), F32)], where, attended, head, tail)[0]


def mix(where, attended, part, got_head, got_tail, other):
    length = attended.shape[0] // 2
    width = part.shape[2]
    half = got_head.shape[0] + got_tail.shape[0]
    dtype = BF16 if other else F32

    def body(where_ref, att, part_ref, head, tail, out):
        rows = at(where_ref[HEAD] ^ (1 if other else 0), length)
        core = where_ref[0] // 2
        got = jnp.concatenate([head[...], tail[...]], axis=0)
        total = part_ref[0 if other else 1]
        total += jnp.dot(att[rows, at(1 - core, half)], got, preferred_element_type=F32)
        out[...] = total.astype(dtype)

    return run(body, [shaped((length, width), dtype)], where, attended, part, got_head, got_tail)[0]


def weight_terms(where, attended, grad_own, grad_got):
    tokens, width = grad_own.shape

    def body(where_ref, att, own, got, send, keep):
        def term(m):
            total = None
            for k, ref in enumerate((own, got)):
                a = att[at(where_ref[HEAD] ^ k, tokens), at(where_ref[m], DH)]
                part = dot(a, ref[...], ((0,), (0,)))
                total = part if total is None else total + part
            return total

        send[0] = term(2).astype(BF16)
        send[1] = term(3).astype(BF16)
        keep[0] = term(0)
        keep[1] = term(1)

    return run(
        body, [shaped((2, DH, width)), shaped((2, DH, width), F32)], where, attended, grad_own, grad_got
    )


def add_core(where, keep, got):
    shape = keep.shape[1:]

    def body(where_ref, keep_ref, got_ref, send, rest):
        rest[...] = keep_ref[0] + got_ref[0].astype(F32)
        send[...] = (keep_ref[1] + got_ref[1].astype(F32)).astype(BF16)

    return run(body, [shaped(shape), shaped(shape, F32)], where, keep, got)


def add_far(where, keep, got, n_dp):
    rows, width = keep.shape
    cols = width // n_dp

    def body(where_ref, keep_ref, got_ref, rest, *send):
        for k in range(n_dp):
            cut = at(where_ref[DP] ^ k, cols)
            total = keep_ref[:, cut] + got_ref[:, cut].astype(F32)
            if k:
                send[k - 1][...] = total.astype(BF16)
            else:
                rest[...] = total

    return run(body, [shaped((rows, cols), F32)] + [shaped((rows, cols))] * (n_dp - 1), where, keep, got)


def add_all(where, keep, got):
    def body(where_ref, keep_ref, *refs):
        total = keep_ref[...]
        for ref in refs[:-1]:
            total = total + ref[...].astype(F32)
        refs[-1][...] = total.astype(BF16)

    return run(body, [shaped(keep.shape)], where, keep, *got)[0]


def rows_together(where, pieces):
    rows, cols = pieces[0].shape

    def body(where_ref, *refs):
        for m, ref in enumerate(refs[:-1]):
            refs[-1][at(where_ref[m], rows), :] = ref[...].astype(F32)

    return run(body, [shaped((rows * 4, cols), F32)], where, *pieces)[0]


def grad_attend(where, grad_own, grad_got, own_head, own_tail, got_head, got_tail, queries):
    tokens, width = grad_own.shape
    length, width_dev = queries.shape
    half = width_dev // 2

    def body(where_ref, own, got, head, tail, got_head, got_tail, q_ref, rows, back):
        for c, ends in enumerate(((head, tail), (got_head, got_tail))):
            block = jnp.concatenate([ends[0][...], ends[1][...]], axis=0)
            for k, ref in enumerate((own, got)):
                part = dot(ref[...], block, ((1,), (1,))).astype(BF16)
                rows[at(where_ref[HEAD] ^ k, tokens), at((where_ref[0] // 2) ^ c, half)] = part
        for i in range(width_dev // DH):
            cut = slice(i * DH, (i + 1) * DH)
            back[i] = dot(q_ref[:, cut], rows[:, cut], ((0,), (0,))).astype(BF16)

    outs = [shaped((length, width_dev)), shaped((width_dev // DH, DH, DH))]
    return run(body, outs, where, grad_own, grad_got, own_head, own_tail, got_head, got_tail, queries)


def query_grads(where, grad_rows, keys, values, state, att_scale):
    length, width_dev = keys.shape

    def body(where_ref, g_ref, k_ref, v_ref, s_ref, out):
        keep = lower(length)
        for i in range(width_dev // DH):
            cut = slice(i * DH, (i + 1) * DH)
            g = g_ref[:, cut]
            scores = jnp.where(keep, dot(g, v_ref[:, cut], ((1,), (1,))), 0.0).astype(BF16)
            both = jnp.dot(scores, k_ref[:, cut], preferred_element_type=F32)
            both += dot(g, s_ref[i], ((1,), (1,)))
            out[:, cut] = (att_scale * both).astype(BF16)

    return run(body, [shaped((length, width_dev))], where, grad_rows, keys, values, state)[0]


def key_value_parts(where, grad_rows, queries, keys, values):
    length, width_dev = keys.shape

    def body(where_ref, g_ref, q_ref, k_ref, v_ref, dk, dv):
        keep = upper(length)
        for i in range(width_dev // DH):
            cut = slice(i * DH, (i + 1) * DH)
            g, q, k, v = g_ref[:, cut], q_ref[:, cut], k_ref[:, cut], v_ref[:, cut]
            grad_scores = jnp.where(keep, dot(v, g, ((1,), (1,))), 0.0).astype(BF16)
            dk[:, cut] = jnp.dot(grad_scores, q, preferred_element_type=F32)
            scores = jnp.where(keep, dot(k, q, ((1,), (1,))), 0.0).astype(BF16)
            dv[:, cut] = jnp.dot(scores, g, preferred_element_type=F32)

    outs = [shaped((length, width_dev), F32)] * 2
    return run(body, outs, where, grad_rows, queries, keys, values)


def key_value_grads(where, key_part, value_part, keys, values, from_core, from_far, att_scale):
    length, width_dev = keys.shape

    def body(where_ref, kp_ref, vp_ref, k_ref, v_ref, core_ref, far_ref, dk, dv):
        near = 1.0 - (where_ref[0] // 2).astype(F32)
        far = 1.0 - (where_ref[0] % 2).astype(F32)
        for i in range(width_dev // DH):
            cut = slice(i * DH, (i + 1) * DH)
            back = (core_ref[i].astype(F32) * near + far_ref[i].astype(F32) * far).astype(BF16)
            both = kp_ref[:, cut] + dot(v_ref[:, cut], back, ((1,), (1,)))
            dk[:, cut] = (att_scale * both).astype(BF16)
            both = vp_ref[:, cut] + jnp.dot(k_ref[:, cut], back, preferred_element_type=F32)
            dv[:, cut] = (att_scale * both).astype(BF16)

    outs = [shaped((length, width_dev))] * 2
    return run(body, outs, where, key_part, value_part, keys, values, from_core, from_far)


def fits(queries, out_proj, depth_proj, code_table, code_ids):
    n_seq, n_head = lax.axis_size("seq"), lax.axis_size("head")
    return (
        n_seq == 4
        and n_head == 2
        and queries.shape[2] == 4 * DH
        and code_table.shape[0] == 2
        and out_proj.shape[1] % 128 == 0
        and depth_proj.shape[1] % 128 == 0
        and code_table.shape[1] % 128 == 0
        and code_ids.shape[1] % DH == 0
        and code_table.shape[1] * n_head * lax.axis_size("dp") <= 32 * 256
    )


def on_device(queries, keys, values, out_proj, depth_proj, code_table, code_ids, depth_cotangent):
    if not fits(queries, out_proj, depth_proj, code_table, code_ids):
        return on_device_any(
            queries, keys, values, out_proj, depth_proj, code_table, code_ids, depth_cotangent
        )
    n_dp = lax.axis_size("dp")
    me_seq, me_head, me_dp = (lax.axis_index(a) for a in ("seq", "head", "dp"))
    group_len = queries.shape[1]
    width = code_table.shape[2]
    att_scale = float(group_len * lax.axis_size("seq")) ** (-0.5)
    core, far = me_seq % 2, me_seq // 2
    lane = 2 * core + far
    where = jnp.stack([lane, lane ^ 1, lane ^ 2, lane ^ 3, me_head, me_dp, me_seq]).astype(jnp.int32)
    queries, keys, values = queries[0], keys[0], values[0]

    def far_swap(block):
        return swap(block, "seq", 2)

    def core_swap(block):
        return swap(block, "seq", 1)

    def all_lanes(block):
        got = far_swap(block)
        return [block, got, core_swap(block), core_swap(got)]

    t_rows, tokens = code_table.shape[1], code_ids.shape[1]
    half = t_rows * n_dp
    lanes_0 = first_lanes(code_table, depth_proj, n_dp)
    pieces_0 = lax.all_to_all(lanes_0, "dp", 0, 0)
    lanes_1 = second_lanes(code_table, out_proj, lanes_0)
    distances = [n_dp // 2] + [k for k in range(1, n_dp) if k != n_dp // 2]
    pieces_1 = [lanes_1] + [swap(lanes_1, "dp", k) for k in distances]

    top = keys.shape[1]
    keys, values, _ = lax.optimization_barrier((keys, values, lanes_1))
    mine = pack(where, keys, values, code_ids[0].T)
    from_core = core_swap(mine)
    chip = pack_chip(where, mine, from_core, top)
    from_far = far_swap(chip)
    packed = (mine, from_core, from_far)

    attended, state_in = attend(where, queries, keys, values, from_core, from_far, att_scale)

    pieces_0, _ = lax.optimization_barrier((pieces_0, attended))
    fold = depth_proj.shape[0] // 4
    early = fold + fold * 7 // 16
    late = 2 * fold - early
    part_0, depth_part, depth_top = first_parts(where, pieces_0, t_rows, early)
    got_0 = swap(part_0, "head", 1)
    depth_far = far_swap(depth_top)

    pieces_1, depth_far = lax.optimization_barrier((pieces_1, depth_far))
    part_1, out_head, out_tail = second_parts(where, pieces_1, [0, *distances], t_rows)
    got_head, got_tail = core_swap(out_head), core_swap(out_tail)
    got_1 = swap(part_1, "head", 1)

    mixed_part = mix_own(where, attended, out_head, out_tail)
    got_0, got_head, _, _ = lax.optimization_barrier((got_0, got_head, part_1, mixed_part))
    own_0, to_core, to_far = embed(where, packed, top, 0, 2, tokens, part_0, got_0, half, n_dp, late)
    far_0 = far_swap(to_far)

    got_tail, _ = lax.optimization_barrier((got_tail, to_far))
    mixed_send = mix(where, attended, mixed_part, got_head, got_tail, True)
    mixed_got = swap(mixed_send, "head", 1)
    mixed_part, got_1 = lax.optimization_barrier((mixed_part, got_1))
    mixed = mix(where, attended, mixed_part, got_head, got_tail, False)
    core_0 = core_swap(to_core)

    got_1, _, _ = lax.optimization_barrier((got_1, mixed, mixed_send))
    own_1, to_core, to_far = embed(where, packed, top, 1, 2, tokens, part_1, got_1, half, n_dp, 0)
    far_1 = far_swap(to_far)
    depth_core, depth_core_far = core_swap(depth_part), core_swap(depth_far)
    far_0, far_1, mixed_got, depth_core, depth_core_far, core_0 = lax.optimization_barrier(
        (far_0, far_1, mixed_got, depth_core, depth_core_far, core_0)
    )
    core_far_0, core_1, core_far_1 = core_swap(far_0), core_swap(to_core), core_swap(far_1)

    end = 2 * tokens
    folds = [(depth_part, 0), (depth_part, fold), (got_0, half), (got_0, half + fold)]
    folds += [(depth_far, 0), (depth_far, fold), (far_0, end), (far_0, end + fold)]
    folds += [(depth_core, 0), (depth_core, fold), (core_0, tokens), (core_0, tokens + fold)]
    folds += [(depth_core_far, 0), (depth_core_far, fold), (core_far_0, end), (core_far_0, end + fold)]
    rest = [None] * 16
    rest[5], rest[13] = (far_0, end + 2 * fold), (core_far_0, end + 2 * fold)
    first = [(own_0, 0), (far_0, 0), (core_0, 0), (core_far_0, tokens)]
    second = [(own_1, 0), (far_1, 0), (core_1, 0), (core_far_1, tokens)]
    cot = depth_cotangent[0].reshape(tokens, -1)
    grad_mixed = depth_grad(where, folds, rest, late, first, second, mixed, mixed_got, cot)

    grad_got = swap(grad_mixed, "head", 1)
    send, keep = weight_terms(where, attended, grad_mixed, grad_got)
    send, keep = add_core(where, keep, core_swap(send))
    from_far = far_swap(send)
    grad_rows, back = grad_attend(where, grad_mixed, grad_got, out_head, out_tail, got_head, got_tail, queries)
    back, send = lax.optimization_barrier((back, send))
    back_core = core_swap(back)
    back_chip = (back.astype(F32) + back_core.astype(F32)).astype(BF16)
    key_part, value_part = key_value_parts(where, grad_rows, queries, keys, values)
    grad_query = query_grads(where, grad_rows, keys, values, state_in, att_scale)
    from_far, key_part, value_part, grad_query, back_chip = lax.optimization_barrier(
        (from_far, key_part, value_part, grad_query, back_chip)
    )
    keep, *send = add_far(where, keep, from_far, n_dp)
    got = [swap(send[k - 1], "dp", k) for k in reversed(range(1, n_dp))]
    back_chip, keep = lax.optimization_barrier((back_chip, keep))
    back_far = far_swap(back_chip)
    block = add_all(where, keep, got)
    blocks = [block, far_swap(block), core_swap(block), swap(block, "seq", 3)]
    key_part, block = lax.optimization_barrier((key_part, block))
    grad_key, grad_value = key_value_grads(
        where, key_part, value_part, keys, values, back_core, back_far, att_scale
    )
    blocks, grad_key, grad_value = lax.optimization_barrier((blocks, grad_key, grad_value))
    grad_out_proj = rows_together(where, blocks)
    return grad_query[None], grad_key[None], grad_value[None], grad_out_proj


def solution(mesh):
    in_specs = (
        P("dp", "seq", "head"),
        P("dp", "seq", "head"),
        P("dp", "seq", "head"),
        P("head", "dp"),
        P(None, ("head", "dp")),
        P(None, ("head", "dp"), None),
        P("dp", ("seq", "head"), None),
        P("dp", ("seq", "head"), None, None),
    )
    out_specs = (
        P("dp", "seq", "head"),
        P("dp", "seq", "head"),
        P("dp", "seq", "head"),
        P("head", "dp"),
    )
    return jax.shard_map(
        on_device, mesh=mesh, in_specs=in_specs, out_specs=out_specs, check_vma=False
    )
```

```python
import jax
import jax.numpy as jnp
from jax import lax
from jax.experimental import pallas as pl
from jax.experimental.pallas import tpu as pltpu
from jax.sharding import PartitionSpec as P

DH = 128
F32 = jnp.float32
BF16 = jnp.bfloat16


def swap(block, axis, mask):
    return lax.ppermute(block, axis, [(i, i ^ mask) for i in range(lax.axis_size(axis))])


def has_bit(index, bit):
    return lax.bitwise_and(index, jnp.int32(bit)) != 0


def in_order(pieces, index):
    pieces = list(pieces)
    bit = 1
    while bit < len(pieces):
        odd = has_bit(index, bit)
        pieces = [jnp.where(odd, pieces[j ^ bit], pieces[j]) for j in range(len(pieces))]
        bit *= 2
    return pieces


def pick(array, index, dim):
    return lax.dynamic_index_in_dim(array, index, dim, keepdims=False)


def exchange(block, axis):
    return [block] + [swap(block, axis, k) for k in range(1, lax.axis_size(axis))]


def dot(a, b, dims):
    return lax.dot_general(a, b, ((dims[0], dims[1]), ((), ())), preferred_element_type=F32)


def earlier_sum(state, backward):
    n_seq = lax.axis_size("seq")
    me = lax.axis_index("seq")
    before = jnp.zeros_like(state)
    total = state
    bit = 1
    while bit < n_seq:
        got = swap(total.astype(BF16), "seq", bit).astype(F32)
        mine = has_bit(me, bit)
        takes = jnp.logical_not(mine) if backward else mine
        before = before + jnp.where(takes, got, 0.0)
        total = total + got
        bit *= 2
    return before.astype(BF16)


def on_device_any(queries, keys, values, out_proj, depth_proj, code_table, code_ids, depth_cotangent):
    n_seq, n_head, n_dp = (lax.axis_size(a) for a in ("seq", "head", "dp"))
    me_seq, me_head, me_dp = (lax.axis_index(a) for a in ("seq", "head", "dp"))
    group_len, width_dev = queries.shape[1:]
    heads_here = width_dev // DH
    tokens = group_len // n_head
    n_far = n_seq // 2
    me_core = lax.bitwise_and(me_seq, jnp.int32(1))
    me_far = lax.shift_right_logical(me_seq, jnp.int32(1))
    lane = me_core * n_far + me_far
    att_scale = float(group_len * n_seq) ** (-0.5)
    width = code_table.shape[2]
    wide = width // n_seq
    far = [2 * m for m in range(n_far)]

    def far_exchange(block):
        return [block] + [swap(block, "seq", m) for m in far[1:]]

    def seq_lanes(block):
        near = jnp.stack(in_order(far_exchange(block), me_far))
        both = in_order([near, swap(near, "seq", 1)], me_core)
        return jnp.concatenate(both, axis=0)

    ids = code_ids[0].T
    ids_far = jnp.stack(far_exchange(ids))
    ids_rel = jnp.stack([ids_far, swap(ids_far, "seq", 1)])

    table = lax.dynamic_slice_in_dim(code_table, lane * wide, wide, axis=2)
    rows_dev = table.shape[1]
    embedded = []
    row_no = []
    for k_head in range(n_head):
        for k_dp in range(n_dp):
            owner = (me_head ^ k_head) * n_dp + (me_dp ^ k_dp)
            row_no.append(owner * rows_dev + jnp.arange(rows_dev, dtype=jnp.int32))
    row_no = jnp.concatenate(row_no)
    for level in range(table.shape[0]):
        part = jnp.concatenate(exchange(table[level], "dp"), axis=0)
        part = jnp.concatenate(exchange(part, "head"), axis=0)
        level_ids = ids_rel[:, :, level].reshape(-1)
        onehot = (level_ids[:, None] == row_no[None, :]).astype(BF16)
        rel = dot(onehot, part, ((1,), (0,))).astype(BF16).reshape(2, n_far, tokens, wide)
        mine = [rel[:, 0]] + [swap(rel[:, m // 2], "seq", m) for m in far[1:]]
        near = jnp.stack([block[0] for block in mine])
        other = swap(jnp.stack([block[1] for block in mine]), "seq", 1)
        near = jnp.stack(in_order(list(near), me_far))
        other = jnp.stack(in_order(list(other), me_far))
        lanes = jnp.concatenate(in_order([near, other], me_core), axis=0)
        embedded.append(lanes.transpose(1, 0, 2).reshape(tokens, width))

    out_rows = out_proj.shape[0] // n_seq
    out_lane = lax.dynamic_slice_in_dim(out_proj, lane * out_rows, out_rows, axis=0)
    out_part = jnp.concatenate(in_order(exchange(out_lane, "dp"), me_dp), axis=1)
    out_part = jnp.stack(in_order(exchange(out_part, "head"), me_head))
    out_full = seq_lanes(out_part).transpose(1, 0, 2, 3).reshape(n_head * width_dev, width)

    depth_rows = depth_proj.shape[0] // n_seq
    depth_lane = lax.dynamic_slice_in_dim(depth_proj, lane * depth_rows, depth_rows, axis=0)
    depth_part = jnp.concatenate(in_order(exchange(depth_lane, "dp"), me_dp), axis=1)
    depth_part = jnp.concatenate(in_order(exchange(depth_part, "head"), me_head), axis=1)
    proj_mat = seq_lanes(depth_part).reshape(width, width)

    query_rows = queries[0].reshape(group_len, heads_here, DH)
    key_rows = keys[0].reshape(group_len, heads_here, DH)
    value_rows = values[0].reshape(group_len, heads_here, DH)
    places = jnp.arange(group_len, dtype=jnp.int32)
    causal = (places[:, None] >= places[None, :]).astype(F32)
    state_local = jnp.einsum("thd,the->hde", key_rows, value_rows, preferred_element_type=F32)
    state_in = earlier_sum(state_local, False)
    scores = (
        jnp.einsum("thd,shd->hts", query_rows, key_rows, preferred_element_type=F32) * causal
    ).astype(BF16)
    attended = (
        att_scale
        * (
            jnp.einsum("hts,she->the", scores, value_rows, preferred_element_type=F32)
            + jnp.einsum("thd,hde->the", query_rows, state_in, preferred_element_type=F32)
        )
    ).astype(BF16)
    attended = attended.reshape(n_head, tokens, width_dev)
    att_all = [pick(attended, me_head, 0)]
    att_all += [swap(pick(attended, me_head ^ k, 0), "head", k) for k in range(1, n_head)]
    att_all = jnp.concatenate(in_order(att_all, me_head), axis=1)
    mixed = dot(att_all, out_full, ((1,), (0,)))

    cot = depth_cotangent[0]
    n_level = cot.shape[1]
    carried = mixed
    kept = []
    for level in range(n_level):
        summed = carried + embedded[level].astype(F32)
        inv = lax.rsqrt(jnp.mean(summed * summed, axis=-1, keepdims=True) + 1e-05)
        if level < n_level - 1:
            projected = dot((summed * inv).astype(BF16), proj_mat, ((1,), (0,)))
            carried = summed + projected * jax.nn.sigmoid(projected)
        else:
            projected = None
        kept.append((summed, inv, projected))
    grad = None
    for level in reversed(range(n_level)):
        summed, inv, projected = kept[level]
        grad_proj = cot[:, level, :]
        if grad is not None:
            gate = jax.nn.sigmoid(projected)
            slope = gate * (1.0 + projected * (1.0 - gate))
            grad_proj = (grad_proj.astype(F32) + grad * slope).astype(BF16)
        grad_normed = dot(grad_proj, proj_mat, ((1,), (1,)))
        along = jnp.mean(grad_normed * summed, axis=-1, keepdims=True)
        grad_sum = grad_normed * inv - summed * (along * inv * inv * inv)
        grad = grad_sum if grad is None else grad + grad_sum
    grad_mixed = grad.astype(BF16)

    out_heads = out_full.reshape(n_head, width_dev, width)
    grad_rows = []
    for k in range(1, n_head):
        part = dot(grad_mixed, pick(out_heads, me_head ^ k, 0), ((1,), (1,))).astype(BF16)
        grad_rows.append(swap(part, "head", k))
    own_part = dot(grad_mixed, pick(out_heads, me_head, 0), ((1,), (1,))).astype(BF16)
    grad_rows = jnp.concatenate(in_order([own_part] + grad_rows, me_head), axis=0)
    grad_rows = grad_rows.reshape(group_len, heads_here, DH)

    rows = width_dev // n_seq
    att_lanes = att_all.reshape(tokens, n_head, 2, n_far, rows)

    def term(core):
        part = pick(att_lanes, core, 2).reshape(tokens, n_head * n_far * rows)
        return dot(part, grad_mixed, ((0,), (0,)))

    got = swap(term(1 - me_core).astype(BF16), "seq", 1)
    chip = term(me_core) + got.astype(F32)
    chip = chip.reshape(n_head, n_far, rows, width)
    total = pick(pick(chip, me_head, 0), me_far, 0)
    for m in far:
        for k in range(n_head):
            if m or k:
                piece = pick(pick(chip, me_head ^ k, 0), me_far ^ (m // 2), 0).astype(BF16)
                mask = m * n_head + k
                total = total + swap(piece, ("seq", "head"), mask).astype(F32)
    columns = total.reshape(rows, n_dp, width // n_dp)
    block = pick(columns, me_dp, 1)
    for k in range(1, n_dp):
        block = block + swap(pick(columns, me_dp ^ k, 1).astype(BF16), "dp", k).astype(F32)
    grad_out_proj = seq_lanes(block.astype(BF16)).reshape(width_dev, width // n_dp).astype(F32)

    back_local = jnp.einsum("thd,the->hde", query_rows, grad_rows, preferred_element_type=F32)
    back_state = earlier_sum(back_local, True)
    grad_scores = (
        jnp.einsum("the,she->hts", grad_rows, value_rows, preferred_element_type=F32) * causal
    ).astype(BF16)
    grad_query = att_scale * (
        jnp.einsum("hts,shd->thd", grad_scores, key_rows, preferred_element_type=F32)
        + jnp.einsum("the,hde->thd", grad_rows, state_in, preferred_element_type=F32)
    )
    grad_key = att_scale * (
        jnp.einsum("hts,thd->shd", grad_scores, query_rows, preferred_element_type=F32)
        + jnp.einsum("she,hde->shd", value_rows, back_state, preferred_element_type=F32)
    )
    grad_value = att_scale * (
        jnp.einsum("hts,the->she", scores, grad_rows, preferred_element_type=F32)
        + jnp.einsum("shd,hde->she", key_rows, back_state, preferred_element_type=F32)
    )
    out_shape = (1, group_len, width_dev)
    return (
        grad_query.reshape(out_shape).astype(BF16),
        grad_key.reshape(out_shape).astype(BF16),
        grad_value.reshape(out_shape).astype(BF16),
        grad_out_proj,
    )


VMEM_BYTES = 48 * 1024 * 1024


def run(body, outs, where, *args):
    vmem = pl.BlockSpec(memory_space=pltpu.VMEM)
    return pl.pallas_call(
        body,
        out_shape=outs,
        in_specs=[pl.BlockSpec(memory_space=pltpu.SMEM)] + [vmem] * len(args),
        out_specs=[vmem] * len(outs),
        compiler_params=pltpu.CompilerParams(vmem_limit_bytes=VMEM_BYTES),
    )(where, *args)


def shaped(shape, dtype=BF16):
    return jax.ShapeDtypeStruct(shape, dtype)


def at(index, size):
    return pl.ds(pl.multiple_of(index * size, size), size)


HEAD, DP, SEQ = 4, 5, 6


def own_lane():
    me = lax.axis_index("seq")
    return 2 * (me % 2) + me // 2


def copies(body_of, outs, args):
    n_copies = len(body_of(None))

    def body(*refs):
        sems = refs[-1]
        going = [pltpu.make_async_copy(src, dst, sems.at[i]) for i, (src, dst) in enumerate(body_of(refs[:-1]))]
        for copy in going:
            copy.start()
        for copy in going:
            copy.wait()

    anywhere = pl.BlockSpec(memory_space=pl.ANY)
    return pl.pallas_call(
        body,
        out_shape=outs,
        in_specs=[anywhere] * len(args),
        out_specs=pl.BlockSpec(memory_space=pltpu.VMEM),
        scratch_shapes=[pltpu.SemaphoreType.DMA((n_copies,))],
    )(*args)


def first_lanes(code_table, depth_proj, n_dp):
    t_rows, t_cols = code_table.shape[1], code_table.shape[2] // 4
    d_half, d_cols = depth_proj.shape[0] // 8, depth_proj.shape[1]

    def body(table, depth, lanes, sems):
        moves = [(table.at[0, :, at(own_lane(), t_cols)], lanes.at[0, 0:t_rows])]
        for half in range(2):
            cols = slice(half * d_cols, (half + 1) * d_cols)
            moves.append((depth.at[at(2 * own_lane() + half, d_half)], lanes.at[0, t_rows:t_rows + d_half, cols]))
        going = [pltpu.make_async_copy(src, dst, sems.at[i]) for i, (src, dst) in enumerate(moves)]
        for copy in going:
            copy.start()
        for copy in going:
            copy.wait()
        for k in range(1, n_dp):
            lanes[k] = lanes[0]

    return pl.pallas_call(
        body,
        out_shape=shaped((n_dp, t_rows + d_half, t_cols)),
        in_specs=[pl.BlockSpec(memory_space=pl.ANY)] * 2,
        out_specs=pl.BlockSpec(memory_space=pltpu.VMEM),
        scratch_shapes=[pltpu.SemaphoreType.DMA((3,))],
    )(code_table, depth_proj)


def second_lanes(code_table, out_proj, after):
    t_rows, t_cols = code_table.shape[1], code_table.shape[2] // 4
    rows, cols = out_proj.shape[0] // 2, out_proj.shape[1]

    def views(refs):
        if refs is None:
            return [0, 1]
        table, out, _, lanes = refs
        return [
            (table.at[1, :, at(own_lane(), t_cols)], lanes.at[0:t_rows]),
            (out.at[at(own_lane() // 2, rows)], lanes.at[t_rows:t_rows + rows]),
        ]

    return copies(views, shaped((t_rows + rows, cols)), [code_table, out_proj, after])


def first_parts(where, pieces, t_rows, early):
    n, d_half, t_cols = pieces.shape
    d_half, d_cols = d_half - t_rows, t_cols // 2
    top, fold = n * t_rows, 2 * d_half

    def body(where_ref, ref, both, depth, top_fold):
        for k in range(n):
            both[k * t_rows:(k + 1) * t_rows, :] = ref[where_ref[DP] ^ k, :t_rows]
            place = where_ref[DP] ^ k
            cols = at(place % 2, d_cols)
            for half in range(2):
                part = ref[place, t_rows:, half * d_cols:(half + 1) * d_cols]
                row = pl.multiple_of((place // 2) * fold + half * d_half, d_half)
                both[pl.ds(pl.multiple_of(top + row, d_half), d_half), cols] = part
                depth[pl.ds(row, d_half), cols] = part
        top_fold[...] = depth[:early]

    rows = fold * n // 2
    return run(body, [shaped((top + rows, t_cols)), shaped((rows, t_cols)), shaped((early, t_cols))], where, pieces)


def second_parts(where, pieces, distances, t_rows):
    rows, cols = pieces[0].shape[0] - t_rows, pieces[0].shape[1]
    n = len(pieces)
    first = rows * 5 // 8

    def body(where_ref, *refs):
        table, head, tail = refs[n:]
        for k, ref in zip(distances, refs):
            cut = at(where_ref[DP] ^ k, cols)
            table[k * t_rows:(k + 1) * t_rows, :] = ref[:t_rows]
            head[:, cut] = ref[t_rows:t_rows + first]
            tail[:, cut] = ref[t_rows + first:]

    outs = [shaped((n * t_rows, cols)), shaped((first, n * cols)), shaped((rows - first, n * cols))]
    return run(body, outs, where, *pieces)


def embed(where, packed, top, level, n_level, tokens, own, got, half, n_dp, late):
    folds = tokens // DH
    n_rows = id_rows(n_level, tokens)
    rows, cols = own.shape
    rows_dev, extra = half // n_dp, rows - half

    def body(where_ref, mine_ref, core_ref, far_ref, own_ref, got_ref, *outs):
        def ids_of(ref, start):
            all_ids = ref[start:start + 2 * n_level * folds].astype(F32)
            mine = level * folds
            high = all_ids[mine:mine + folds]
            low = all_ids[(n_level * folds) + mine:(n_level * folds) + mine + folds]
            ids = high * 32.0 + low
            return jnp.concatenate([ids[f:f + 1] for f in range(folds)], axis=1)

        place = lax.broadcasted_iota(jnp.int32, (tokens, half), 1)
        owner = jnp.bitwise_xor(place // rows_dev, where_ref[DP])
        base = owner * rows_dev + place % rows_dev
        rows_of = [(mine_ref, top), (core_ref, top), (far_ref, top), (far_ref, top + n_rows)]
        columns = jnp.concatenate([ids_of(*r) for r in rows_of], axis=0).T.astype(jnp.int32)
        for m in (2, 3, 1, 0):
            col = columns[:, m:m + 1]
            total = None
            for k, ref in enumerate((own_ref, got_ref)):
                start = (where_ref[HEAD] ^ k) * half
                hot = (base == col - start).astype(F32).astype(BF16)
                part = jnp.dot(hot, ref[:half], preferred_element_type=F32)
                total = part if total is None else total + part
            total = total.astype(BF16)
            if m < 2:
                outs[m][:tokens] = total
            else:
                outs[2][(m - 2) * tokens:(m - 1) * tokens, :] = total
        if extra:
            outs[1][tokens:] = got_ref[half:]
            outs[2][2 * tokens:2 * tokens + extra] = got_ref[half:]
            outs[2][2 * tokens + extra:] = own_ref[rows - late:]

    outs = [shaped((tokens, cols)), shaped((tokens + extra, cols)), shaped((2 * tokens + extra + late, cols))]
    return run(body, outs, where, *packed, own, got)


def depth_grad(where, folds, rest, late, first, second, mixed, mixed_got, cot):
    arrays, which = [], []
    for array, _ in folds + first + second:
        found = [i for i, other in enumerate(arrays) if other is array]
        if not found:
            arrays.append(array)
        which.append(found[0] if found else len(arrays) - 1)
    starts = [start for _, start in folds + first + second]
    tokens, width = mixed.shape
    cols = width // 4
    chunk = 32

    def body(where_ref, *refs):
        parts = refs[:len(arrays)]
        mixed_ref, got_ref, cot_ref, out, full, sum_ref, mid_ref, last_ref, row_ref = refs[len(arrays):]
        for n in range(16):
            m, x, j = n // 4, n // 2 % 2, n % 2
            place = (where_ref[HEAD] ^ x) * 2 + j
            if rest[n] is None:
                full[at(where_ref[m], cols), at(place, cols)] = parts[which[n]][starts[n]:starts[n] + cols]
            else:
                main = pl.ds(pl.multiple_of(where_ref[m] * cols, cols), cols - late)
                tail = pl.ds(pl.multiple_of(where_ref[m] * cols + cols - late, 16), late)
                array = next(i for i, other in enumerate(arrays) if other is rest[n][0])
                full[main, at(place, cols)] = parts[which[n]][starts[n]:starts[n] + cols - late]
                full[tail, at(place, cols)] = parts[array][rest[n][1]:rest[n][1] + late]

        def rows_of(i):
            return pl.ds(pl.multiple_of(i * chunk, chunk), chunk)

        def lane_rows(i, n):
            return parts[which[n]][pl.ds(pl.multiple_of(starts[n] + i * chunk, chunk), chunk), :].astype(F32)

        def inverse(total):
            return lax.rsqrt(jnp.mean(total * total, axis=-1, keepdims=True) + 1e-05)

        def enter(i, carry):
            rows = rows_of(i)
            for m in range(4):
                cut = at(where_ref[m], cols)
                sum_ref[rows, cut] = mixed_ref[rows, cut] + got_ref[rows, cut].astype(F32) + lane_rows(i, 16 + m)
            total = sum_ref[rows, :]
            row_ref[rows, :] = (total * inverse(total)).astype(BF16)
            return carry

        lax.fori_loop(0, tokens // chunk, enter, 0, unroll=True)
        mid_ref[...] = jnp.dot(row_ref[...], full[...], preferred_element_type=F32)
        last_ref[...] = dot(cot_ref[:, width:], full[...], ((1,), (1,)))

        def middle(i, carry):
            rows = rows_of(i)
            projected = mid_ref[rows, :]
            gate = jax.nn.sigmoid(projected)
            mid_ref[rows, :] = sum_ref[rows, :] + projected * gate
            for m in range(4):
                cut = at(where_ref[m], cols)
                mid_ref[rows, cut] += lane_rows(i, 20 + m)
            total = mid_ref[rows, :]
            inv = inverse(total)
            grad = last_ref[rows, :]
            along = jnp.mean(grad * total, axis=-1, keepdims=True)
            grad = grad * inv - total * (along * inv * inv * inv)
            last_ref[rows, :] = grad
            slope = gate * (1.0 + projected * (1.0 - gate))
            row_ref[rows, :] = (cot_ref[rows, :width].astype(F32) + grad * slope).astype(BF16)
            return carry

        lax.fori_loop(0, tokens // chunk, middle, 0, unroll=True)
        mid_ref[...] = dot(row_ref[...], full[...], ((1,), (1,)))

        def leave(i, carry):
            rows = rows_of(i)
            total = sum_ref[rows, :]
            inv = inverse(total)
            grad = mid_ref[rows, :]
            along = jnp.mean(grad * total, axis=-1, keepdims=True)
            grad = last_ref[rows, :] + grad * inv - total * (along * inv * inv * inv)
            out[rows, :] = grad.astype(BF16)
            return carry

        lax.fori_loop(0, tokens // chunk, leave, 0, unroll=True)

    vmem = pl.BlockSpec(memory_space=pltpu.VMEM)
    return pl.pallas_call(
        body,
        out_shape=shaped((tokens, width)),
        in_specs=[pl.BlockSpec(memory_space=pltpu.SMEM)] + [vmem] * (len(arrays) + 3),
        out_specs=vmem,
        scratch_shapes=[
            pltpu.VMEM((width, width), BF16),
            pltpu.VMEM((tokens, width), F32),
            pltpu.VMEM((tokens, width), F32),
            pltpu.VMEM((tokens, width), F32),
            pltpu.VMEM((tokens, width), BF16),
        ],
        compiler_params=pltpu.CompilerParams(vmem_limit_bytes=VMEM_BYTES),
    )(where, *arrays, mixed, mixed_got, cot)


def id_rows(n_level, tokens):
    return -(-2 * n_level * (tokens // DH) // 16) * 16


def pack(where, keys, values, ids):
    heads = keys.shape[1] // DH
    n_level, tokens = ids.shape
    folds = tokens // DH
    top = heads * DH

    def body(where_ref, k_ref, v_ref, ids_ref, out):
        parts = []
        for level in range(n_level):
            for fold in range(folds):
                parts.append(ids_ref[level:level + 1, fold * DH:(fold + 1) * DH])
        whole = jnp.concatenate(parts, axis=0)
        both = jnp.concatenate([whole // 32, whole % 32], axis=0).astype(F32).astype(BF16)
        out[top:top + 2 * n_level * folds] = both
        for i in range(heads):
            cut = slice(i * DH, (i + 1) * DH)
            out[cut] = dot(k_ref[:, cut], v_ref[:, cut], ((0,), (0,))).astype(BF16)

    return run(body, [shaped((top + id_rows(n_level, tokens), DH))], where, keys, values, ids)[0]


def pack_chip(where, own, core, top):
    rows = own.shape[0] - top

    def body(where_ref, own_ref, core_ref, out):
        out[:top] = (own_ref[:top].astype(F32) + core_ref[:top].astype(F32)).astype(BF16)
        out[top:top + rows] = own_ref[top:]
        out[top + rows:] = core_ref[top:]

    return run(body, [shaped((top + 2 * rows, DH))], where, own, core)[0]


def lower(size):
    rows = lax.broadcasted_iota(jnp.int32, (size, size), 0)
    cols = lax.broadcasted_iota(jnp.int32, (size, size), 1)
    return rows >= cols


def upper(size):
    rows = lax.broadcasted_iota(jnp.int32, (size, size), 0)
    cols = lax.broadcasted_iota(jnp.int32, (size, size), 1)
    return rows <= cols


def attend(where, queries, keys, values, from_core, from_far, att_scale):
    length, width_dev = queries.shape
    heads = width_dev // DH

    def body(where_ref, q_ref, k_ref, v_ref, core_ref, far_ref, att, state):
        near = (where_ref[0] // 2).astype(F32)
        far = (where_ref[0] % 2).astype(F32)
        keep = lower(length)
        for i in range(heads):
            cut = slice(i * DH, (i + 1) * DH)
            state[i] = (core_ref[cut].astype(F32) * near + far_ref[cut].astype(F32) * far).astype(BF16)
            q = q_ref[:, cut]
            scores = jnp.where(keep, dot(q, k_ref[:, cut], ((1,), (1,))), 0.0).astype(BF16)
            both = jnp.dot(scores, v_ref[:, cut], preferred_element_type=F32)
            both += jnp.dot(q, state[i], preferred_element_type=F32)
            att[:, cut] = (att_scale * both).astype(BF16)

    return run(
        body, [shaped((length, width_dev)), shaped((heads, DH, DH))], where, queries, keys, values, from_core, from_far
    )


def mix_own(where, attended, head, tail):
    length = attended.shape[0] // 2
    half, width = head.shape[0] + tail.shape[0], head.shape[1]

    def body(where_ref, att, head_ref, tail_ref, out):
        core = where_ref[0] // 2
        own = jnp.concatenate([head_ref[...], tail_ref[...]], axis=0)
        for k in range(2):
            rows = at(where_ref[HEAD] ^ (1 - k), length)
            out[k] = jnp.dot(att[rows, at(core, half)], own, preferred_element_type=F32)

    return run(body, [shaped((2, length, width), F32)], where, attended, head, tail)[0]


def mix(where, attended, part, got_head, got_tail, other):
    length = attended.shape[0] // 2
    width = part.shape[2]
    half = got_head.shape[0] + got_tail.shape[0]
    dtype = BF16 if other else F32

    def body(where_ref, att, part_ref, head, tail, out):
        rows = at(where_ref[HEAD] ^ (1 if other else 0), length)
        core = where_ref[0] // 2
        got = jnp.concatenate([head[...], tail[...]], axis=0)
        total = part_ref[0 if other else 1]
        total += jnp.dot(att[rows, at(1 - core, half)], got, preferred_element_type=F32)
        out[...] = total.astype(dtype)

    return run(body, [shaped((length, width), dtype)], where, attended, part, got_head, got_tail)[0]


def weight_own(where, attended, grad_own):
    tokens, width = grad_own.shape

    def body(where_ref, att, own, out):
        for m in range(4):
            out[m] = dot(att[at(where_ref[HEAD], tokens), at(where_ref[m], DH)], own[...], ((0,), (0,)))

    return run(body, [shaped((4, DH, width), F32)], where, attended, grad_own)[0]


def weight_terms(where, attended, part, grad_got):
    tokens, width = grad_got.shape

    def body(where_ref, att, part_ref, got, send, keep):
        def term(m):
            a = att[at(1 - where_ref[HEAD], tokens), at(where_ref[m], DH)]
            return part_ref[m] + dot(a, got[...], ((0,), (0,)))

        send[0] = term(2).astype(BF16)
        send[1] = term(3).astype(BF16)
        keep[0] = term(0)
        keep[1] = term(1)

    return run(
        body, [shaped((2, DH, width)), shaped((2, DH, width), F32)], where, attended, part, grad_got
    )


def add_core(where, keep, got):
    shape = keep.shape[1:]

    def body(where_ref, keep_ref, got_ref, send, rest):
        rest[...] = keep_ref[0] + got_ref[0].astype(F32)
        send[...] = (keep_ref[1] + got_ref[1].astype(F32)).astype(BF16)

    return run(body, [shaped(shape), shaped(shape, F32)], where, keep, got)


def add_far(where, keep, got, n_dp):
    rows, width = keep.shape
    cols = width // n_dp

    def body(where_ref, keep_ref, got_ref, rest, *send):
        for k in range(n_dp):
            cut = at(where_ref[DP] ^ k, cols)
            total = keep_ref[:, cut] + got_ref[:, cut].astype(F32)
            if k:
                send[k - 1][...] = total.astype(BF16)
            else:
                rest[...] = total

    return run(body, [shaped((rows, cols), F32)] + [shaped((rows, cols))] * (n_dp - 1), where, keep, got)


def add_all(where, keep, got):
    def body(where_ref, keep_ref, *refs):
        total = keep_ref[...]
        for ref in refs[:-1]:
            total = total + ref[...].astype(F32)
        refs[-1][...] = total.astype(BF16)

    return run(body, [shaped(keep.shape)], where, keep, *got)[0]


def rows_together(where, pieces):
    rows, cols = pieces[0].shape

    def body(where_ref, *refs):
        for m, ref in enumerate(refs[:-1]):
            refs[-1][at(where_ref[m], rows), :] = ref[...].astype(F32)

    return run(body, [shaped((rows * 4, cols), F32)], where, *pieces)[0]


def grad_attend(where, grad_own, grad_got, own_head, own_tail, got_head, got_tail, queries):
    tokens, width = grad_own.shape
    length, width_dev = queries.shape
    half = width_dev // 2

    def body(where_ref, own, got, head, tail, got_head, got_tail, q_ref, rows, back):
        for c, ends in enumerate(((head, tail), (got_head, got_tail))):
            block = jnp.concatenate([ends[0][...], ends[1][...]], axis=0)
            for k, ref in enumerate((own, got)):
                part = dot(ref[...], block, ((1,), (1,))).astype(BF16)
                rows[at(where_ref[HEAD] ^ k, tokens), at((where_ref[0] // 2) ^ c, half)] = part
        for i in range(width_dev // DH):
            cut = slice(i * DH, (i + 1) * DH)
            back[i] = dot(q_ref[:, cut], rows[:, cut], ((0,), (0,))).astype(BF16)

    outs = [shaped((length, width_dev)), shaped((width_dev // DH, DH, DH))]
    return run(body, outs, where, grad_own, grad_got, own_head, own_tail, got_head, got_tail, queries)


def query_grads(where, grad_rows, keys, values, state, att_scale):
    length, width_dev = keys.shape

    def body(where_ref, g_ref, k_ref, v_ref, s_ref, out):
        keep = lower(length)
        for i in range(width_dev // DH):
            cut = slice(i * DH, (i + 1) * DH)
            g = g_ref[:, cut]
            scores = jnp.where(keep, dot(g, v_ref[:, cut], ((1,), (1,))), 0.0).astype(BF16)
            both = jnp.dot(scores, k_ref[:, cut], preferred_element_type=F32)
            both += dot(g, s_ref[i], ((1,), (1,)))
            out[:, cut] = (att_scale * both).astype(BF16)

    return run(body, [shaped((length, width_dev))], where, grad_rows, keys, values, state)[0]


def key_value_parts(where, grad_rows, queries, keys, values):
    length, width_dev = keys.shape

    def body(where_ref, g_ref, q_ref, k_ref, v_ref, dk, dv):
        keep = upper(length)
        for i in range(width_dev // DH):
            cut = slice(i * DH, (i + 1) * DH)
            g, q, k, v = g_ref[:, cut], q_ref[:, cut], k_ref[:, cut], v_ref[:, cut]
            grad_scores = jnp.where(keep, dot(v, g, ((1,), (1,))), 0.0).astype(BF16)
            dk[:, cut] = jnp.dot(grad_scores, q, preferred_element_type=F32)
            scores = jnp.where(keep, dot(k, q, ((1,), (1,))), 0.0).astype(BF16)
            dv[:, cut] = jnp.dot(scores, g, preferred_element_type=F32)

    outs = [shaped((length, width_dev), F32)] * 2
    return run(body, outs, where, grad_rows, queries, keys, values)


def key_value_grads(where, key_part, value_part, keys, values, from_core, from_far, att_scale):
    length, width_dev = keys.shape

    def body(where_ref, kp_ref, vp_ref, k_ref, v_ref, core_ref, far_ref, dk, dv):
        near = 1.0 - (where_ref[0] // 2).astype(F32)
        far = 1.0 - (where_ref[0] % 2).astype(F32)
        for i in range(width_dev // DH):
            cut = slice(i * DH, (i + 1) * DH)
            back = (core_ref[i].astype(F32) * near + far_ref[i].astype(F32) * far).astype(BF16)
            both = kp_ref[:, cut] + dot(v_ref[:, cut], back, ((1,), (1,)))
            dk[:, cut] = (att_scale * both).astype(BF16)
            both = vp_ref[:, cut] + jnp.dot(k_ref[:, cut], back, preferred_element_type=F32)
            dv[:, cut] = (att_scale * both).astype(BF16)

    outs = [shaped((length, width_dev))] * 2
    return run(body, outs, where, key_part, value_part, keys, values, from_core, from_far)


def fits(queries, out_proj, depth_proj, code_table, code_ids):
    n_seq, n_head = lax.axis_size("seq"), lax.axis_size("head")
    return (
        n_seq == 4
        and n_head == 2
        and queries.shape[2] == 4 * DH
        and code_table.shape[0] == 2
        and out_proj.shape[1] % 128 == 0
        and depth_proj.shape[1] % 128 == 0
        and code_table.shape[1] % 128 == 0
        and code_ids.shape[1] % DH == 0
        and code_table.shape[1] * n_head * lax.axis_size("dp") <= 32 * 256
    )


def on_device(queries, keys, values, out_proj, depth_proj, code_table, code_ids, depth_cotangent):
    if not fits(queries, out_proj, depth_proj, code_table, code_ids):
        return on_device_any(
            queries, keys, values, out_proj, depth_proj, code_table, code_ids, depth_cotangent
        )
    n_dp = lax.axis_size("dp")
    me_seq, me_head, me_dp = (lax.axis_index(a) for a in ("seq", "head", "dp"))
    group_len = queries.shape[1]
    width = code_table.shape[2]
    att_scale = float(group_len * lax.axis_size("seq")) ** (-0.5)
    core, far = me_seq % 2, me_seq // 2
    lane = 2 * core + far
    where = jnp.stack([lane, lane ^ 1, lane ^ 2, lane ^ 3, me_head, me_dp, me_seq]).astype(jnp.int32)
    queries, keys, values = queries[0], keys[0], values[0]

    def far_swap(block):
        return swap(block, "seq", 2)

    def core_swap(block):
        return swap(block, "seq", 1)

    def all_lanes(block):
        got = far_swap(block)
        return [block, got, core_swap(block), core_swap(got)]

    t_rows, tokens = code_table.shape[1], code_ids.shape[1]
    half = t_rows * n_dp
    lanes_0 = first_lanes(code_table, depth_proj, n_dp)
    pieces_0 = lax.all_to_all(lanes_0, "dp", 0, 0)
    lanes_1 = second_lanes(code_table, out_proj, lanes_0)
    distances = [n_dp // 2] + [k for k in range(1, n_dp) if k != n_dp // 2]
    pieces_1 = [lanes_1] + [swap(lanes_1, "dp", k) for k in distances]

    top = keys.shape[1]
    keys, values, _ = lax.optimization_barrier((keys, values, lanes_1))
    mine = pack(where, keys, values, code_ids[0].T)
    from_core = core_swap(mine)
    chip = pack_chip(where, mine, from_core, top)
    from_far = far_swap(chip)
    packed = (mine, from_core, from_far)

    attended, state_in = attend(where, queries, keys, values, from_core, from_far, att_scale)

    pieces_0, _ = lax.optimization_barrier((pieces_0, attended))
    fold = depth_proj.shape[0] // 4
    early = fold + fold * 7 // 16
    late = 2 * fold - early
    part_0, depth_part, depth_top = first_parts(where, pieces_0, t_rows, early)
    got_0 = swap(part_0, "head", 1)
    depth_far = far_swap(depth_top)

    pieces_1, depth_far = lax.optimization_barrier((pieces_1, depth_far))
    part_1, out_head, out_tail = second_parts(where, pieces_1, [0, *distances], t_rows)
    got_head, got_tail = core_swap(out_head), core_swap(out_tail)
    got_1 = swap(part_1, "head", 1)

    mixed_part = mix_own(where, attended, out_head, out_tail)
    got_0, got_head, _, _ = lax.optimization_barrier((got_0, got_head, part_1, mixed_part))
    own_0, to_core, to_far = embed(where, packed, top, 0, 2, tokens, part_0, got_0, half, n_dp, late)
    far_0 = far_swap(to_far)

    got_tail, _ = lax.optimization_barrier((got_tail, to_far))
    mixed_send = mix(where, attended, mixed_part, got_head, got_tail, True)
    mixed_got = swap(mixed_send, "head", 1)
    mixed_part, got_1 = lax.optimization_barrier((mixed_part, got_1))
    mixed = mix(where, attended, mixed_part, got_head, got_tail, False)
    core_0 = core_swap(to_core)

    got_1, _, _ = lax.optimization_barrier((got_1, mixed, mixed_send))
    own_1, to_core, to_far = embed(where, packed, top, 1, 2, tokens, part_1, got_1, half, n_dp, 0)
    far_1 = far_swap(to_far)
    depth_core, depth_core_far = core_swap(depth_part), core_swap(depth_far)
    far_0, far_1, mixed_got, depth_core, depth_core_far, core_0 = lax.optimization_barrier(
        (far_0, far_1, mixed_got, depth_core, depth_core_far, core_0)
    )
    core_far_0, core_1, core_far_1 = core_swap(far_0), core_swap(to_core), core_swap(far_1)

    end = 2 * tokens
    folds = [(depth_part, 0), (depth_part, fold), (got_0, half), (got_0, half + fold)]
    folds += [(depth_far, 0), (depth_far, fold), (far_0, end), (far_0, end + fold)]
    folds += [(depth_core, 0), (depth_core, fold), (core_0, tokens), (core_0, tokens + fold)]
    folds += [(depth_core_far, 0), (depth_core_far, fold), (core_far_0, end), (core_far_0, end + fold)]
    rest = [None] * 16
    rest[5], rest[13] = (far_0, end + 2 * fold), (core_far_0, end + 2 * fold)
    first = [(own_0, 0), (far_0, 0), (core_0, 0), (core_far_0, tokens)]
    second = [(own_1, 0), (far_1, 0), (core_1, 0), (core_far_1, tokens)]
    cot = depth_cotangent[0].reshape(tokens, -1)
    grad_mixed = depth_grad(where, folds, rest, late, first, second, mixed, mixed_got, cot)

    grad_got = swap(grad_mixed, "head", 1)
    part = weight_own(where, attended, grad_mixed)
    send, keep = weight_terms(where, attended, part, grad_got)
    send, keep = add_core(where, keep, core_swap(send))
    from_far = far_swap(send)
    grad_rows, back = grad_attend(where, grad_mixed, grad_got, out_head, out_tail, got_head, got_tail, queries)
    back, send = lax.optimization_barrier((back, send))
    back_core = core_swap(back)
    back_chip = (back.astype(F32) + back_core.astype(F32)).astype(BF16)
    key_part, value_part = key_value_parts(where, grad_rows, queries, keys, values)
    grad_query = query_grads(where, grad_rows, keys, values, state_in, att_scale)
    from_far, key_part, value_part, grad_query, back_chip = lax.optimization_barrier(
        (from_far, key_part, value_part, grad_query, back_chip)
    )
    keep, *send = add_far(where, keep, from_far, n_dp)
    got = [swap(send[k - 1], "dp", k) for k in reversed(range(1, n_dp))]
    back_chip, keep = lax.optimization_barrier((back_chip, keep))
    back_far = far_swap(back_chip)
    block = add_all(where, keep, got)
    blocks = [block, far_swap(block), core_swap(block), swap(block, "seq", 3)]
    key_part, block = lax.optimization_barrier((key_part, block))
    grad_key, grad_value = key_value_grads(
        where, key_part, value_part, keys, values, back_core, back_far, att_scale
    )
    blocks, grad_key, grad_value = lax.optimization_barrier((blocks, grad_key, grad_value))
    grad_out_proj = rows_together(where, blocks)
    return grad_query[None], grad_key[None], grad_value[None], grad_out_proj


def solution(mesh):
    in_specs = (
        P("dp", "seq", "head"),
        P("dp", "seq", "head"),
        P("dp", "seq", "head"),
        P("head", "dp"),
        P(None, ("head", "dp")),
        P(None, ("head", "dp"), None),
        P("dp", ("seq", "head"), None),
        P("dp", ("seq", "head"), None, None),
    )
    out_specs = (
        P("dp", "seq", "head"),
        P("dp", "seq", "head"),
        P("dp", "seq", "head"),
        P("head", "dp"),
    )
    return jax.shard_map(
        on_device, mesh=mesh, in_specs=in_specs, out_specs=out_specs, check_vma=False
    )
```

```python
import jax
import jax.numpy as jnp
from jax import lax
from jax.experimental import pallas as pl
from jax.experimental.pallas import tpu as pltpu
from jax.sharding import PartitionSpec as P

DH = 128
F32 = jnp.float32
BF16 = jnp.bfloat16


def swap(block, axis, mask):
    return lax.ppermute(block, axis, [(i, i ^ mask) for i in range(lax.axis_size(axis))])


def has_bit(index, bit):
    return lax.bitwise_and(index, jnp.int32(bit)) != 0


def in_order(pieces, index):
    pieces = list(pieces)
    bit = 1
    while bit < len(pieces):
        odd = has_bit(index, bit)
        pieces = [jnp.where(odd, pieces[j ^ bit], pieces[j]) for j in range(len(pieces))]
        bit *= 2
    return pieces


def pick(array, index, dim):
    return lax.dynamic_index_in_dim(array, index, dim, keepdims=False)


def exchange(block, axis):
    return [block] + [swap(block, axis, k) for k in range(1, lax.axis_size(axis))]


def dot(a, b, dims):
    return lax.dot_general(a, b, ((dims[0], dims[1]), ((), ())), preferred_element_type=F32)


def earlier_sum(state, backward):
    n_seq = lax.axis_size("seq")
    me = lax.axis_index("seq")
    before = jnp.zeros_like(state)
    total = state
    bit = 1
    while bit < n_seq:
        got = swap(total.astype(BF16), "seq", bit).astype(F32)
        mine = has_bit(me, bit)
        takes = jnp.logical_not(mine) if backward else mine
        before = before + jnp.where(takes, got, 0.0)
        total = total + got
        bit *= 2
    return before.astype(BF16)


def on_device_any(queries, keys, values, out_proj, depth_proj, code_table, code_ids, depth_cotangent):
    n_seq, n_head, n_dp = (lax.axis_size(a) for a in ("seq", "head", "dp"))
    me_seq, me_head, me_dp = (lax.axis_index(a) for a in ("seq", "head", "dp"))
    group_len, width_dev = queries.shape[1:]
    heads_here = width_dev // DH
    tokens = group_len // n_head
    n_far = n_seq // 2
    me_core = lax.bitwise_and(me_seq, jnp.int32(1))
    me_far = lax.shift_right_logical(me_seq, jnp.int32(1))
    lane = me_core * n_far + me_far
    att_scale = float(group_len * n_seq) ** (-0.5)
    width = code_table.shape[2]
    wide = width // n_seq
    far = [2 * m for m in range(n_far)]

    def far_exchange(block):
        return [block] + [swap(block, "seq", m) for m in far[1:]]

    def seq_lanes(block):
        near = jnp.stack(in_order(far_exchange(block), me_far))
        both = in_order([near, swap(near, "seq", 1)], me_core)
        return jnp.concatenate(both, axis=0)

    ids = code_ids[0].T
    ids_far = jnp.stack(far_exchange(ids))
    ids_rel = jnp.stack([ids_far, swap(ids_far, "seq", 1)])

    table = lax.dynamic_slice_in_dim(code_table, lane * wide, wide, axis=2)
    rows_dev = table.shape[1]
    embedded = []
    row_no = []
    for k_head in range(n_head):
        for k_dp in range(n_dp):
            owner = (me_head ^ k_head) * n_dp + (me_dp ^ k_dp)
            row_no.append(owner * rows_dev + jnp.arange(rows_dev, dtype=jnp.int32))
    row_no = jnp.concatenate(row_no)
    for level in range(table.shape[0]):
        part = jnp.concatenate(exchange(table[level], "dp"), axis=0)
        part = jnp.concatenate(exchange(part, "head"), axis=0)
        level_ids = ids_rel[:, :, level].reshape(-1)
        onehot = (level_ids[:, None] == row_no[None, :]).astype(BF16)
        rel = dot(onehot, part, ((1,), (0,))).astype(BF16).reshape(2, n_far, tokens, wide)
        mine = [rel[:, 0]] + [swap(rel[:, m // 2], "seq", m) for m in far[1:]]
        near = jnp.stack([block[0] for block in mine])
        other = swap(jnp.stack([block[1] for block in mine]), "seq", 1)
        near = jnp.stack(in_order(list(near), me_far))
        other = jnp.stack(in_order(list(other), me_far))
        lanes = jnp.concatenate(in_order([near, other], me_core), axis=0)
        embedded.append(lanes.transpose(1, 0, 2).reshape(tokens, width))

    out_rows = out_proj.shape[0] // n_seq
    out_lane = lax.dynamic_slice_in_dim(out_proj, lane * out_rows, out_rows, axis=0)
    out_part = jnp.concatenate(in_order(exchange(out_lane, "dp"), me_dp), axis=1)
    out_part = jnp.stack(in_order(exchange(out_part, "head"), me_head))
    out_full = seq_lanes(out_part).transpose(1, 0, 2, 3).reshape(n_head * width_dev, width)

    depth_rows = depth_proj.shape[0] // n_seq
    depth_lane = lax.dynamic_slice_in_dim(depth_proj, lane * depth_rows, depth_rows, axis=0)
    depth_part = jnp.concatenate(in_order(exchange(depth_lane, "dp"), me_dp), axis=1)
    depth_part = jnp.concatenate(in_order(exchange(depth_part, "head"), me_head), axis=1)
    proj_mat = seq_lanes(depth_part).reshape(width, width)

    query_rows = queries[0].reshape(group_len, heads_here, DH)
    key_rows = keys[0].reshape(group_len, heads_here, DH)
    value_rows = values[0].reshape(group_len, heads_here, DH)
    places = jnp.arange(group_len, dtype=jnp.int32)
    causal = (places[:, None] >= places[None, :]).astype(F32)
    state_local = jnp.einsum("thd,the->hde", key_rows, value_rows, preferred_element_type=F32)
    state_in = earlier_sum(state_local, False)
    scores = (
        jnp.einsum("thd,shd->hts", query_rows, key_rows, preferred_element_type=F32) * causal
    ).astype(BF16)
    attended = (
        att_scale
        * (
            jnp.einsum("hts,she->the", scores, value_rows, preferred_element_type=F32)
            + jnp.einsum("thd,hde->the", query_rows, state_in, preferred_element_type=F32)
        )
    ).astype(BF16)
    attended = attended.reshape(n_head, tokens, width_dev)
    att_all = [pick(attended, me_head, 0)]
    att_all += [swap(pick(attended, me_head ^ k, 0), "head", k) for k in range(1, n_head)]
    att_all = jnp.concatenate(in_order(att_all, me_head), axis=1)
    mixed = dot(att_all, out_full, ((1,), (0,)))

    cot = depth_cotangent[0]
    n_level = cot.shape[1]
    carried = mixed
    kept = []
    for level in range(n_level):
        summed = carried + embedded[level].astype(F32)
        inv = lax.rsqrt(jnp.mean(summed * summed, axis=-1, keepdims=True) + 1e-05)
        if level < n_level - 1:
            projected = dot((summed * inv).astype(BF16), proj_mat, ((1,), (0,)))
            carried = summed + projected * jax.nn.sigmoid(projected)
        else:
            projected = None
        kept.append((summed, inv, projected))
    grad = None
    for level in reversed(range(n_level)):
        summed, inv, projected = kept[level]
        grad_proj = cot[:, level, :]
        if grad is not None:
            gate = jax.nn.sigmoid(projected)
            slope = gate * (1.0 + projected * (1.0 - gate))
            grad_proj = (grad_proj.astype(F32) + grad * slope).astype(BF16)
        grad_normed = dot(grad_proj, proj_mat, ((1,), (1,)))
        along = jnp.mean(grad_normed * summed, axis=-1, keepdims=True)
        grad_sum = grad_normed * inv - summed * (along * inv * inv * inv)
        grad = grad_sum if grad is None else grad + grad_sum
    grad_mixed = grad.astype(BF16)

    out_heads = out_full.reshape(n_head, width_dev, width)
    grad_rows = []
    for k in range(1, n_head):
        part = dot(grad_mixed, pick(out_heads, me_head ^ k, 0), ((1,), (1,))).astype(BF16)
        grad_rows.append(swap(part, "head", k))
    own_part = dot(grad_mixed, pick(out_heads, me_head, 0), ((1,), (1,))).astype(BF16)
    grad_rows = jnp.concatenate(in_order([own_part] + grad_rows, me_head), axis=0)
    grad_rows = grad_rows.reshape(group_len, heads_here, DH)

    rows = width_dev // n_seq
    att_lanes = att_all.reshape(tokens, n_head, 2, n_far, rows)

    def term(core):
        part = pick(att_lanes, core, 2).reshape(tokens, n_head * n_far * rows)
        return dot(part, grad_mixed, ((0,), (0,)))

    got = swap(term(1 - me_core).astype(BF16), "seq", 1)
    chip = term(me_core) + got.astype(F32)
    chip = chip.reshape(n_head, n_far, rows, width)
    total = pick(pick(chip, me_head, 0), me_far, 0)
    for m in far:
        for k in range(n_head):
            if m or k:
                piece = pick(pick(chip, me_head ^ k, 0), me_far ^ (m // 2), 0).astype(BF16)
                mask = m * n_head + k
                total = total + swap(piece, ("seq", "head"), mask).astype(F32)
    columns = total.reshape(rows, n_dp, width // n_dp)
    block = pick(columns, me_dp, 1)
    for k in range(1, n_dp):
        block = block + swap(pick(columns, me_dp ^ k, 1).astype(BF16), "dp", k).astype(F32)
    grad_out_proj = seq_lanes(block.astype(BF16)).reshape(width_dev, width // n_dp).astype(F32)

    back_local = jnp.einsum("thd,the->hde", query_rows, grad_rows, preferred_element_type=F32)
    back_state = earlier_sum(back_local, True)
    grad_scores = (
        jnp.einsum("the,she->hts", grad_rows, value_rows, preferred_element_type=F32) * causal
    ).astype(BF16)
    grad_query = att_scale * (
        jnp.einsum("hts,shd->thd", grad_scores, key_rows, preferred_element_type=F32)
        + jnp.einsum("the,hde->thd", grad_rows, state_in, preferred_element_type=F32)
    )
    grad_key = att_scale * (
        jnp.einsum("hts,thd->shd", grad_scores, query_rows, preferred_element_type=F32)
        + jnp.einsum("she,hde->shd", value_rows, back_state, preferred_element_type=F32)
    )
    grad_value = att_scale * (
        jnp.einsum("hts,the->she", scores, grad_rows, preferred_element_type=F32)
        + jnp.einsum("shd,hde->she", key_rows, back_state, preferred_element_type=F32)
    )
    out_shape = (1, group_len, width_dev)
    return (
        grad_query.reshape(out_shape).astype(BF16),
        grad_key.reshape(out_shape).astype(BF16),
        grad_value.reshape(out_shape).astype(BF16),
        grad_out_proj,
    )


VMEM_BYTES = 48 * 1024 * 1024


def run(body, outs, where, *args):
    vmem = pl.BlockSpec(memory_space=pltpu.VMEM)
    return pl.pallas_call(
        body,
        out_shape=outs,
        in_specs=[pl.BlockSpec(memory_space=pltpu.SMEM)] + [vmem] * len(args),
        out_specs=[vmem] * len(outs),
        compiler_params=pltpu.CompilerParams(vmem_limit_bytes=VMEM_BYTES),
    )(where, *args)


def shaped(shape, dtype=BF16):
    return jax.ShapeDtypeStruct(shape, dtype)


def at(index, size):
    return pl.ds(pl.multiple_of(index * size, size), size)


HEAD, DP, SEQ = 4, 5, 6


def own_lane():
    me = lax.axis_index("seq")
    return 2 * (me % 2) + me // 2


def copies(body_of, outs, args):
    n_copies = len(body_of(None))

    def body(*refs):
        sems = refs[-1]
        going = [pltpu.make_async_copy(src, dst, sems.at[i]) for i, (src, dst) in enumerate(body_of(refs[:-1]))]
        for copy in going:
            copy.start()
        for copy in going:
            copy.wait()

    anywhere = pl.BlockSpec(memory_space=pl.ANY)
    return pl.pallas_call(
        body,
        out_shape=outs,
        in_specs=[anywhere] * len(args),
        out_specs=pl.BlockSpec(memory_space=pltpu.VMEM),
        scratch_shapes=[pltpu.SemaphoreType.DMA((n_copies,))],
    )(*args)


def first_lanes(code_table, depth_proj, n_dp):
    t_rows, t_cols = code_table.shape[1], code_table.shape[2] // 4
    d_half, d_cols = depth_proj.shape[0] // 8, depth_proj.shape[1]

    def body(table, depth, lanes, sems):
        moves = [(table.at[0, :, at(own_lane(), t_cols)], lanes.at[0, 0:t_rows])]
        for half in range(2):
            cols = slice(half * d_cols, (half + 1) * d_cols)
            moves.append((depth.at[at(2 * own_lane() + half, d_half)], lanes.at[0, t_rows:t_rows + d_half, cols]))
        going = [pltpu.make_async_copy(src, dst, sems.at[i]) for i, (src, dst) in enumerate(moves)]
        for copy in going:
            copy.start()
        for copy in going:
            copy.wait()
        for k in range(1, n_dp):
            lanes[k] = lanes[0]

    return pl.pallas_call(
        body,
        out_shape=shaped((n_dp, t_rows + d_half, t_cols)),
        in_specs=[pl.BlockSpec(memory_space=pl.ANY)] * 2,
        out_specs=pl.BlockSpec(memory_space=pltpu.VMEM),
        scratch_shapes=[pltpu.SemaphoreType.DMA((3,))],
    )(code_table, depth_proj)


def second_lanes(code_table, out_proj, after):
    t_rows, t_cols = code_table.shape[1], code_table.shape[2] // 4
    rows, cols = out_proj.shape[0] // 2, out_proj.shape[1]

    def views(refs):
        if refs is None:
            return [0, 1]
        table, out, _, lanes = refs
        return [
            (table.at[1, :, at(own_lane(), t_cols)], lanes.at[0:t_rows]),
            (out.at[at(own_lane() // 2, rows)], lanes.at[t_rows:t_rows + rows]),
        ]

    return copies(views, shaped((t_rows + rows, cols)), [code_table, out_proj, after])


def first_parts(where, pieces, t_rows, early):
    n, d_half, t_cols = pieces.shape
    d_half, d_cols = d_half - t_rows, t_cols // 2
    top, fold = n * t_rows, 2 * d_half

    def body(where_ref, ref, both, depth, top_fold):
        for k in range(n):
            both[k * t_rows:(k + 1) * t_rows, :] = ref[where_ref[DP] ^ k, :t_rows]
            place = where_ref[DP] ^ k
            cols = at(place % 2, d_cols)
            for half in range(2):
                part = ref[place, t_rows:, half * d_cols:(half + 1) * d_cols]
                row = pl.multiple_of((place // 2) * fold + half * d_half, d_half)
                both[pl.ds(pl.multiple_of(top + row, d_half), d_half), cols] = part
                depth[pl.ds(row, d_half), cols] = part
        top_fold[...] = depth[:early]

    rows = fold * n // 2
    return run(body, [shaped((top + rows, t_cols)), shaped((rows, t_cols)), shaped((early, t_cols))], where, pieces)


def second_parts(where, pieces, distances, t_rows):
    rows, cols = pieces[0].shape[0] - t_rows, pieces[0].shape[1]
    n = len(pieces)
    first = rows * 5 // 8

    def body(where_ref, *refs):
        table, head, tail = refs[n:]
        for k, ref in zip(distances, refs):
            cut = at(where_ref[DP] ^ k, cols)
            table[k * t_rows:(k + 1) * t_rows, :] = ref[:t_rows]
            head[:, cut] = ref[t_rows:t_rows + first]
            tail[:, cut] = ref[t_rows + first:]

    outs = [shaped((n * t_rows, cols)), shaped((first, n * cols)), shaped((rows - first, n * cols))]
    return run(body, outs, where, *pieces)


def embed(where, packed, top, level, n_level, tokens, own, got, half, n_dp, late, away):
    folds = tokens // DH
    n_rows = id_rows(n_level, tokens)
    rows, cols = own.shape
    rows_dev, extra = half // n_dp, rows - half

    def body(where_ref, mine_ref, core_ref, far_ref, own_ref, got_ref, *outs):
        def ids_of(ref, start):
            all_ids = ref[start:start + 2 * n_level * folds].astype(F32)
            mine = level * folds
            high = all_ids[mine:mine + folds]
            low = all_ids[(n_level * folds) + mine:(n_level * folds) + mine + folds]
            ids = high * 32.0 + low
            return jnp.concatenate([ids[f:f + 1] for f in range(folds)], axis=1)

        place = lax.broadcasted_iota(jnp.int32, (tokens, half), 1)
        owner = jnp.bitwise_xor(place // rows_dev, where_ref[DP])
        base = owner * rows_dev + place % rows_dev
        rows_of = [(mine_ref, top), (core_ref, top), (far_ref, top), (far_ref, top + n_rows)]
        columns = jnp.concatenate([ids_of(*r) for r in rows_of], axis=0).T.astype(jnp.int32)
        for m in (2, 3) if away else (1, 0):
            col = columns[:, m:m + 1]
            total = None
            for k, ref in enumerate((own_ref, got_ref)):
                start = (where_ref[HEAD] ^ k) * half
                hot = (base == col - start).astype(F32).astype(BF16)
                part = jnp.dot(hot, ref[:half], preferred_element_type=F32)
                total = part if total is None else total + part
            total = total.astype(BF16)
            if away:
                outs[0][(m - 2) * tokens:(m - 1) * tokens, :] = total
            else:
                outs[m][:tokens] = total
        if extra and away:
            outs[0][2 * tokens:2 * tokens + extra] = got_ref[half:]
            outs[0][2 * tokens + extra:] = own_ref[rows - late:]
        elif extra:
            outs[1][tokens:] = got_ref[half:]

    if away:
        outs = [shaped((2 * tokens + extra + late, cols))]
    else:
        outs = [shaped((tokens, cols)), shaped((tokens + extra, cols))]
    return run(body, outs, where, *packed, own, got)


def depth_grad(where, folds, rest, late, first, second, mixed, mixed_got, cot):
    arrays, which = [], []
    for array, _ in folds + first + second:
        found = [i for i, other in enumerate(arrays) if other is array]
        if not found:
            arrays.append(array)
        which.append(found[0] if found else len(arrays) - 1)
    starts = [start for _, start in folds + first + second]
    tokens, width = mixed.shape
    cols = width // 4
    chunk = 32

    def body(where_ref, *refs):
        parts = refs[:len(arrays)]
        mixed_ref, got_ref, cot_ref, out, full, sum_ref, mid_ref, last_ref, row_ref = refs[len(arrays):]
        for n in range(16):
            m, x, j = n // 4, n // 2 % 2, n % 2
            place = (where_ref[HEAD] ^ x) * 2 + j
            if rest[n] is None:
                full[at(where_ref[m], cols), at(place, cols)] = parts[which[n]][starts[n]:starts[n] + cols]
            else:
                main = pl.ds(pl.multiple_of(where_ref[m] * cols, cols), cols - late)
                tail = pl.ds(pl.multiple_of(where_ref[m] * cols + cols - late, 16), late)
                array = next(i for i, other in enumerate(arrays) if other is rest[n][0])
                full[main, at(place, cols)] = parts[which[n]][starts[n]:starts[n] + cols - late]
                full[tail, at(place, cols)] = parts[array][rest[n][1]:rest[n][1] + late]

        def rows_of(i):
            return pl.ds(pl.multiple_of(i * chunk, chunk), chunk)

        def lane_rows(i, n):
            return parts[which[n]][pl.ds(pl.multiple_of(starts[n] + i * chunk, chunk), chunk), :].astype(F32)

        def inverse(total):
            return lax.rsqrt(jnp.mean(total * total, axis=-1, keepdims=True) + 1e-05)

        def enter(i, carry):
            rows = rows_of(i)
            for m in range(4):
                cut = at(where_ref[m], cols)
                sum_ref[rows, cut] = mixed_ref[rows, cut] + got_ref[rows, cut].astype(F32) + lane_rows(i, 16 + m)
            total = sum_ref[rows, :]
            row_ref[rows, :] = (total * inverse(total)).astype(BF16)
            return carry

        lax.fori_loop(0, tokens // chunk, enter, 0, unroll=True)
        mid_ref[...] = jnp.dot(row_ref[...], full[...], preferred_element_type=F32)
        last_ref[...] = dot(cot_ref[:, width:], full[...], ((1,), (1,)))

        def middle(i, carry):
            rows = rows_of(i)
            projected = mid_ref[rows, :]
            gate = jax.nn.sigmoid(projected)
            mid_ref[rows, :] = sum_ref[rows, :] + projected * gate
            for m in range(4):
                cut = at(where_ref[m], cols)
                mid_ref[rows, cut] += lane_rows(i, 20 + m)
            total = mid_ref[rows, :]
            inv = inverse(total)
            grad = last_ref[rows, :]
            along = jnp.mean(grad * total, axis=-1, keepdims=True)
            grad = grad * inv - total * (along * inv * inv * inv)
            last_ref[rows, :] = grad
            slope = gate * (1.0 + projected * (1.0 - gate))
            row_ref[rows, :] = (cot_ref[rows, :width].astype(F32) + grad * slope).astype(BF16)
            return carry

        lax.fori_loop(0, tokens // chunk, middle, 0, unroll=True)
        mid_ref[...] = dot(row_ref[...], full[...], ((1,), (1,)))

        def leave(i, carry):
            rows = rows_of(i)
            total = sum_ref[rows, :]
            inv = inverse(total)
            grad = mid_ref[rows, :]
            along = jnp.mean(grad * total, axis=-1, keepdims=True)
            grad = last_ref[rows, :] + grad * inv - total * (along * inv * inv * inv)
            out[rows, :] = grad.astype(BF16)
            return carry

        lax.fori_loop(0, tokens // chunk, leave, 0, unroll=True)

    vmem = pl.BlockSpec(memory_space=pltpu.VMEM)
    return pl.pallas_call(
        body,
        out_shape=shaped((tokens, width)),
        in_specs=[pl.BlockSpec(memory_space=pltpu.SMEM)] + [vmem] * (len(arrays) + 3),
        out_specs=vmem,
        scratch_shapes=[
            pltpu.VMEM((width, width), BF16),
            pltpu.VMEM((tokens, width), F32),
            pltpu.VMEM((tokens, width), F32),
            pltpu.VMEM((tokens, width), F32),
            pltpu.VMEM((tokens, width), BF16),
        ],
        compiler_params=pltpu.CompilerParams(vmem_limit_bytes=VMEM_BYTES),
    )(where, *arrays, mixed, mixed_got, cot)


def id_rows(n_level, tokens):
    return -(-2 * n_level * (tokens // DH) // 16) * 16


def pack(where, keys, values, ids):
    heads = keys.shape[1] // DH
    n_level, tokens = ids.shape
    folds = tokens // DH
    top = heads * DH

    def body(where_ref, k_ref, v_ref, ids_ref, out):
        parts = []
        for level in range(n_level):
            for fold in range(folds):
                parts.append(ids_ref[level:level + 1, fold * DH:(fold + 1) * DH])
        whole = jnp.concatenate(parts, axis=0)
        both = jnp.concatenate([whole // 32, whole % 32], axis=0).astype(F32).astype(BF16)
        out[top:top + 2 * n_level * folds] = both
        for i in range(heads):
            cut = slice(i * DH, (i + 1) * DH)
            out[cut] = dot(k_ref[:, cut], v_ref[:, cut], ((0,), (0,))).astype(BF16)

    return run(body, [shaped((top + id_rows(n_level, tokens), DH))], where, keys, values, ids)[0]


def pack_chip(where, own, core, top):
    rows = own.shape[0] - top

    def body(where_ref, own_ref, core_ref, out):
        out[:top] = (own_ref[:top].astype(F32) + core_ref[:top].astype(F32)).astype(BF16)
        out[top:top + rows] = own_ref[top:]
        out[top + rows:] = core_ref[top:]

    return run(body, [shaped((top + 2 * rows, DH))], where, own, core)[0]


def lower(size):
    rows = lax.broadcasted_iota(jnp.int32, (size, size), 0)
    cols = lax.broadcasted_iota(jnp.int32, (size, size), 1)
    return rows >= cols


def upper(size):
    rows = lax.broadcasted_iota(jnp.int32, (size, size), 0)
    cols = lax.broadcasted_iota(jnp.int32, (size, size), 1)
    return rows <= cols


def attend(where, queries, keys, values, from_core, from_far, att_scale):
    length, width_dev = queries.shape
    heads = width_dev // DH

    def body(where_ref, q_ref, k_ref, v_ref, core_ref, far_ref, att, state):
        near = (where_ref[0] // 2).astype(F32)
        far = (where_ref[0] % 2).astype(F32)
        keep = lower(length)
        for i in range(heads):
            cut = slice(i * DH, (i + 1) * DH)
            state[i] = (core_ref[cut].astype(F32) * near + far_ref[cut].astype(F32) * far).astype(BF16)
            q = q_ref[:, cut]
            scores = jnp.where(keep, dot(q, k_ref[:, cut], ((1,), (1,))), 0.0).astype(BF16)
            both = jnp.dot(scores, v_ref[:, cut], preferred_element_type=F32)
            both += jnp.dot(q, state[i], preferred_element_type=F32)
            att[:, cut] = (att_scale * both).astype(BF16)

    return run(
        body, [shaped((length, width_dev)), shaped((heads, DH, DH))], where, queries, keys, values, from_core, from_far
    )


def mix_own(where, attended, head, tail):
    length = attended.shape[0] // 2
    half, width = head.shape[0] + tail.shape[0], head.shape[1]

    def body(where_ref, att, head_ref, tail_ref, out):
        core = where_ref[0] // 2
        own = jnp.concatenate([head_ref[...], tail_ref[...]], axis=0)
        for k in range(2):
            rows = at(where_ref[HEAD] ^ (1 - k), length)
            out[k] = jnp.dot(att[rows, at(core, half)], own, preferred_element_type=F32)

    return run(body, [shaped((2, length, width), F32)], where, attended, head, tail)[0]


def mix(where, attended, part, got_head, got_tail, other):
    length = attended.shape[0] // 2
    width = part.shape[2]
    half = got_head.shape[0] + got_tail.shape[0]
    dtype = BF16 if other else F32

    def body(where_ref, att, part_ref, head, tail, out):
        rows = at(where_ref[HEAD] ^ (1 if other else 0), length)
        core = where_ref[0] // 2
        got = jnp.concatenate([head[...], tail[...]], axis=0)
        total = part_ref[0 if other else 1]
        total += jnp.dot(att[rows, at(1 - core, half)], got, preferred_element_type=F32)
        out[...] = total.astype(dtype)

    return run(body, [shaped((length, width), dtype)], where, attended, part, got_head, got_tail)[0]


def weight_own(where, attended, grad_own):
    tokens, width = grad_own.shape

    def body(where_ref, att, own, out):
        for m in range(4):
            out[m] = dot(att[at(where_ref[HEAD], tokens), at(where_ref[m], DH)], own[...], ((0,), (0,)))

    return run(body, [shaped((4, DH, width), F32)], where, attended, grad_own)[0]


def weight_terms(where, attended, part, grad_got):
    tokens, width = grad_got.shape

    def body(where_ref, att, part_ref, got, send, keep):
        def term(m):
            a = att[at(1 - where_ref[HEAD], tokens), at(where_ref[m], DH)]
            return part_ref[m] + dot(a, got[...], ((0,), (0,)))

        send[0] = term(2).astype(BF16)
        send[1] = term(3).astype(BF16)
        keep[0] = term(0)
        keep[1] = term(1)

    return run(
        body, [shaped((2, DH, width)), shaped((2, DH, width), F32)], where, attended, part, grad_got
    )


def add_core(where, keep, got):
    shape = keep.shape[1:]

    def body(where_ref, keep_ref, got_ref, send, rest):
        rest[...] = keep_ref[0] + got_ref[0].astype(F32)
        send[...] = (keep_ref[1] + got_ref[1].astype(F32)).astype(BF16)

    return run(body, [shaped(shape), shaped(shape, F32)], where, keep, got)


def add_far(where, keep, got, n_dp):
    rows, width = keep.shape
    cols = width // n_dp

    def body(where_ref, keep_ref, got_ref, rest, *send):
        for k in range(n_dp):
            cut = at(where_ref[DP] ^ k, cols)
            total = keep_ref[:, cut] + got_ref[:, cut].astype(F32)
            if k:
                send[k - 1][...] = total.astype(BF16)
            else:
                rest[...] = total

    return run(body, [shaped((rows, cols), F32)] + [shaped((rows, cols))] * (n_dp - 1), where, keep, got)


def add_all(where, keep, got):
    def body(where_ref, keep_ref, *refs):
        total = keep_ref[...]
        for ref in refs[:-1]:
            total = total + ref[...].astype(F32)
        refs[-1][...] = total.astype(BF16)

    return run(body, [shaped(keep.shape)], where, keep, *got)[0]


def rows_together(where, pieces):
    rows, cols = pieces[0].shape

    def body(where_ref, *refs):
        for m, ref in enumerate(refs[:-1]):
            refs[-1][at(where_ref[m], rows), :] = ref[...].astype(F32)

    return run(body, [shaped((rows * 4, cols), F32)], where, *pieces)[0]


def grad_attend(where, grad_own, grad_got, own_head, own_tail, got_head, got_tail, queries):
    tokens, width = grad_own.shape
    length, width_dev = queries.shape
    half = width_dev // 2

    def body(where_ref, own, got, head, tail, got_head, got_tail, q_ref, rows, back):
        for c, ends in enumerate(((head, tail), (got_head, got_tail))):
            block = jnp.concatenate([ends[0][...], ends[1][...]], axis=0)
            for k, ref in enumerate((own, got)):
                part = dot(ref[...], block, ((1,), (1,))).astype(BF16)
                rows[at(where_ref[HEAD] ^ k, tokens), at((where_ref[0] // 2) ^ c, half)] = part
        for i in range(width_dev // DH):
            cut = slice(i * DH, (i + 1) * DH)
            back[i] = dot(q_ref[:, cut], rows[:, cut], ((0,), (0,))).astype(BF16)

    outs = [shaped((length, width_dev)), shaped((width_dev // DH, DH, DH))]
    return run(body, outs, where, grad_own, grad_got, own_head, own_tail, got_head, got_tail, queries)


def query_grads(where, grad_rows, keys, values, state, att_scale):
    length, width_dev = keys.shape

    def body(where_ref, g_ref, k_ref, v_ref, s_ref, out):
        keep = lower(length)
        for i in range(width_dev // DH):
            cut = slice(i * DH, (i + 1) * DH)
            g = g_ref[:, cut]
            scores = jnp.where(keep, dot(g, v_ref[:, cut], ((1,), (1,))), 0.0).astype(BF16)
            both = jnp.dot(scores, k_ref[:, cut], preferred_element_type=F32)
            both += dot(g, s_ref[i], ((1,), (1,)))
            out[:, cut] = (att_scale * both).astype(BF16)

    return run(body, [shaped((length, width_dev))], where, grad_rows, keys, values, state)[0]


def key_value_parts(where, grad_rows, queries, keys, values):
    length, width_dev = keys.shape

    def body(where_ref, g_ref, q_ref, k_ref, v_ref, dk, dv):
        keep = upper(length)
        for i in range(width_dev // DH):
            cut = slice(i * DH, (i + 1) * DH)
            g, q, k, v = g_ref[:, cut], q_ref[:, cut], k_ref[:, cut], v_ref[:, cut]
            grad_scores = jnp.where(keep, dot(v, g, ((1,), (1,))), 0.0).astype(BF16)
            dk[:, cut] = jnp.dot(grad_scores, q, preferred_element_type=F32)
            scores = jnp.where(keep, dot(k, q, ((1,), (1,))), 0.0).astype(BF16)
            dv[:, cut] = jnp.dot(scores, g, preferred_element_type=F32)

    outs = [shaped((length, width_dev), F32)] * 2
    return run(body, outs, where, grad_rows, queries, keys, values)


def key_value_grads(where, key_part, value_part, keys, values, from_core, from_far, att_scale):
    length, width_dev = keys.shape

    def body(where_ref, kp_ref, vp_ref, k_ref, v_ref, core_ref, far_ref, dk, dv):
        near = 1.0 - (where_ref[0] // 2).astype(F32)
        far = 1.0 - (where_ref[0] % 2).astype(F32)
        for i in range(width_dev // DH):
            cut = slice(i * DH, (i + 1) * DH)
            back = (core_ref[i].astype(F32) * near + far_ref[i].astype(F32) * far).astype(BF16)
            both = kp_ref[:, cut] + dot(v_ref[:, cut], back, ((1,), (1,)))
            dk[:, cut] = (att_scale * both).astype(BF16)
            both = vp_ref[:, cut] + jnp.dot(k_ref[:, cut], back, preferred_element_type=F32)
            dv[:, cut] = (att_scale * both).astype(BF16)

    outs = [shaped((length, width_dev))] * 2
    return run(body, outs, where, key_part, value_part, keys, values, from_core, from_far)


def fits(queries, out_proj, depth_proj, code_table, code_ids):
    n_seq, n_head = lax.axis_size("seq"), lax.axis_size("head")
    return (
        n_seq == 4
        and n_head == 2
        and queries.shape[2] == 4 * DH
        and code_table.shape[0] == 2
        and out_proj.shape[1] % 128 == 0
        and depth_proj.shape[1] % 128 == 0
        and code_table.shape[1] % 128 == 0
        and code_ids.shape[1] % DH == 0
        and code_table.shape[1] * n_head * lax.axis_size("dp") <= 32 * 256
    )


def on_device(queries, keys, values, out_proj, depth_proj, code_table, code_ids, depth_cotangent):
    if not fits(queries, out_proj, depth_proj, code_table, code_ids):
        return on_device_any(
            queries, keys, values, out_proj, depth_proj, code_table, code_ids, depth_cotangent
        )
    n_dp = lax.axis_size("dp")
    me_seq, me_head, me_dp = (lax.axis_index(a) for a in ("seq", "head", "dp"))
    group_len = queries.shape[1]
    width = code_table.shape[2]
    att_scale = float(group_len * lax.axis_size("seq")) ** (-0.5)
    core, far = me_seq % 2, me_seq // 2
    lane = 2 * core + far
    where = jnp.stack([lane, lane ^ 1, lane ^ 2, lane ^ 3, me_head, me_dp, me_seq]).astype(jnp.int32)
    queries, keys, values = queries[0], keys[0], values[0]

    def far_swap(block):
        return swap(block, "seq", 2)

    def core_swap(block):
        return swap(block, "seq", 1)

    def all_lanes(block):
        got = far_swap(block)
        return [block, got, core_swap(block), core_swap(got)]

    t_rows, tokens = code_table.shape[1], code_ids.shape[1]
    half = t_rows * n_dp
    lanes_0 = first_lanes(code_table, depth_proj, n_dp)
    pieces_0 = lax.all_to_all(lanes_0, "dp", 0, 0)
    lanes_1 = second_lanes(code_table, out_proj, lanes_0)
    distances = [n_dp // 2] + [k for k in range(1, n_dp) if k != n_dp // 2]
    pieces_1 = [lanes_1] + [swap(lanes_1, "dp", k) for k in distances]

    top = keys.shape[1]
    keys, values, _ = lax.optimization_barrier((keys, values, lanes_1))
    mine = pack(where, keys, values, code_ids[0].T)
    from_core = core_swap(mine)
    chip = pack_chip(where, mine, from_core, top)
    from_far = far_swap(chip)
    packed = (mine, from_core, from_far)

    attended, state_in = attend(where, queries, keys, values, from_core, from_far, att_scale)

    pieces_0, _ = lax.optimization_barrier((pieces_0, attended))
    fold = depth_proj.shape[0] // 4
    early = fold + fold * 7 // 16
    late = 2 * fold - early
    part_0, depth_part, depth_top = first_parts(where, pieces_0, t_rows, early)
    got_0 = swap(part_0, "head", 1)
    depth_far = far_swap(depth_top)

    pieces_1, depth_far = lax.optimization_barrier((pieces_1, depth_far))
    part_1, out_head, out_tail = second_parts(where, pieces_1, [0, *distances], t_rows)
    got_head, got_tail = core_swap(out_head), core_swap(out_tail)
    got_1 = swap(part_1, "head", 1)

    mixed_part = mix_own(where, attended, out_head, out_tail)
    got_0, got_head, _ = lax.optimization_barrier((got_0, got_head, part_1))
    (to_far,) = embed(where, packed, top, 0, 2, tokens, part_0, got_0, half, n_dp, late, True)
    far_0 = far_swap(to_far)

    got_tail, _ = lax.optimization_barrier((got_tail, to_far))
    mixed_send = mix(where, attended, mixed_part, got_head, got_tail, True)
    mixed_got = swap(mixed_send, "head", 1)
    mixed_part, got_1 = lax.optimization_barrier((mixed_part, got_1))
    mixed = mix(where, attended, mixed_part, got_head, got_tail, False)
    near_0, _, _ = lax.optimization_barrier((got_0, mixed, mixed_send))
    own_0, to_core = embed(where, packed, top, 0, 2, tokens, part_0, near_0, half, n_dp, late, False)
    core_0 = core_swap(to_core)

    got_1, _, _ = lax.optimization_barrier((got_1, mixed, mixed_send))
    (to_far,) = embed(where, packed, top, 1, 2, tokens, part_1, got_1, half, n_dp, 0, True)
    near_1, _ = lax.optimization_barrier((got_1, to_far))
    own_1, to_core = embed(where, packed, top, 1, 2, tokens, part_1, near_1, half, n_dp, 0, False)
    far_1 = far_swap(to_far)
    depth_core, depth_core_far = core_swap(depth_part), core_swap(depth_far)
    far_0, far_1, mixed_got, depth_core, depth_core_far, core_0, to_core, own_1 = lax.optimization_barrier(
        (far_0, far_1, mixed_got, depth_core, depth_core_far, core_0, to_core, own_1)
    )
    core_far_0, core_1, core_far_1 = core_swap(far_0), core_swap(to_core), core_swap(far_1)

    end = 2 * tokens
    folds = [(depth_part, 0), (depth_part, fold), (got_0, half), (got_0, half + fold)]
    folds += [(depth_far, 0), (depth_far, fold), (far_0, end), (far_0, end + fold)]
    folds += [(depth_core, 0), (depth_core, fold), (core_0, tokens), (core_0, tokens + fold)]
    folds += [(depth_core_far, 0), (depth_core_far, fold), (core_far_0, end), (core_far_0, end + fold)]
    rest = [None] * 16
    rest[5], rest[13] = (far_0, end + 2 * fold), (core_far_0, end + 2 * fold)
    first = [(own_0, 0), (far_0, 0), (core_0, 0), (core_far_0, tokens)]
    second = [(own_1, 0), (far_1, 0), (core_1, 0), (core_far_1, tokens)]
    cot = depth_cotangent[0].reshape(tokens, -1)
    grad_mixed = depth_grad(where, folds, rest, late, first, second, mixed, mixed_got, cot)

    grad_got = swap(grad_mixed, "head", 1)
    part = weight_own(where, attended, grad_mixed)
    send, keep = weight_terms(where, attended, part, grad_got)
    send, keep = add_core(where, keep, core_swap(send))
    from_far = far_swap(send)
    grad_rows, back = grad_attend(where, grad_mixed, grad_got, out_head, out_tail, got_head, got_tail, queries)
    back, send = lax.optimization_barrier((back, send))
    back_core = core_swap(back)
    back_chip = (back.astype(F32) + back_core.astype(F32)).astype(BF16)
    key_part, value_part = key_value_parts(where, grad_rows, queries, keys, values)
    grad_query = query_grads(where, grad_rows, keys, values, state_in, att_scale)
    from_far, key_part, value_part, grad_query, back_chip = lax.optimization_barrier(
        (from_far, key_part, value_part, grad_query, back_chip)
    )
    keep, *send = add_far(where, keep, from_far, n_dp)
    got = [swap(send[k - 1], "dp", k) for k in reversed(range(1, n_dp))]
    back_chip, keep = lax.optimization_barrier((back_chip, keep))
    back_far = far_swap(back_chip)
    block = add_all(where, keep, got)
    blocks = [block, far_swap(block), core_swap(block), swap(block, "seq", 3)]
    key_part, block = lax.optimization_barrier((key_part, block))
    grad_key, grad_value = key_value_grads(
        where, key_part, value_part, keys, values, back_core, back_far, att_scale
    )
    blocks, grad_key, grad_value = lax.optimization_barrier((blocks, grad_key, grad_value))
    grad_out_proj = rows_together(where, blocks)
    return grad_query[None], grad_key[None], grad_value[None], grad_out_proj


def solution(mesh):
    in_specs = (
        P("dp", "seq", "head"),
        P("dp", "seq", "head"),
        P("dp", "seq", "head"),
        P("head", "dp"),
        P(None, ("head", "dp")),
        P(None, ("head", "dp"), None),
        P("dp", ("seq", "head"), None),
        P("dp", ("seq", "head"), None, None),
    )
    out_specs = (
        P("dp", "seq", "head"),
        P("dp", "seq", "head"),
        P("dp", "seq", "head"),
        P("head", "dp"),
    )
    return jax.shard_map(
        on_device, mesh=mesh, in_specs=in_specs, out_specs=out_specs, check_vma=False
    )
```

```python
import jax
import jax.numpy as jnp
from jax import lax
from jax.experimental import pallas as pl
from jax.experimental.pallas import tpu as pltpu
from jax.sharding import PartitionSpec as P

DH = 128
F32 = jnp.float32
BF16 = jnp.bfloat16


def swap(block, axis, mask):
    return lax.ppermute(block, axis, [(i, i ^ mask) for i in range(lax.axis_size(axis))])


def has_bit(index, bit):
    return lax.bitwise_and(index, jnp.int32(bit)) != 0


def in_order(pieces, index):
    pieces = list(pieces)
    bit = 1
    while bit < len(pieces):
        odd = has_bit(index, bit)
        pieces = [jnp.where(odd, pieces[j ^ bit], pieces[j]) for j in range(len(pieces))]
        bit *= 2
    return pieces


def pick(array, index, dim):
    return lax.dynamic_index_in_dim(array, index, dim, keepdims=False)


def exchange(block, axis):
    return [block] + [swap(block, axis, k) for k in range(1, lax.axis_size(axis))]


def dot(a, b, dims):
    return lax.dot_general(a, b, ((dims[0], dims[1]), ((), ())), preferred_element_type=F32)


def earlier_sum(state, backward):
    n_seq = lax.axis_size("seq")
    me = lax.axis_index("seq")
    before = jnp.zeros_like(state)
    total = state
    bit = 1
    while bit < n_seq:
        got = swap(total.astype(BF16), "seq", bit).astype(F32)
        mine = has_bit(me, bit)
        takes = jnp.logical_not(mine) if backward else mine
        before = before + jnp.where(takes, got, 0.0)
        total = total + got
        bit *= 2
    return before.astype(BF16)


def on_device_any(queries, keys, values, out_proj, depth_proj, code_table, code_ids, depth_cotangent):
    n_seq, n_head, n_dp = (lax.axis_size(a) for a in ("seq", "head", "dp"))
    me_seq, me_head, me_dp = (lax.axis_index(a) for a in ("seq", "head", "dp"))
    group_len, width_dev = queries.shape[1:]
    heads_here = width_dev // DH
    tokens = group_len // n_head
    n_far = n_seq // 2
    me_core = lax.bitwise_and(me_seq, jnp.int32(1))
    me_far = lax.shift_right_logical(me_seq, jnp.int32(1))
    lane = me_core * n_far + me_far
    att_scale = float(group_len * n_seq) ** (-0.5)
    width = code_table.shape[2]
    wide = width // n_seq
    far = [2 * m for m in range(n_far)]

    def far_exchange(block):
        return [block] + [swap(block, "seq", m) for m in far[1:]]

    def seq_lanes(block):
        near = jnp.stack(in_order(far_exchange(block), me_far))
        both = in_order([near, swap(near, "seq", 1)], me_core)
        return jnp.concatenate(both, axis=0)

    ids = code_ids[0].T
    ids_far = jnp.stack(far_exchange(ids))
    ids_rel = jnp.stack([ids_far, swap(ids_far, "seq", 1)])

    table = lax.dynamic_slice_in_dim(code_table, lane * wide, wide, axis=2)
    rows_dev = table.shape[1]
    embedded = []
    row_no = []
    for k_head in range(n_head):
        for k_dp in range(n_dp):
            owner = (me_head ^ k_head) * n_dp + (me_dp ^ k_dp)
            row_no.append(owner * rows_dev + jnp.arange(rows_dev, dtype=jnp.int32))
    row_no = jnp.concatenate(row_no)
    for level in range(table.shape[0]):
        part = jnp.concatenate(exchange(table[level], "dp"), axis=0)
        part = jnp.concatenate(exchange(part, "head"), axis=0)
        level_ids = ids_rel[:, :, level].reshape(-1)
        onehot = (level_ids[:, None] == row_no[None, :]).astype(BF16)
        rel = dot(onehot, part, ((1,), (0,))).astype(BF16).reshape(2, n_far, tokens, wide)
        mine = [rel[:, 0]] + [swap(rel[:, m // 2], "seq", m) for m in far[1:]]
        near = jnp.stack([block[0] for block in mine])
        other = swap(jnp.stack([block[1] for block in mine]), "seq", 1)
        near = jnp.stack(in_order(list(near), me_far))
        other = jnp.stack(in_order(list(other), me_far))
        lanes = jnp.concatenate(in_order([near, other], me_core), axis=0)
        embedded.append(lanes.transpose(1, 0, 2).reshape(tokens, width))

    out_rows = out_proj.shape[0] // n_seq
    out_lane = lax.dynamic_slice_in_dim(out_proj, lane * out_rows, out_rows, axis=0)
    out_part = jnp.concatenate(in_order(exchange(out_lane, "dp"), me_dp), axis=1)
    out_part = jnp.stack(in_order(exchange(out_part, "head"), me_head))
    out_full = seq_lanes(out_part).transpose(1, 0, 2, 3).reshape(n_head * width_dev, width)

    depth_rows = depth_proj.shape[0] // n_seq
    depth_lane = lax.dynamic_slice_in_dim(depth_proj, lane * depth_rows, depth_rows, axis=0)
    depth_part = jnp.concatenate(in_order(exchange(depth_lane, "dp"), me_dp), axis=1)
    depth_part = jnp.concatenate(in_order(exchange(depth_part, "head"), me_head), axis=1)
    proj_mat = seq_lanes(depth_part).reshape(width, width)

    query_rows = queries[0].reshape(group_len, heads_here, DH)
    key_rows = keys[0].reshape(group_len, heads_here, DH)
    value_rows = values[0].reshape(group_len, heads_here, DH)
    places = jnp.arange(group_len, dtype=jnp.int32)
    causal = (places[:, None] >= places[None, :]).astype(F32)
    state_local = jnp.einsum("thd,the->hde", key_rows, value_rows, preferred_element_type=F32)
    state_in = earlier_sum(state_local, False)
    scores = (
        jnp.einsum("thd,shd->hts", query_rows, key_rows, preferred_element_type=F32) * causal
    ).astype(BF16)
    attended = (
        att_scale
        * (
            jnp.einsum("hts,she->the", scores, value_rows, preferred_element_type=F32)
            + jnp.einsum("thd,hde->the", query_rows, state_in, preferred_element_type=F32)
        )
    ).astype(BF16)
    attended = attended.reshape(n_head, tokens, width_dev)
    att_all = [pick(attended, me_head, 0)]
    att_all += [swap(pick(attended, me_head ^ k, 0), "head", k) for k in range(1, n_head)]
    att_all = jnp.concatenate(in_order(att_all, me_head), axis=1)
    mixed = dot(att_all, out_full, ((1,), (0,)))

    cot = depth_cotangent[0]
    n_level = cot.shape[1]
    carried = mixed
    kept = []
    for level in range(n_level):
        summed = carried + embedded[level].astype(F32)
        inv = lax.rsqrt(jnp.mean(summed * summed, axis=-1, keepdims=True) + 1e-05)
        if level < n_level - 1:
            projected = dot((summed * inv).astype(BF16), proj_mat, ((1,), (0,)))
            carried = summed + projected * jax.nn.sigmoid(projected)
        else:
            projected = None
        kept.append((summed, inv, projected))
    grad = None
    for level in reversed(range(n_level)):
        summed, inv, projected = kept[level]
        grad_proj = cot[:, level, :]
        if grad is not None:
            gate = jax.nn.sigmoid(projected)
            slope = gate * (1.0 + projected * (1.0 - gate))
            grad_proj = (grad_proj.astype(F32) + grad * slope).astype(BF16)
        grad_normed = dot(grad_proj, proj_mat, ((1,), (1,)))
        along = jnp.mean(grad_normed * summed, axis=-1, keepdims=True)
        grad_sum = grad_normed * inv - summed * (along * inv * inv * inv)
        grad = grad_sum if grad is None else grad + grad_sum
    grad_mixed = grad.astype(BF16)

    out_heads = out_full.reshape(n_head, width_dev, width)
    grad_rows = []
    for k in range(1, n_head):
        part = dot(grad_mixed, pick(out_heads, me_head ^ k, 0), ((1,), (1,))).astype(BF16)
        grad_rows.append(swap(part, "head", k))
    own_part = dot(grad_mixed, pick(out_heads, me_head, 0), ((1,), (1,))).astype(BF16)
    grad_rows = jnp.concatenate(in_order([own_part] + grad_rows, me_head), axis=0)
    grad_rows = grad_rows.reshape(group_len, heads_here, DH)

    rows = width_dev // n_seq
    att_lanes = att_all.reshape(tokens, n_head, 2, n_far, rows)

    def term(core):
        part = pick(att_lanes, core, 2).reshape(tokens, n_head * n_far * rows)
        return dot(part, grad_mixed, ((0,), (0,)))

    got = swap(term(1 - me_core).astype(BF16), "seq", 1)
    chip = term(me_core) + got.astype(F32)
    chip = chip.reshape(n_head, n_far, rows, width)
    total = pick(pick(chip, me_head, 0), me_far, 0)
    for m in far:
        for k in range(n_head):
            if m or k:
                piece = pick(pick(chip, me_head ^ k, 0), me_far ^ (m // 2), 0).astype(BF16)
                mask = m * n_head + k
                total = total + swap(piece, ("seq", "head"), mask).astype(F32)
    columns = total.reshape(rows, n_dp, width // n_dp)
    block = pick(columns, me_dp, 1)
    for k in range(1, n_dp):
        block = block + swap(pick(columns, me_dp ^ k, 1).astype(BF16), "dp", k).astype(F32)
    grad_out_proj = seq_lanes(block.astype(BF16)).reshape(width_dev, width // n_dp).astype(F32)

    back_local = jnp.einsum("thd,the->hde", query_rows, grad_rows, preferred_element_type=F32)
    back_state = earlier_sum(back_local, True)
    grad_scores = (
        jnp.einsum("the,she->hts", grad_rows, value_rows, preferred_element_type=F32) * causal
    ).astype(BF16)
    grad_query = att_scale * (
        jnp.einsum("hts,shd->thd", grad_scores, key_rows, preferred_element_type=F32)
        + jnp.einsum("the,hde->thd", grad_rows, state_in, preferred_element_type=F32)
    )
    grad_key = att_scale * (
        jnp.einsum("hts,thd->shd", grad_scores, query_rows, preferred_element_type=F32)
        + jnp.einsum("she,hde->shd", value_rows, back_state, preferred_element_type=F32)
    )
    grad_value = att_scale * (
        jnp.einsum("hts,the->she", scores, grad_rows, preferred_element_type=F32)
        + jnp.einsum("shd,hde->she", key_rows, back_state, preferred_element_type=F32)
    )
    out_shape = (1, group_len, width_dev)
    return (
        grad_query.reshape(out_shape).astype(BF16),
        grad_key.reshape(out_shape).astype(BF16),
        grad_value.reshape(out_shape).astype(BF16),
        grad_out_proj,
    )


VMEM_BYTES = 48 * 1024 * 1024


def run(body, outs, where, *args):
    vmem = pl.BlockSpec(memory_space=pltpu.VMEM)
    return pl.pallas_call(
        body,
        out_shape=outs,
        in_specs=[pl.BlockSpec(memory_space=pltpu.SMEM)] + [vmem] * len(args),
        out_specs=[vmem] * len(outs),
        compiler_params=pltpu.CompilerParams(vmem_limit_bytes=VMEM_BYTES),
    )(where, *args)


def shaped(shape, dtype=BF16):
    return jax.ShapeDtypeStruct(shape, dtype)


def at(index, size):
    return pl.ds(pl.multiple_of(index * size, size), size)


HEAD, DP, SEQ = 4, 5, 6


def own_lane():
    me = lax.axis_index("seq")
    return 2 * (me % 2) + me // 2


def copies(body_of, outs, args):
    n_copies = len(body_of(None))

    def body(*refs):
        sems = refs[-1]
        going = [pltpu.make_async_copy(src, dst, sems.at[i]) for i, (src, dst) in enumerate(body_of(refs[:-1]))]
        for copy in going:
            copy.start()
        for copy in going:
            copy.wait()

    anywhere = pl.BlockSpec(memory_space=pl.ANY)
    return pl.pallas_call(
        body,
        out_shape=outs,
        in_specs=[anywhere] * len(args),
        out_specs=pl.BlockSpec(memory_space=pltpu.VMEM),
        scratch_shapes=[pltpu.SemaphoreType.DMA((n_copies,))],
    )(*args)


def first_lanes(code_table, depth_proj, n_dp):
    t_rows, t_cols = code_table.shape[1], code_table.shape[2] // 4
    d_half, d_cols = depth_proj.shape[0] // 8, depth_proj.shape[1]

    def body(table, depth, lanes, sems):
        moves = [(table.at[0, :, at(own_lane(), t_cols)], lanes.at[0, 0:t_rows])]
        for half in range(2):
            cols = slice(half * d_cols, (half + 1) * d_cols)
            moves.append((depth.at[at(2 * own_lane() + half, d_half)], lanes.at[0, t_rows:t_rows + d_half, cols]))
        going = [pltpu.make_async_copy(src, dst, sems.at[i]) for i, (src, dst) in enumerate(moves)]
        for copy in going:
            copy.start()
        for copy in going:
            copy.wait()
        for k in range(1, n_dp):
            lanes[k] = lanes[0]

    return pl.pallas_call(
        body,
        out_shape=shaped((n_dp, t_rows + d_half, t_cols)),
        in_specs=[pl.BlockSpec(memory_space=pl.ANY)] * 2,
        out_specs=pl.BlockSpec(memory_space=pltpu.VMEM),
        scratch_shapes=[pltpu.SemaphoreType.DMA((3,))],
    )(code_table, depth_proj)


def second_lanes(code_table, out_proj, after):
    t_rows, t_cols = code_table.shape[1], code_table.shape[2] // 4
    rows, cols = out_proj.shape[0] // 2, out_proj.shape[1]

    def views(refs):
        if refs is None:
            return [0, 1]
        table, out, _, lanes = refs
        return [
            (table.at[1, :, at(own_lane(), t_cols)], lanes.at[0:t_rows]),
            (out.at[at(own_lane() // 2, rows)], lanes.at[t_rows:t_rows + rows]),
        ]

    return copies(views, shaped((t_rows + rows, cols)), [code_table, out_proj, after])


def first_parts(where, pieces, t_rows, early):
    n, d_half, t_cols = pieces.shape
    d_half, d_cols = d_half - t_rows, t_cols // 2
    top, fold = n * t_rows, 2 * d_half

    def body(where_ref, ref, both, depth, top_fold):
        for k in range(n):
            both[k * t_rows:(k + 1) * t_rows, :] = ref[where_ref[DP] ^ k, :t_rows]
            place = where_ref[DP] ^ k
            cols = at(place % 2, d_cols)
            for half in range(2):
                part = ref[place, t_rows:, half * d_cols:(half + 1) * d_cols]
                row = pl.multiple_of((place // 2) * fold + half * d_half, d_half)
                both[pl.ds(pl.multiple_of(top + row, d_half), d_half), cols] = part
                depth[pl.ds(row, d_half), cols] = part
        top_fold[...] = depth[:early]

    rows = fold * n // 2
    return run(body, [shaped((top + rows, t_cols)), shaped((rows, t_cols)), shaped((early, t_cols))], where, pieces)


def second_parts(where, pieces, distances, t_rows):
    rows, cols = pieces[0].shape[0] - t_rows, pieces[0].shape[1]
    n = len(pieces)
    first = rows * 5 // 8

    def body(where_ref, *refs):
        table, head, tail = refs[n:]
        for k, ref in zip(distances, refs):
            cut = at(where_ref[DP] ^ k, cols)
            table[k * t_rows:(k + 1) * t_rows, :] = ref[:t_rows]
            head[:, cut] = ref[t_rows:t_rows + first]
            tail[:, cut] = ref[t_rows + first:]

    outs = [shaped((n * t_rows, cols)), shaped((first, n * cols)), shaped((rows - first, n * cols))]
    return run(body, outs, where, *pieces)


def embed(where, packed, top, level, n_level, tokens, own, got, half, n_dp, late, away):
    folds = tokens // DH
    n_rows = id_rows(n_level, tokens)
    rows, cols = own.shape
    rows_dev, extra = half // n_dp, rows - half

    def body(where_ref, mine_ref, core_ref, far_ref, own_ref, got_ref, *outs):
        def ids_of(ref, start):
            all_ids = ref[start:start + 2 * n_level * folds].astype(F32)
            mine = level * folds
            high = all_ids[mine:mine + folds]
            low = all_ids[(n_level * folds) + mine:(n_level * folds) + mine + folds]
            ids = high * 32.0 + low
            return jnp.concatenate([ids[f:f + 1] for f in range(folds)], axis=1)

        place = lax.broadcasted_iota(jnp.int32, (tokens, half), 1)
        owner = jnp.bitwise_xor(place // rows_dev, where_ref[DP])
        base = owner * rows_dev + place % rows_dev
        rows_of = [(mine_ref, top), (core_ref, top), (far_ref, top), (far_ref, top + n_rows)]
        columns = jnp.concatenate([ids_of(*r) for r in rows_of], axis=0).T.astype(jnp.int32)
        for m in (2, 3) if away else (1, 0):
            col = columns[:, m:m + 1]
            total = None
            for k, ref in enumerate((own_ref, got_ref)):
                start = (where_ref[HEAD] ^ k) * half
                hot = (base == col - start).astype(F32).astype(BF16)
                part = jnp.dot(hot, ref[:half], preferred_element_type=F32)
                total = part if total is None else total + part
            total = total.astype(BF16)
            if away:
                outs[0][(m - 2) * tokens:(m - 1) * tokens, :] = total
            else:
                outs[m][:tokens] = total
        if extra and away:
            outs[0][2 * tokens:2 * tokens + extra] = got_ref[half:]
            outs[0][2 * tokens + extra:] = own_ref[rows - late:]
        elif extra:
            outs[1][tokens:] = got_ref[half:]

    if away:
        outs = [shaped((2 * tokens + extra + late, cols))]
    else:
        outs = [shaped((tokens, cols)), shaped((tokens + extra, cols))]
    return run(body, outs, where, *packed, own, got)


def depth_grad(where, folds, rest, late, first, second, mixed, mixed_got, cot):
    arrays, which = [], []
    for array, _ in folds + first + second:
        found = [i for i, other in enumerate(arrays) if other is array]
        if not found:
            arrays.append(array)
        which.append(found[0] if found else len(arrays) - 1)
    starts = [start for _, start in folds + first + second]
    tokens, width = mixed.shape
    cols = width // 4
    chunk = 32

    def body(where_ref, *refs):
        parts = refs[:len(arrays)]
        mixed_ref, got_ref, cot_ref, out, full, sum_ref, mid_ref, last_ref, row_ref = refs[len(arrays):]
        for n in range(16):
            m, x, j = n // 4, n // 2 % 2, n % 2
            place = (where_ref[HEAD] ^ x) * 2 + j
            if rest[n] is None:
                full[at(where_ref[m], cols), at(place, cols)] = parts[which[n]][starts[n]:starts[n] + cols]
            else:
                main = pl.ds(pl.multiple_of(where_ref[m] * cols, cols), cols - late)
                tail = pl.ds(pl.multiple_of(where_ref[m] * cols + cols - late, 16), late)
                array = next(i for i, other in enumerate(arrays) if other is rest[n][0])
                full[main, at(place, cols)] = parts[which[n]][starts[n]:starts[n] + cols - late]
                full[tail, at(place, cols)] = parts[array][rest[n][1]:rest[n][1] + late]

        def rows_of(i):
            return pl.ds(pl.multiple_of(i * chunk, chunk), chunk)

        def lane_rows(i, n):
            return parts[which[n]][pl.ds(pl.multiple_of(starts[n] + i * chunk, chunk), chunk), :].astype(F32)

        def inverse(total):
            return lax.rsqrt(jnp.mean(total * total, axis=-1, keepdims=True) + 1e-05)

        def enter(i, carry):
            rows = rows_of(i)
            for m in range(4):
                cut = at(where_ref[m], cols)
                sum_ref[rows, cut] = mixed_ref[rows, cut] + got_ref[rows, cut].astype(F32) + lane_rows(i, 16 + m)
            total = sum_ref[rows, :]
            row_ref[rows, :] = (total * inverse(total)).astype(BF16)
            return carry

        lax.fori_loop(0, tokens // chunk, enter, 0, unroll=True)
        mid_ref[...] = jnp.dot(row_ref[...], full[...], preferred_element_type=F32)
        last_ref[...] = dot(cot_ref[:, width:], full[...], ((1,), (1,)))

        def middle(i, carry):
            rows = rows_of(i)
            projected = mid_ref[rows, :]
            gate = jax.nn.sigmoid(projected)
            mid_ref[rows, :] = sum_ref[rows, :] + projected * gate
            for m in range(4):
                cut = at(where_ref[m], cols)
                mid_ref[rows, cut] += lane_rows(i, 20 + m)
            total = mid_ref[rows, :]
            inv = inverse(total)
            grad = last_ref[rows, :]
            along = jnp.mean(grad * total, axis=-1, keepdims=True)
            grad = grad * inv - total * (along * inv * inv * inv)
            last_ref[rows, :] = grad
            slope = gate * (1.0 + projected * (1.0 - gate))
            row_ref[rows, :] = (cot_ref[rows, :width].astype(F32) + grad * slope).astype(BF16)
            return carry

        lax.fori_loop(0, tokens // chunk, middle, 0, unroll=True)
        mid_ref[...] = dot(row_ref[...], full[...], ((1,), (1,)))

        def leave(i, carry):
            rows = rows_of(i)
            total = sum_ref[rows, :]
            inv = inverse(total)
            grad = mid_ref[rows, :]
            along = jnp.mean(grad * total, axis=-1, keepdims=True)
            grad = last_ref[rows, :] + grad * inv - total * (along * inv * inv * inv)
            out[rows, :] = grad.astype(BF16)
            return carry

        lax.fori_loop(0, tokens // chunk, leave, 0, unroll=True)

    vmem = pl.BlockSpec(memory_space=pltpu.VMEM)
    return pl.pallas_call(
        body,
        out_shape=shaped((tokens, width)),
        in_specs=[pl.BlockSpec(memory_space=pltpu.SMEM)] + [vmem] * (len(arrays) + 3),
        out_specs=vmem,
        scratch_shapes=[
            pltpu.VMEM((width, width), BF16),
            pltpu.VMEM((tokens, width), F32),
            pltpu.VMEM((tokens, width), F32),
            pltpu.VMEM((tokens, width), F32),
            pltpu.VMEM((tokens, width), BF16),
        ],
        compiler_params=pltpu.CompilerParams(vmem_limit_bytes=VMEM_BYTES),
    )(where, *arrays, mixed, mixed_got, cot)


def id_rows(n_level, tokens):
    return -(-2 * n_level * (tokens // DH) // 16) * 16


def pack(where, keys, values, ids):
    heads = keys.shape[1] // DH
    n_level, tokens = ids.shape
    folds = tokens // DH
    top = heads * DH

    def body(where_ref, k_ref, v_ref, ids_ref, out):
        parts = []
        for level in range(n_level):
            for fold in range(folds):
                parts.append(ids_ref[level:level + 1, fold * DH:(fold + 1) * DH])
        whole = jnp.concatenate(parts, axis=0)
        both = jnp.concatenate([whole // 32, whole % 32], axis=0).astype(F32).astype(BF16)
        out[top:top + 2 * n_level * folds] = both
        for i in range(heads):
            cut = slice(i * DH, (i + 1) * DH)
            out[cut] = dot(k_ref[:, cut], v_ref[:, cut], ((0,), (0,))).astype(BF16)

    return run(body, [shaped((top + id_rows(n_level, tokens), DH))], where, keys, values, ids)[0]


def pack_chip(where, own, core, top):
    rows = own.shape[0] - top

    def body(where_ref, own_ref, core_ref, out):
        out[:top] = (own_ref[:top].astype(F32) + core_ref[:top].astype(F32)).astype(BF16)
        out[top:top + rows] = own_ref[top:]
        out[top + rows:] = core_ref[top:]

    return run(body, [shaped((top + 2 * rows, DH))], where, own, core)[0]


def lower(size):
    rows = lax.broadcasted_iota(jnp.int32, (size, size), 0)
    cols = lax.broadcasted_iota(jnp.int32, (size, size), 1)
    return rows >= cols


def upper(size):
    rows = lax.broadcasted_iota(jnp.int32, (size, size), 0)
    cols = lax.broadcasted_iota(jnp.int32, (size, size), 1)
    return rows <= cols


def attend(where, queries, keys, values, from_core, from_far, att_scale):
    length, width_dev = queries.shape
    heads = width_dev // DH

    def body(where_ref, q_ref, k_ref, v_ref, core_ref, far_ref, att, state):
        near = (where_ref[0] // 2).astype(F32)
        far = (where_ref[0] % 2).astype(F32)
        keep = lower(length)
        for i in range(heads):
            cut = slice(i * DH, (i + 1) * DH)
            state[i] = (core_ref[cut].astype(F32) * near + far_ref[cut].astype(F32) * far).astype(BF16)
            q = q_ref[:, cut]
            scores = jnp.where(keep, dot(q, k_ref[:, cut], ((1,), (1,))), 0.0).astype(BF16)
            both = jnp.dot(scores, v_ref[:, cut], preferred_element_type=F32)
            both += jnp.dot(q, state[i], preferred_element_type=F32)
            att[:, cut] = (att_scale * both).astype(BF16)

    return run(
        body, [shaped((length, width_dev)), shaped((heads, DH, DH))], where, queries, keys, values, from_core, from_far
    )


def mix_own(where, attended, head, tail):
    length = attended.shape[0] // 2
    half, width = head.shape[0] + tail.shape[0], head.shape[1]

    def body(where_ref, att, head_ref, tail_ref, out):
        core = where_ref[0] // 2
        own = jnp.concatenate([head_ref[...], tail_ref[...]], axis=0)
        for k in range(2):
            rows = at(where_ref[HEAD] ^ (1 - k), length)
            out[k] = jnp.dot(att[rows, at(core, half)], own, preferred_element_type=F32)

    return run(body, [shaped((2, length, width), F32)], where, attended, head, tail)[0]


def mix(where, attended, part, got_head, got_tail, other):
    length = attended.shape[0] // 2
    width = part.shape[2]
    half = got_head.shape[0] + got_tail.shape[0]
    dtype = BF16 if other else F32

    def body(where_ref, att, part_ref, head, tail, out):
        rows = at(where_ref[HEAD] ^ (1 if other else 0), length)
        core = where_ref[0] // 2
        got = jnp.concatenate([head[...], tail[...]], axis=0)
        total = part_ref[0 if other else 1]
        total += jnp.dot(att[rows, at(1 - core, half)], got, preferred_element_type=F32)
        out[...] = total.astype(dtype)

    return run(body, [shaped((length, width), dtype)], where, attended, part, got_head, got_tail)[0]


def weight_own(where, attended, grad_own):
    tokens, width = grad_own.shape

    def body(where_ref, att, own, out):
        for m in range(4):
            out[m] = dot(att[at(where_ref[HEAD], tokens), at(where_ref[m], DH)], own[...], ((0,), (0,)))

    return run(body, [shaped((4, DH, width), F32)], where, attended, grad_own)[0]


def weight_terms(where, attended, part, grad_got):
    tokens, width = grad_got.shape

    def body(where_ref, att, part_ref, got, send, keep):
        def term(m):
            a = att[at(1 - where_ref[HEAD], tokens), at(where_ref[m], DH)]
            return part_ref[m] + dot(a, got[...], ((0,), (0,)))

        send[0] = term(2).astype(BF16)
        send[1] = term(3).astype(BF16)
        keep[0] = term(0)
        keep[1] = term(1)

    return run(
        body, [shaped((2, DH, width)), shaped((2, DH, width), F32)], where, attended, part, grad_got
    )


def add_core(where, keep, got):
    shape = keep.shape[1:]

    def body(where_ref, keep_ref, got_ref, send, rest):
        rest[...] = keep_ref[0] + got_ref[0].astype(F32)
        send[...] = (keep_ref[1] + got_ref[1].astype(F32)).astype(BF16)

    return run(body, [shaped(shape), shaped(shape, F32)], where, keep, got)


def add_far(where, keep, got, n_dp):
    rows, width = keep.shape
    cols = width // n_dp

    def body(where_ref, keep_ref, got_ref, rest, *send):
        for k in range(n_dp):
            cut = at(where_ref[DP] ^ k, cols)
            total = keep_ref[:, cut] + got_ref[:, cut].astype(F32)
            if k:
                send[k - 1][...] = total.astype(BF16)
            else:
                rest[...] = total

    return run(body, [shaped((rows, cols), F32)] + [shaped((rows, cols))] * (n_dp - 1), where, keep, got)


def add_all(where, keep, got):
    def body(where_ref, keep_ref, *refs):
        total = keep_ref[...]
        for ref in refs[:-1]:
            total = total + ref[...].astype(F32)
        refs[-1][...] = total.astype(BF16)

    return run(body, [shaped(keep.shape)], where, keep, *got)[0]


def rows_together(where, pieces):
    rows, cols = pieces[0].shape

    def body(where_ref, *refs):
        for m, ref in enumerate(refs[:-1]):
            refs[-1][at(where_ref[m], rows), :] = ref[...].astype(F32)

    return run(body, [shaped((rows * 4, cols), F32)], where, *pieces)[0]


def grad_attend(where, grad_own, grad_got, own_head, own_tail, got_head, got_tail, queries):
    tokens, width = grad_own.shape
    length, width_dev = queries.shape
    half = width_dev // 2

    def body(where_ref, own, got, head, tail, got_head, got_tail, q_ref, rows, back):
        for c, ends in enumerate(((head, tail), (got_head, got_tail))):
            block = jnp.concatenate([ends[0][...], ends[1][...]], axis=0)
            for k, ref in enumerate((own, got)):
                part = dot(ref[...], block, ((1,), (1,))).astype(BF16)
                rows[at(where_ref[HEAD] ^ k, tokens), at((where_ref[0] // 2) ^ c, half)] = part
        for i in range(width_dev // DH):
            cut = slice(i * DH, (i + 1) * DH)
            back[i] = dot(q_ref[:, cut], rows[:, cut], ((0,), (0,))).astype(BF16)

    outs = [shaped((length, width_dev)), shaped((width_dev // DH, DH, DH))]
    return run(body, outs, where, grad_own, grad_got, own_head, own_tail, got_head, got_tail, queries)


def query_grads(where, grad_rows, keys, values, state, att_scale):
    length, width_dev = keys.shape

    def body(where_ref, g_ref, k_ref, v_ref, s_ref, out):
        keep = lower(length)
        for i in range(width_dev // DH):
            cut = slice(i * DH, (i + 1) * DH)
            g = g_ref[:, cut]
            scores = jnp.where(keep, dot(g, v_ref[:, cut], ((1,), (1,))), 0.0).astype(BF16)
            both = jnp.dot(scores, k_ref[:, cut], preferred_element_type=F32)
            both += dot(g, s_ref[i], ((1,), (1,)))
            out[:, cut] = (att_scale * both).astype(BF16)

    return run(body, [shaped((length, width_dev))], where, grad_rows, keys, values, state)[0]


def key_value_parts(where, grad_rows, queries, keys, values):
    length, width_dev = keys.shape

    def body(where_ref, g_ref, q_ref, k_ref, v_ref, dk, dv):
        keep = upper(length)
        for i in range(width_dev // DH):
            cut = slice(i * DH, (i + 1) * DH)
            g, q, k, v = g_ref[:, cut], q_ref[:, cut], k_ref[:, cut], v_ref[:, cut]
            grad_scores = jnp.where(keep, dot(v, g, ((1,), (1,))), 0.0).astype(BF16)
            dk[:, cut] = jnp.dot(grad_scores, q, preferred_element_type=F32)
            scores = jnp.where(keep, dot(k, q, ((1,), (1,))), 0.0).astype(BF16)
            dv[:, cut] = jnp.dot(scores, g, preferred_element_type=F32)

    outs = [shaped((length, width_dev), F32)] * 2
    return run(body, outs, where, grad_rows, queries, keys, values)


def key_value_grads(where, key_part, value_part, keys, values, from_core, from_far, att_scale):
    length, width_dev = keys.shape

    def body(where_ref, kp_ref, vp_ref, k_ref, v_ref, core_ref, far_ref, dk, dv):
        near = 1.0 - (where_ref[0] // 2).astype(F32)
        far = 1.0 - (where_ref[0] % 2).astype(F32)
        for i in range(width_dev // DH):
            cut = slice(i * DH, (i + 1) * DH)
            back = (core_ref[i].astype(F32) * near + far_ref[i].astype(F32) * far).astype(BF16)
            both = kp_ref[:, cut] + dot(v_ref[:, cut], back, ((1,), (1,)))
            dk[:, cut] = (att_scale * both).astype(BF16)
            both = vp_ref[:, cut] + jnp.dot(k_ref[:, cut], back, preferred_element_type=F32)
            dv[:, cut] = (att_scale * both).astype(BF16)

    outs = [shaped((length, width_dev))] * 2
    return run(body, outs, where, key_part, value_part, keys, values, from_core, from_far)


def fits(queries, out_proj, depth_proj, code_table, code_ids):
    n_seq, n_head = lax.axis_size("seq"), lax.axis_size("head")
    return (
        n_seq == 4
        and n_head == 2
        and queries.shape[2] == 4 * DH
        and code_table.shape[0] == 2
        and out_proj.shape[1] % 128 == 0
        and depth_proj.shape[1] % 128 == 0
        and code_table.shape[1] % 128 == 0
        and code_ids.shape[1] % DH == 0
        and code_table.shape[1] * n_head * lax.axis_size("dp") <= 32 * 256
    )


def on_device(queries, keys, values, out_proj, depth_proj, code_table, code_ids, depth_cotangent):
    if not fits(queries, out_proj, depth_proj, code_table, code_ids):
        return on_device_any(
            queries, keys, values, out_proj, depth_proj, code_table, code_ids, depth_cotangent
        )
    n_dp = lax.axis_size("dp")
    me_seq, me_head, me_dp = (lax.axis_index(a) for a in ("seq", "head", "dp"))
    group_len = queries.shape[1]
    width = code_table.shape[2]
    att_scale = float(group_len * lax.axis_size("seq")) ** (-0.5)
    core, far = me_seq % 2, me_seq // 2
    lane = 2 * core + far
    where = jnp.stack([lane, lane ^ 1, lane ^ 2, lane ^ 3, me_head, me_dp, me_seq]).astype(jnp.int32)
    queries, keys, values = queries[0], keys[0], values[0]

    def far_swap(block):
        return swap(block, "seq", 2)

    def core_swap(block):
        return swap(block, "seq", 1)

    def all_lanes(block):
        got = far_swap(block)
        return [block, got, core_swap(block), core_swap(got)]

    t_rows, tokens = code_table.shape[1], code_ids.shape[1]
    half = t_rows * n_dp
    lanes_0 = first_lanes(code_table, depth_proj, n_dp)
    pieces_0 = lax.all_to_all(lanes_0, "dp", 0, 0)
    lanes_1 = second_lanes(code_table, out_proj, lanes_0)
    distances = [n_dp // 2] + [k for k in range(1, n_dp) if k != n_dp // 2]
    pieces_1 = [lanes_1] + [swap(lanes_1, "dp", k) for k in distances]

    top = keys.shape[1]
    keys, values, _ = lax.optimization_barrier((keys, values, lanes_1))
    mine = pack(where, keys, values, code_ids[0].T)
    from_core = core_swap(mine)
    chip = pack_chip(where, mine, from_core, top)
    from_far = far_swap(chip)
    packed = (mine, from_core, from_far)

    attended, state_in = attend(where, queries, keys, values, from_core, from_far, att_scale)

    pieces_0, _ = lax.optimization_barrier((pieces_0, attended))
    fold = depth_proj.shape[0] // 4
    early = fold + fold * 7 // 16
    late = 2 * fold - early
    part_0, depth_part, depth_top = first_parts(where, pieces_0, t_rows, early)
    got_0 = swap(part_0, "head", 1)
    depth_far = far_swap(depth_top)

    pieces_1, depth_far = lax.optimization_barrier((pieces_1, depth_far))
    part_1, out_head, out_tail = second_parts(where, pieces_1, [0, *distances], t_rows)
    got_head, got_tail = core_swap(out_head), core_swap(out_tail)
    got_1 = swap(part_1, "head", 1)

    mixed_part = mix_own(where, attended, out_head, out_tail)
    got_0, got_head, _ = lax.optimization_barrier((got_0, got_head, part_1))
    (to_far,) = embed(where, packed, top, 0, 2, tokens, part_0, got_0, half, n_dp, late, True)
    far_0 = far_swap(to_far)

    got_tail, _ = lax.optimization_barrier((got_tail, to_far))
    mixed_send = mix(where, attended, mixed_part, got_head, got_tail, True)
    mixed_got = swap(mixed_send, "head", 1)
    mixed_part, got_1 = lax.optimization_barrier((mixed_part, got_1))
    mixed = mix(where, attended, mixed_part, got_head, got_tail, False)

    got_1, _, _ = lax.optimization_barrier((got_1, mixed, mixed_send))
    (to_far,) = embed(where, packed, top, 1, 2, tokens, part_1, got_1, half, n_dp, 0, True)
    near_0, _ = lax.optimization_barrier((got_0, to_far))
    own_0, to_core = embed(where, packed, top, 0, 2, tokens, part_0, near_0, half, n_dp, late, False)
    core_0 = core_swap(to_core)
    near_1, _ = lax.optimization_barrier((got_1, to_far))
    own_1, to_core = embed(where, packed, top, 1, 2, tokens, part_1, near_1, half, n_dp, 0, False)
    far_1 = far_swap(to_far)
    depth_core, depth_core_far = core_swap(depth_part), core_swap(depth_far)
    far_0, far_1, mixed_got, depth_core, depth_core_far, core_0, to_core, own_1 = lax.optimization_barrier(
        (far_0, far_1, mixed_got, depth_core, depth_core_far, core_0, to_core, own_1)
    )
    core_far_0, core_1, core_far_1 = core_swap(far_0), core_swap(to_core), core_swap(far_1)

    end = 2 * tokens
    folds = [(depth_part, 0), (depth_part, fold), (got_0, half), (got_0, half + fold)]
    folds += [(depth_far, 0), (depth_far, fold), (far_0, end), (far_0, end + fold)]
    folds += [(depth_core, 0), (depth_core, fold), (core_0, tokens), (core_0, tokens + fold)]
    folds += [(depth_core_far, 0), (depth_core_far, fold), (core_far_0, end), (core_far_0, end + fold)]
    rest = [None] * 16
    rest[5], rest[13] = (far_0, end + 2 * fold), (core_far_0, end + 2 * fold)
    first = [(own_0, 0), (far_0, 0), (core_0, 0), (core_far_0, tokens)]
    second = [(own_1, 0), (far_1, 0), (core_1, 0), (core_far_1, tokens)]
    cot = depth_cotangent[0].reshape(tokens, -1)
    grad_mixed = depth_grad(where, folds, rest, late, first, second, mixed, mixed_got, cot)

    grad_got = swap(grad_mixed, "head", 1)
    part = weight_own(where, attended, grad_mixed)
    send, keep = weight_terms(where, attended, part, grad_got)
    send, keep = add_core(where, keep, core_swap(send))
    from_far = far_swap(send)
    grad_rows, back = grad_attend(where, grad_mixed, grad_got, out_head, out_tail, got_head, got_tail, queries)
    back, send = lax.optimization_barrier((back, send))
    back_core = core_swap(back)
    back_chip = (back.astype(F32) + back_core.astype(F32)).astype(BF16)
    key_part, value_part = key_value_parts(where, grad_rows, queries, keys, values)
    grad_query = query_grads(where, grad_rows, keys, values, state_in, att_scale)
    from_far, key_part, value_part, grad_query, back_chip = lax.optimization_barrier(
        (from_far, key_part, value_part, grad_query, back_chip)
    )
    keep, *send = add_far(where, keep, from_far, n_dp)
    got = [swap(send[k - 1], "dp", k) for k in reversed(range(1, n_dp))]
    back_chip, keep = lax.optimization_barrier((back_chip, keep))
    back_far = far_swap(back_chip)
    block = add_all(where, keep, got)
    blocks = [block, far_swap(block), core_swap(block), swap(block, "seq", 3)]
    key_part, block = lax.optimization_barrier((key_part, block))
    grad_key, grad_value = key_value_grads(
        where, key_part, value_part, keys, values, back_core, back_far, att_scale
    )
    blocks, grad_key, grad_value = lax.optimization_barrier((blocks, grad_key, grad_value))
    grad_out_proj = rows_together(where, blocks)
    return grad_query[None], grad_key[None], grad_value[None], grad_out_proj


def solution(mesh):
    in_specs = (
        P("dp", "seq", "head"),
        P("dp", "seq", "head"),
        P("dp", "seq", "head"),
        P("head", "dp"),
        P(None, ("head", "dp")),
        P(None, ("head", "dp"), None),
        P("dp", ("seq", "head"), None),
        P("dp", ("seq", "head"), None, None),
    )
    out_specs = (
        P("dp", "seq", "head"),
        P("dp", "seq", "head"),
        P("dp", "seq", "head"),
        P("head", "dp"),
    )
    return jax.shard_map(
        on_device, mesh=mesh, in_specs=in_specs, out_specs=out_specs, check_vma=False
    )
```
